256 devices in a mesh: tm: 32 (over y, x, z_lo), cam: 8 (over z_hi, core).
Axes of the slice: x: 4, y: 4, z: 8 (z_hi: 4, z_lo: 2; z = z_hi * 2 + z_lo), core: 2. Of those that a mesh axis runs over, the one named last changes fastest.
Arguments:
- tokens: bfloat16 [32, 8, 128, 1024], P('tm', 'cam'), may hold values from -6 to 6
- gain: float32 [1024], replicated, may hold values from 0.1 to 1.9
- w_qkv: bfloat16 [1024, 3072], replicated
- w_out: bfloat16 [1024, 1024], replicated, may hold values from -4.5 to 4.5
- window: int32 [8], replicated, may hold values from 1 to 8, as said below
- valid: int32 [32], P('tm'), may hold values 0 or 1
- cotangent: bfloat16 [32, 8, 128, 1024], P('tm', 'cam'), may hold values from -3 to 3
Outputs:
- mixed: bfloat16 [32, 8, 128, 1024], P('tm', 'cam')
- d_tokens: bfloat16 [32, 8, 128, 1024], P('tm', 'cam')
The draws below stay inside these ranges and needn't reach their ends.
Inputs may be any that keep to these rules, and one draw needn't show every extreme that they name: At least one head has window 8.
All inputs are finite; a program needn't handle non-finite values. No bound on the sum of `valid` on one device may be relied on, other than what follows from the above.
Results may differ from the reference program's by a relative error of at most 0.02.
Values may be sent and summed in bfloat16 or wider, within the bound.
No kernel may reach another device: no remote copies, remote signals or barrier semaphores. Data moves between devices by JAX's collectives and lax.ppermute only.
A program may use at most 128 MiB of HBM per device.

```python
import jax
import jax.numpy as jnp
from jax import lax

D = 1024
H = 8
DH = 128
HW = 128
WIN = 8
F_DEV = 1
FRAMES = 32
CAMS = 8


def draw_w_qkv(key, part):
    key = jax.random.fold_in(key, 7)
    noise_key = jax.random.fold_in(key, 0)
    noise = jax.random.normal(noise_key, (D, 3 * D), jnp.float32) * D ** (-0.5)
    return noise.astype(jnp.bfloat16)


def draw_window(key, part):
    key = jax.random.fold_in(key, 11)
    first, second = jax.random.split(key)
    lengths = jax.random.randint(first, (H,), 1, WIN + 1)
    chosen = jax.random.randint(second, (), 0, H)
    return lengths.at[chosen].set(WIN).astype(jnp.int32)


def place_ends(drawn, stream_key, low, high):
    spot = [jax.random.randint(jax.random.fold_in(stream_key, axis), (), 0, length) for axis, length in enumerate(drawn.shape)]
    widest = drawn.shape.index(max(drawn.shape))
    neighbour = spot[:widest] + [(spot[widest] + 1) % drawn.shape[widest]] + spot[widest + 1:]
    return drawn.at[tuple(spot)].set(low).at[tuple(neighbour)].set(high)


def steps_of(own_key, shape, cuts, least, top_value):
    loudness, own = 1.0, jax.random.fold_in(own_key, 6)
    for axis_at, shards_of in cuts:
        heights = jnp.exp(jax.random.uniform(jax.random.fold_in(own, axis_at), (shards_of,), jnp.float32, least / len(cuts), top_value / len(cuts)))
        loudness = loudness * jnp.repeat(heights, shape[axis_at] // shards_of).reshape([-1 if axis == axis_at else 1 for axis in range(len(shape))])
    return loudness


def scatter_about(stream_key, extent, scale, bound, pieces=(), kind=jnp.bfloat16):
    entries = scale * jax.random.normal(stream_key, extent, jnp.float32)
    if pieces:
        entries = entries * steps_of(stream_key, extent, pieces, -0.22, 0.18)
    return jnp.clip(entries, -bound, bound).astype(kind)


def setup_inputs(seed: int = 0) -> dict:
    splits = jax.random.split(jax.random.key(seed), 8)
    tokens = scatter_about(splits[0], (FRAMES, CAMS, HW, D), 1.0, 6.0, ((0, 32), (1, 8)))
    gain = jnp.clip(1.0 + 0.18 * jax.random.normal(splits[1], (D,), jnp.float32), 0.1, 1.9)
    w_qkv = draw_w_qkv(jax.random.fold_in(splits[7], 71), 0)
    w_out = scatter_about(splits[3], (D, D), 0.75, 4.5)
    window = draw_window(jax.random.fold_in(splits[7], 71), 0)
    valid = place_ends((jax.random.randint(splits[5], (FRAMES,), 0, 4) < 3).astype(jnp.int32), jax.random.fold_in(splits[5], 1), 0, 1)
    cotangent = scatter_about(splits[6], (FRAMES, CAMS, HW, D), 0.5, 3.0, ((0, 32), (1, 8)))
    return dict(tokens=tokens, gain=gain, w_qkv=w_qkv, w_out=w_out, window=window, valid=valid, cotangent=cotangent)


EPS = 1e-05

def reference(tokens, gain, w_qkv, w_out, window, valid, cotangent):
    scale = DH ** (-0.5)
    reach = WIN // F_DEV
    shards = FRAMES // F_DEV
    split = CAMS * HW
    inputs = tokens.astype(jnp.float32)
    rinv = lax.rsqrt(lax.optimization_barrier(jnp.mean(inputs * inputs, axis=-1, keepdims=True)) + EPS)
    normed = (inputs * rinv * gain).astype(jnp.bfloat16)
    proj = jnp.dot(normed.reshape(-1, D), w_qkv, preferred_element_type=jnp.float32).astype(jnp.bfloat16)
    proj = proj.reshape(FRAMES, CAMS, HW, 3, H, DH)
    query = proj[:, :, :, 0]
    keys = proj[:, :, :, 1]
    values = proj[:, :, :, 2]
    blank = jnp.zeros((WIN, CAMS, HW, H, DH), jnp.bfloat16)
    keys_pad = jnp.concatenate([blank, keys], axis=0)
    values_pad = jnp.concatenate([blank, values], axis=0)
    valid_pad = jnp.concatenate([jnp.zeros((WIN,), jnp.int32), valid.astype(jnp.int32)], axis=0)
    offsets = jnp.arange(WIN, dtype=jnp.int32)
    head_ok = offsets[None, :] >= (WIN - window)[:, None]

    def frame_inputs(frame):
        frame_keys = keys[frame].reshape(split, H, DH).astype(jnp.float32)
        frame_values = values[frame].reshape(split, H, DH).astype(jnp.float32)
        past_keys = lax.dynamic_slice_in_dim(keys_pad, frame, WIN, 0)
        past_keys = past_keys.transpose(1, 0, 2, 3, 4).reshape(CAMS, WIN * HW, H, DH).astype(jnp.float32)
        past_values = lax.dynamic_slice_in_dim(values_pad, frame, WIN, 0)
        past_values = past_values.transpose(1, 0, 2, 3, 4).reshape(CAMS, WIN * HW, H, DH).astype(jnp.float32)
        past_ok = lax.dynamic_slice_in_dim(valid_pad, frame, WIN, 0)
        allowed = jnp.repeat(head_ok & (past_ok[None, :] == 1), HW, axis=1)
        return (frame_keys, frame_values, past_keys, past_values, allowed)

    def scores_of(queries, frame_keys, past_keys, allowed):
        near = jnp.einsum('cphd,khd->chpk', queries, frame_keys) * scale
        past = jnp.einsum('cphd,ckhd->chpk', queries, past_keys) * scale
        past = jnp.where(allowed[None, :, None, :], past, -jnp.inf)
        return jnp.concatenate([near, past], axis=-1)

    def forward_frame(frame):
        frame_keys, frame_values, past_keys, past_values, allowed = frame_inputs(frame)
        queries = query[frame].astype(jnp.float32)
        scores = scores_of(queries, frame_keys, past_keys, allowed)
        peak = lax.optimization_barrier(jnp.max(scores, axis=-1, keepdims=True))
        expd = jnp.exp(scores - peak)
        total = lax.optimization_barrier(jnp.sum(expd, axis=-1, keepdims=True))
        weights = lax.optimization_barrier((expd / total).astype(jnp.bfloat16)).astype(jnp.float32)
        attended = jnp.einsum('chpk,khd->cphd', weights[..., :split], frame_values)
        attended = attended + jnp.einsum('chpk,ckhd->cphd', weights[..., split:], past_values)
        return (attended.astype(jnp.bfloat16), peak, total)
    attended, peaks, totals = lax.map(forward_frame, jnp.arange(FRAMES, dtype=jnp.int32))
    output = jnp.dot(attended.reshape(-1, D), w_out, preferred_element_type=jnp.float32).reshape(inputs.shape)
    mixed = (inputs + output).astype(jnp.bfloat16)
    d_attended = jnp.dot(cotangent.reshape(-1, D), w_out.T, preferred_element_type=jnp.float32)
    d_attended = d_attended.astype(jnp.bfloat16).reshape(FRAMES, CAMS, HW, H, DH)
    deltas = lax.optimization_barrier(jnp.sum(d_attended.astype(jnp.float32) * attended.astype(jnp.float32), axis=-1))
    deltas = deltas.transpose(0, 1, 3, 2)[..., None]

    def backward_frame(frame):
        frame_keys, frame_values, past_keys, past_values, allowed = frame_inputs(frame)
        queries = query[frame].astype(jnp.float32)
        scores = scores_of(queries, frame_keys, past_keys, allowed)
        probs = jnp.exp(scores - peaks[frame]) / totals[frame]
        weights = lax.optimization_barrier(probs.astype(jnp.bfloat16)).astype(jnp.float32)
        grads_out = d_attended[frame].astype(jnp.float32)
        d_probs = jnp.concatenate([jnp.einsum('cphd,khd->chpk', grads_out, frame_values), jnp.einsum('cphd,ckhd->chpk', grads_out, past_values)], axis=-1)
        d_scores = (probs * (d_probs - deltas[frame]) * scale).astype(jnp.bfloat16)
        d_scores = lax.optimization_barrier(d_scores).astype(jnp.float32)
        d_query = jnp.einsum('chpk,khd->cphd', d_scores[..., :split], frame_keys)
        d_query = d_query + jnp.einsum('chpk,ckhd->cphd', d_scores[..., split:], past_keys)
        near_keys = jnp.einsum('chpk,cphd->ckhd', d_scores[..., :split], queries)
        near_keys = lax.optimization_barrier(near_keys.astype(jnp.bfloat16)).astype(jnp.float32)
        near_keys = lax.optimization_barrier(jnp.sum(near_keys, axis=0)).reshape(CAMS, HW, H, DH)
        near_values = jnp.einsum('chpk,cphd->ckhd', weights[..., :split], grads_out)
        near_values = lax.optimization_barrier(near_values.astype(jnp.bfloat16)).astype(jnp.float32)
        near_values = lax.optimization_barrier(jnp.sum(near_values, axis=0)).reshape(CAMS, HW, H, DH)
        far_keys = jnp.einsum('chpk,cphd->ckhd', d_scores[..., split:], queries)
        far_values = jnp.einsum('chpk,cphd->ckhd', weights[..., split:], grads_out)
        return (d_query, near_keys, near_values, far_keys, far_values)

    def backward_shard(shard):
        buffer_keys = jnp.zeros((CAMS, (WIN + F_DEV) * HW, H, DH), jnp.float32)
        buffer_values = jnp.zeros((CAMS, (WIN + F_DEV) * HW, H, DH), jnp.float32)
        queries_grad = []
        keys_grad = []
        values_grad = []
        for index in range(F_DEV):
            results = backward_frame(shard * F_DEV + index)
            buffer_keys = buffer_keys.at[:, index * HW:(index + WIN) * HW].add(results[3])
            buffer_values = buffer_values.at[:, index * HW:(index + WIN) * HW].add(results[4])
            queries_grad.append(results[0])
            keys_grad.append(results[1])
            values_grad.append(results[2])
        return (jnp.stack(queries_grad), jnp.stack(keys_grad), jnp.stack(values_grad), buffer_keys.astype(jnp.bfloat16), buffer_values.astype(jnp.bfloat16))
    d_query, near_keys, near_values, far_keys, far_values = lax.map(backward_shard, jnp.arange(shards, dtype=jnp.int32))

    def spread(buffers):
        buffers = buffers.reshape(shards, CAMS, reach + 1, F_DEV, HW, H, DH)
        sums = jnp.zeros((shards + reach, CAMS, F_DEV, HW, H, DH), jnp.float32)
        for step in range(reach + 1):
            sums = sums.at[step:step + shards].add(buffers[:, :, step].astype(jnp.float32))
        sums = sums[reach:].transpose(0, 2, 1, 3, 4, 5)
        return sums.reshape(FRAMES, CAMS, HW, H, DH)
    d_query = d_query.reshape(FRAMES, CAMS, HW, H, DH)
    d_keys = near_keys.reshape(FRAMES, CAMS, HW, H, DH) + spread(far_keys)
    d_values = near_values.reshape(FRAMES, CAMS, HW, H, DH) + spread(far_values)
    grads = jnp.stack([d_query, d_keys, d_values], axis=3).reshape(-1, 3 * D).astype(jnp.bfloat16)
    d_normed = jnp.dot(grads, w_qkv.T, preferred_element_type=jnp.float32).reshape(inputs.shape)
    scaled = d_normed * gain
    d_inputs = rinv * scaled - inputs * rinv ** 3 * lax.optimization_barrier(jnp.mean(scaled * inputs, axis=-1, keepdims=True))
    d_tokens = (cotangent.astype(jnp.float32) + d_inputs).astype(jnp.bfloat16)
    return (mixed, d_tokens)
```

```python
import math

import jax
import jax.numpy as jnp
from jax import lax
from jax.experimental import pallas as pl
from jax.experimental.pallas import tpu as pltpu
from jax.sharding import Mesh
from jax.sharding import PartitionSpec as P

D = 1024
H = 8
DH = 128
HW = 128
WIN = 8
EPS = 1e-05

HALF = H // 2
PAIR = 2 * HW
GROUP = 8
SCALE = DH ** (-0.5)
SCALE2 = SCALE * math.log2(math.e)
FLOOR = -3.0e38
F32 = jnp.float32
BF16 = jnp.bfloat16
NT = (((1,), (1,)), ((), ()))
VMEM_LIMIT = 48 * 1024 * 1024

Q0, G0, K0, V0, OK0, ROWS = 0, 128, 256, 384, 512, 528
KEYS = (WIN + 1) * HW


def params(**kw):
    return pltpu.CompilerParams(vmem_limit_bytes=VMEM_LIMIT, **kw)


def mm(a, b):
    return jnp.dot(a, b, preferred_element_type=F32)


def mm_nt(a, b):
    return lax.dot_general(a, b, NT, preferred_element_type=F32)


def turn(a):
    return a.astype(F32).T


def project_kernel(core, valid, own, other, cot_own, cot_other, gain, wq, wk, wv, wo, packed, kv):
    del core
    x = jnp.concatenate([own[...], other[...]], axis=0).astype(F32)
    rinv = lax.rsqrt(jnp.mean(x * x, axis=-1, keepdims=True) + EPS)
    normed = (x * rinv * gain[...]).astype(BF16)
    cot = jnp.concatenate([cot_own[...], cot_other[...]], axis=0)
    flags = jnp.full((ROWS - OK0, DH), valid[0], jnp.int32).astype(F32).astype(BF16)
    for row, part in ((K0, wk), (V0, wv), (Q0, wq), (G0, wo)):
        if row == G0:
            got = mm_nt(cot, part[...]).astype(BF16)
        else:
            got = mm(normed, part[...]).astype(BF16)
        for h in range(HALF):
            block = got[:, h * DH : (h + 1) * DH]
            for s in range(2):
                packed[s, h, row : row + HW, :] = block[s * HW : (s + 1) * HW]
            if row == K0:
                kv[0, h] = block
            if row == V0:
                kv[1, h] = block
    for h in range(HALF):
        for s in range(2):
            packed[s, h, OK0:ROWS, :] = flags


def project(core, valid, own, other, cot_own, cot_other, gain, w_qkv, w_out):
    whole = lambda shape: pl.BlockSpec(shape, lambda i, core, valid: (0,) * len(shape))
    part = lambda at: pl.BlockSpec((D, HALF * DH), lambda i, core, valid: (0, at * 2 + core[0]))
    return pl.pallas_call(
        project_kernel,
        grid_spec=pltpu.PrefetchScalarGridSpec(
            num_scalar_prefetch=2,
            grid=(1,),
            in_specs=[whole((HW, D))] * 4
            + [whole((1, D)), part(0), part(1), part(2)]
            + [pl.BlockSpec((HALF * DH, D), lambda i, core, valid: (core[0], 0))],
            out_specs=[whole((2, HALF, ROWS, DH)), whole((2, HALF, PAIR, DH))],
        ),
        out_shape=[
            jax.ShapeDtypeStruct((2, HALF, ROWS, DH), BF16),
            jax.ShapeDtypeStruct((2, HALF, PAIR, DH), BF16),
        ],
        compiler_params=params(),
        cost_estimate=pl.CostEstimate(
            flops=2 * PAIR * D * 4 * HALF * DH, bytes_accessed=7_000_000, transcendentals=0
        ),
        name="project",
    )(core, valid, own, other, cot_own, cot_other, gain, w_qkv, w_qkv, w_qkv, w_out)


def split3(value):
    first = value.astype(BF16)
    rest = value - first.astype(F32)
    second = rest.astype(BF16)
    third = (rest - second.astype(F32)).astype(BF16)
    return [first.astype(F32), second.astype(F32), third.astype(F32)]


def far_forward_kernel(win, mine, past, sent, kept, keys, values_t, scores):
    width = win[0]
    for j in range(GROUP):
        keys[j * HW : (j + 1) * HW, :] = past[j, :HW, :]
        keys[(GROUP + j) * HW : (GROUP + j + 1) * HW, :] = mine[j, K0 : K0 + HW, :]
        values_t[:, j * HW : (j + 1) * HW] = turn(past[j, HW : 2 * HW, :]).astype(BF16)
        values_t[:, (GROUP + j) * HW : (GROUP + j + 1) * HW] = turn(
            mine[j, V0 : V0 + HW, :]
        ).astype(BF16)
    for p in range(GROUP // 2):
        query = jnp.concatenate([mine[2 * p, :HW, :], mine[2 * p + 1, :HW, :]], axis=0)
        grad_t = jnp.concatenate(
            [turn(mine[2 * p, G0 : G0 + HW, :]), turn(mine[2 * p + 1, G0 : G0 + HW, :])], axis=1
        )
        peak = jnp.full((1, PAIR), -jnp.inf, F32)
        for b in range(WIN + 1):
            j = 2 * p + b
            if j < GROUP:
                flag = past[j, 2 * HW : 2 * HW + 1, :].astype(F32)
            else:
                flag = mine[j - GROUP, OK0 : OK0 + 1, :].astype(F32)
            lower = jnp.where((flag > 0.5) & (b >= WIN - width) & (b < WIN), 0.0, -jnp.inf)
            upper = jnp.where((flag > 0.5) & (b >= WIN + 1 - width), 0.0, -jnp.inf)
            bias = jnp.concatenate([lower, upper], axis=1)
            block = mm_nt(keys[j * HW : (j + 1) * HW, :], query) + bias
            scores[b * HW : (b + 1) * HW, :] = block
            peak = jnp.maximum(peak, jnp.max(block, axis=0, keepdims=True))
        peak = jnp.maximum(peak * SCALE2, FLOOR)
        total = jnp.zeros((1, PAIR), F32)
        for b in range(WIN + 1):
            block = jnp.exp2(scores[b * HW : (b + 1) * HW, :] * SCALE2 - peak)
            total = total + jnp.sum(block, axis=0, keepdims=True)
            kept[p, b * HW : (b + 1) * HW, :] = block.astype(BF16)
        result = mm(values_t[:, p * PAIR : p * PAIR + KEYS], kept[p])
        delta = jnp.sum(result * grad_t, axis=0, keepdims=True)
        stats = split3(peak) + split3(total) + split3(delta)
        stats = jnp.concatenate(stats + [jnp.zeros((7, PAIR), F32)], axis=0)
        packed = jnp.concatenate([result, stats], axis=0).astype(BF16)
        sent[2 * p] = packed[:, :HW]
        sent[2 * p + 1] = packed[:, HW:]


VM = pl.BlockSpec(memory_space=pltpu.VMEM)
SM = pl.BlockSpec(memory_space=pltpu.SMEM)


def far_forward(width, mine, past):
    return pl.pallas_call(
        far_forward_kernel,
        in_specs=[SM, VM, VM],
        out_specs=[VM, VM],
        out_shape=[
            jax.ShapeDtypeStruct((GROUP, DH + 16, HW), BF16),
            jax.ShapeDtypeStruct((GROUP // 2, KEYS, PAIR), BF16),
        ],
        scratch_shapes=[
            pltpu.VMEM((2 * GROUP * HW, DH), BF16),
            pltpu.VMEM((DH, 2 * GROUP * HW), BF16),
            pltpu.VMEM((KEYS, PAIR), F32),
        ],
        compiler_params=params(),
        cost_estimate=pl.CostEstimate(
            flops=16 * KEYS * PAIR * DH, bytes_accessed=5_000_000, transcendentals=4 * KEYS * PAIR
        ),
        name="far_forward",
    )(width, mine, past)


def near_kernel(kv, packed, far, dkv, dq, attended, told, scores, kept, grads):
    query = jnp.concatenate([packed[0, 0, :HW, :], packed[1, 0, :HW, :]], axis=0)
    grad = jnp.concatenate([packed[0, 0, G0 : G0 + HW, :], packed[1, 0, G0 : G0 + HW, :]], axis=0)
    grad_t = turn(grad)
    peak = jnp.full((1, PAIR), -jnp.inf, F32)
    for z in range(4):
        block = mm_nt(kv[z, 0, 0], query)
        scores[z * PAIR : (z + 1) * PAIR, :] = block
        peak = jnp.maximum(peak, jnp.max(block, axis=0, keepdims=True))
    peak = peak * SCALE2
    total = jnp.zeros((1, PAIR), F32)
    for b in range(8):
        block = jnp.exp2(scores[b * HW : (b + 1) * HW, :] * SCALE2 - peak)
        total = total + jnp.sum(block, axis=0, keepdims=True)
        kept[b * HW : (b + 1) * HW, :] = block.astype(BF16)
    result = jnp.zeros((DH, PAIR), F32)
    for z in range(4):
        result = result + mm(turn(kv[z, 1, 0]).astype(BF16), kept[z * PAIR : (z + 1) * PAIR, :])
    delta = jnp.sum(result * grad_t, axis=0, keepdims=True)
    other = jnp.concatenate([far[0, 0], far[1, 0]], axis=1).astype(F32)
    row = lambda at: other[DH + at : DH + at + 1, :]
    far_peak = (row(0) + row(1)) + row(2)
    far_total = (row(3) + row(4)) + row(5)
    far_delta = (row(6) + row(7)) + row(8)
    top = jnp.maximum(peak, far_peak)
    near_weight = jnp.exp2(peak - top)
    far_weight = jnp.exp2(far_peak - top)
    inverse = 1.0 / (near_weight * total + far_weight * far_total)
    near_weight = near_weight * inverse
    far_weight = far_weight * inverse
    delta = near_weight * delta + far_weight * far_delta
    mixed_t = near_weight * result + far_weight * other[:DH, :]
    attended[0] = mixed_t.T.astype(BF16)
    far_delta = far_weight * delta
    for s in range(2):
        told[s, 0] = jnp.concatenate(
            [
                far_weight[:, s * HW : (s + 1) * HW],
                far_delta[:, s * HW : (s + 1) * HW],
                jnp.zeros((6, HW), F32),
            ],
            axis=0,
        )
    grad_t = (grad_t * near_weight).astype(BF16)
    delta = near_weight * delta
    back = jnp.zeros((DH, PAIR), F32)
    for z in range(4):
        rows = slice(z * PAIR, (z + 1) * PAIR)
        d_probs = mm(kv[z, 1, 0], grad_t)
        d_scores = (kept[rows, :].astype(F32) * (d_probs - delta)).astype(BF16)
        grads[rows, :] = d_scores
        dkv[z, 1, 0] = mm_nt(kept[rows, :], grad_t).astype(BF16)
        dkv[z, 0, 0] = (mm(d_scores, query) * SCALE).astype(BF16)
        back = back + mm(turn(kv[z, 0, 0]).astype(BF16), d_scores)
    dq[0] = (back * SCALE).T.astype(BF16)


def near(kv, packed, far):
    return pl.pallas_call(
        near_kernel,
        grid=(HALF,),
        in_specs=[
            pl.BlockSpec((4, 2, 1, PAIR, DH), lambda h: (0, 0, h, 0, 0)),
            pl.BlockSpec((2, 1, ROWS, DH), lambda h: (0, h, 0, 0)),
            pl.BlockSpec((2, 1, DH + 16, HW), lambda h: (0, h, 0, 0)),
        ],
        out_specs=[
            pl.BlockSpec((4, 2, 1, PAIR, DH), lambda h: (0, 0, h, 0, 0)),
            pl.BlockSpec((1, PAIR, DH), lambda h: (h, 0, 0)),
            pl.BlockSpec((1, PAIR, DH), lambda h: (h, 0, 0)),
            pl.BlockSpec((2, 1, 8, HW), lambda h: (0, h, 0, 0)),
        ],
        out_shape=[
            jax.ShapeDtypeStruct((4, 2, HALF, PAIR, DH), BF16),
            jax.ShapeDtypeStruct((HALF, PAIR, DH), BF16),
            jax.ShapeDtypeStruct((HALF, PAIR, DH), BF16),
            jax.ShapeDtypeStruct((2, HALF, 8, HW), F32),
        ],
        scratch_shapes=[
            pltpu.VMEM((4 * PAIR, PAIR), F32),
            pltpu.VMEM((4 * PAIR, PAIR), BF16),
            pltpu.VMEM((4 * PAIR, PAIR), BF16),
        ],
        compiler_params=params(),
        cost_estimate=pl.CostEstimate(
            flops=12 * HALF * 4 * PAIR * PAIR * DH,
            bytes_accessed=6_000_000,
            transcendentals=HALF * 4 * PAIR * PAIR,
        ),
        name="near",
    )(kv, packed, far)


def far_backward_kernel(mine, past, kept, told, own, back, keys_t, values, dk, dv, grads):
    for j in range(GROUP):
        keys_t[:, j * HW : (j + 1) * HW] = turn(past[j, :HW, :]).astype(BF16)
        keys_t[:, (GROUP + j) * HW : (GROUP + j + 1) * HW] = turn(
            mine[j, K0 : K0 + HW, :]
        ).astype(BF16)
        values[j * HW : (j + 1) * HW, :] = past[j, HW : 2 * HW, :]
        values[(GROUP + j) * HW : (GROUP + j + 1) * HW, :] = mine[j, V0 : V0 + HW, :]
    dk[...] = jnp.zeros_like(dk)
    dv[...] = jnp.zeros_like(dv)
    for p in range(GROUP // 2):
        query = jnp.concatenate([mine[2 * p, :HW, :], mine[2 * p + 1, :HW, :]], axis=0)
        grad_t = jnp.concatenate(
            [turn(mine[2 * p, G0 : G0 + HW, :]), turn(mine[2 * p + 1, G0 : G0 + HW, :])], axis=1
        )
        stats = jnp.concatenate([told[2 * p], told[2 * p + 1]], axis=1)
        weight = stats[0:1, :]
        delta = stats[1:2, :]
        grad_t = (grad_t * weight).astype(BF16)
        at = p * PAIR
        for lo, size in ((0, 384), (384, 384), (768, 384)):
            rows = slice(lo, lo + size)
            spot = slice(at + lo, at + lo + size)
            d_probs = mm(values[spot, :], grad_t)
            block = kept[p, rows, :]
            d_scores = (block.astype(F32) * (d_probs - delta)).astype(BF16)
            grads[rows, :] = d_scores
            dv[spot, :] += mm_nt(block, grad_t)
            dk[spot, :] += mm(d_scores, query)
        d_query = (mm(keys_t[:, at : at + KEYS], grads[...]) * SCALE).T.astype(BF16)
        own[2 * p, :HW, :] = d_query[:HW]
        own[2 * p + 1, :HW, :] = d_query[HW:]
    for j in range(GROUP):
        early = slice(j * HW, (j + 1) * HW)
        late = slice((GROUP + j) * HW, (GROUP + j + 1) * HW)
        back[j, :HW, :] = (dk[early, :] * SCALE).astype(BF16)
        back[j, HW:, :] = dv[early, :].astype(BF16)
        own[j, HW : 2 * HW, :] = (dk[late, :] * SCALE).astype(BF16)
        own[j, 2 * HW :, :] = dv[late, :].astype(BF16)


def far_backward(mine, past, kept, told):
    return pl.pallas_call(
        far_backward_kernel,
        in_specs=[VM] * 4,
        out_specs=[VM, VM],
        out_shape=[
            jax.ShapeDtypeStruct((GROUP, 3 * HW, DH), BF16),
            jax.ShapeDtypeStruct((GROUP, 2 * HW, DH), BF16),
        ],
        scratch_shapes=[
            pltpu.VMEM((DH, 2 * GROUP * HW), BF16),
            pltpu.VMEM((2 * GROUP * HW, DH), BF16),
            pltpu.VMEM((2 * GROUP * HW, DH), F32),
            pltpu.VMEM((2 * GROUP * HW, DH), F32),
            pltpu.VMEM((KEYS, PAIR), BF16),
        ],
        compiler_params=params(),
        cost_estimate=pl.CostEstimate(
            flops=32 * KEYS * PAIR * DH, bytes_accessed=6_000_000, transcendentals=0
        ),
        name="far_backward",
    )(mine, past, kept, told)


def mix_kernel(core, attended, wo, own, other):
    del core
    rows = jnp.concatenate([attended[h] for h in range(HALF)], axis=1)
    out = mm(rows, wo[...])
    own[...] = out[:HW]
    other[...] = out[HW:].astype(BF16)


def mix(core, attended, w_out):
    return pl.pallas_call(
        mix_kernel,
        grid_spec=pltpu.PrefetchScalarGridSpec(
            num_scalar_prefetch=1,
            grid=(1,),
            in_specs=[
                pl.BlockSpec((HALF, PAIR, DH), lambda i, core: (0, 0, 0)),
                pl.BlockSpec((HALF * DH, D), lambda i, core: (core[0], 0)),
            ],
            out_specs=[pl.BlockSpec((HW, D), lambda i, core: (0, 0))] * 2,
        ),
        out_shape=[jax.ShapeDtypeStruct((HW, D), F32), jax.ShapeDtypeStruct((HW, D), BF16)],
        compiler_params=params(),
        cost_estimate=pl.CostEstimate(
            flops=2 * PAIR * D * HALF * DH, bytes_accessed=2_000_000, transcendentals=0
        ),
        name="mix",
    )(core, attended, w_out)


def unproject_kernel(core, dq, dkv, far, wq, wk, wv, own, other):
    del core
    total = jnp.zeros((PAIR, D), F32)
    for part, weight in enumerate((wq, wk, wv)):
        pieces = []
        for h in range(HALF):
            rows = slice(part * HW, (part + 1) * HW)
            away = jnp.concatenate([far[0, h, rows, :], far[1, h, rows, :]], axis=0)
            close = dq[h] if part == 0 else dkv[part - 1, h]
            pieces.append((away.astype(F32) + close.astype(F32)).astype(BF16))
        total = total + mm_nt(jnp.concatenate(pieces, axis=1), weight[...])
    own[...] = total[:HW]
    other[...] = total[HW:].astype(BF16)


def unproject(core, dq, dkv, far, w_qkv):
    whole = lambda shape: pl.BlockSpec(shape, lambda i, core: (0,) * len(shape))
    part = lambda at: pl.BlockSpec((D, HALF * DH), lambda i, core: (0, at * 2 + core[0]))
    return pl.pallas_call(
        unproject_kernel,
        grid_spec=pltpu.PrefetchScalarGridSpec(
            num_scalar_prefetch=1,
            grid=(1,),
            in_specs=[
                whole((HALF, PAIR, DH)),
                whole((2, HALF, PAIR, DH)),
                whole((2, HALF, 3 * HW, DH)),
                part(0),
                part(1),
                part(2),
            ],
            out_specs=[whole((HW, D))] * 2,
        ),
        out_shape=[jax.ShapeDtypeStruct((HW, D), F32), jax.ShapeDtypeStruct((HW, D), BF16)],
        compiler_params=params(),
        cost_estimate=pl.CostEstimate(
            flops=2 * PAIR * D * 3 * HALF * DH, bytes_accessed=5_000_000, transcendentals=0
        ),
        name="unproject",
    )(core, dq, dkv, far, w_qkv, w_qkv, w_qkv)


def finish_kernel(tokens, cot, gain, own, other, out):
    x = tokens[...].astype(F32)
    rinv = lax.rsqrt(jnp.mean(x * x, axis=-1, keepdims=True) + EPS)
    scaled = (own[...] + other[...].astype(F32)) * gain[...]
    mean = jnp.mean(scaled * x, axis=-1, keepdims=True)
    grad = rinv * scaled - x * (rinv * rinv * rinv * mean)
    out[...] = (cot[...].astype(F32) + grad).astype(BF16)


def finish(tokens, cot, gain, own, other):
    return pl.pallas_call(
        finish_kernel,
        in_specs=[VM] * 5,
        out_specs=VM,
        out_shape=jax.ShapeDtypeStruct((HW, D), BF16),
        compiler_params=params(),
        cost_estimate=pl.CostEstimate(flops=HW * D * 10, bytes_accessed=2_000_000, transcendentals=0),
        name="finish",
    )(tokens, cot, gain, own, other)


SWAP = [(0, 1), (1, 0)]
LANE = ("x", "zl")


def swap(value):
    return lax.ppermute(value, "core", SWAP)


def exchange(value):
    return lax.all_to_all(value, LANE, 0, 0, tiled=True)


def per_device(tokens, gain, w_qkv, w_out, window, valid, cotangent):
    rows = lax.axis_size("y")
    core = lax.axis_index("core").astype(jnp.int32)
    lane = lax.axis_index(LANE).astype(jnp.int32)
    tokens = tokens.reshape(HW, D)
    cot = cotangent.reshape(HW, D)
    gain = gain.reshape(1, D)
    core_arg = core.reshape(1)
    other_tokens = swap(tokens)
    other_cot = swap(cot)
    width = lax.dynamic_slice(window, (core * HALF + lane % HALF,), (1,))
    packed, kv = project(
        core_arg, valid, tokens, other_tokens, cot, other_cot, gain, w_qkv, w_out
    )
    near_kv = lax.all_gather(kv, "zh", axis=0)
    mine = exchange(packed.reshape(2 * HALF, ROWS, DH))
    past = lax.ppermute(mine[:, K0:, :], "y", [(i, i + 1) for i in range(rows - 1)])
    sent, kept = far_forward(width, mine, past)
    far = exchange(sent).reshape(2, HALF, DH + 16, HW)
    dkv, dq, attended, told = near(near_kv, packed, far)
    dkv = lax.psum_scatter(dkv, "zh", scatter_dimension=0)
    told = exchange(told.reshape(2 * HALF, 8, HW))
    own, back = far_backward(mine, past, kept, told)
    back = lax.ppermute(back, "y", [(i + 1, i) for i in range(rows - 1)])
    summed = (own[:, HW:, :].astype(F32) + back.astype(F32)).astype(BF16)
    own = jnp.concatenate([own[:, :HW, :], summed], axis=1)
    far_grads = exchange(own).reshape(2, HALF, 3 * HW, DH)
    mixed_own, mixed_other = mix(core_arg, attended, w_out)
    mixed_other = swap(mixed_other)
    mixed = (tokens.astype(F32) + (mixed_own + mixed_other.astype(F32))).astype(BF16)
    grad_own, grad_other = unproject(core_arg, dq, dkv, far_grads, w_qkv)
    grad_other = swap(grad_other)
    d_tokens = finish(tokens, cot, gain, grad_own, grad_other)
    return mixed.reshape(1, 1, HW, D), d_tokens.reshape(1, 1, HW, D)


def solution(mesh):
    grid = Mesh(mesh.devices.reshape(4, 4, 2, 4, 2), ("y", "x", "zl", "zh", "core"))
    frames, cams = ("y", "x", "zl"), ("zh", "core")
    split = P(frames, cams, None, None)
    return jax.shard_map(
        per_device,
        mesh=grid,
        in_specs=(split, P(), P(), P(), P(), P(frames), split),
        out_specs=(split, split),
        check_vma=False,
    )
```

```python
import math

import jax
import jax.numpy as jnp
from jax import lax
from jax.experimental import pallas as pl
from jax.experimental.pallas import tpu as pltpu
from jax.sharding import Mesh
from jax.sharding import PartitionSpec as P

D = 1024
H = 8
DH = 128
HW = 128
WIN = 8
EPS = 1e-05

HALF = H // 2
PAIR = 2 * HW
GROUP = 8
SCALE = DH ** (-0.5)
SCALE2 = SCALE * math.log2(math.e)
FLOOR = -3.0e38
F32 = jnp.float32
BF16 = jnp.bfloat16
NT = (((1,), (1,)), ((), ()))
VMEM_LIMIT = 20 * 1024 * 1024
STAGE_LIMIT = 48 * 1024 * 1024

Q0, G0, K0, V0, OK0, ROWS = 0, 128, 256, 384, 512, 528
TOKENS = 8 * HW
KEYS = (WIN + 1) * HW


def params(**kw):
    return pltpu.CompilerParams(vmem_limit_bytes=VMEM_LIMIT, **kw)


def mm(a, b):
    return jnp.dot(a, b, preferred_element_type=F32)


def mm_nt(a, b):
    return lax.dot_general(a, b, NT, preferred_element_type=F32)


def turn(a):
    return a.astype(F32).T


VM = pl.BlockSpec(memory_space=pltpu.VMEM)
SM = pl.BlockSpec(memory_space=pltpu.SMEM)
ANY = pl.BlockSpec(memory_space=pltpu.HBM)


def cost(flops, size, exps=0):
    return pl.CostEstimate(flops=flops, bytes_accessed=size, transcendentals=exps)


def stage_kernel(place, tokens, cot, gain, w_qkv, w_out, own, own_cot, own_gain, wq, wk, wv, out, sems):
    core = place[0]
    copies = [
        pltpu.make_async_copy(tokens, own, sems.at[0]),
        pltpu.make_async_copy(cot, own_cot, sems.at[1]),
        pltpu.make_async_copy(gain, own_gain, sems.at[2]),
        pltpu.make_async_copy(
            w_out.at[pl.ds(pl.multiple_of(core * HALF * DH, HALF * DH), HALF * DH), :],
            out,
            sems.at[3],
        ),
    ]
    for part in range(3):
        start = pl.multiple_of(part * D + core * HALF * DH, HALF * DH)
        copies.append(
            pltpu.make_async_copy(
                w_qkv.at[:, pl.ds(start, HALF * DH)], (wq, wk, wv)[part], sems.at[4 + part]
            )
        )
    for copy in copies:
        copy.start()
    for copy in copies:
        copy.wait()


def stage(place, tokens, cot, gain, w_qkv, w_out):
    return pl.pallas_call(
        stage_kernel,
        in_specs=[SM] + [ANY] * 5,
        out_specs=[VM] * 7,
        out_shape=[
            jax.ShapeDtypeStruct((HW, D), BF16),
            jax.ShapeDtypeStruct((HW, D), BF16),
            jax.ShapeDtypeStruct((1, D), F32),
        ]
        + [jax.ShapeDtypeStruct((D, HALF * DH), BF16)] * 3
        + [jax.ShapeDtypeStruct((HALF * DH, D), BF16)],
        scratch_shapes=[pltpu.SemaphoreType.DMA((7,))],
        compiler_params=pltpu.CompilerParams(vmem_limit_bytes=STAGE_LIMIT),
        cost_estimate=cost(0, 9_000_000),
        name="stage",
    )(place, tokens, cot, gain, w_qkv, w_out)


def project_kernel(
    place, valid, own, other, cot_own, cot_other, gain, wq, wk, wv, wo, packed, near0, near1, near2, near3
):
    x = jnp.concatenate([own[...], other[...]], axis=0).astype(F32)
    rinv = lax.rsqrt(jnp.mean(x * x, axis=-1, keepdims=True) + EPS)
    normed = (x * rinv * gain[...]).astype(BF16)
    cot = jnp.concatenate([cot_own[...], cot_other[...]], axis=0)
    flags = jnp.full((ROWS - OK0, DH), valid[0], jnp.int32).astype(F32).astype(BF16)
    for row in (Q0, K0, V0, G0):
        if row == G0:
            got = mm_nt(cot, wo[...]).astype(BF16)
        else:
            got = mm(normed, {Q0: wq, K0: wk, V0: wv}[row][...]).astype(BF16)
        for h in range(HALF):
            for s in range(2):
                packed[h, s, row : row + HW, :] = got[s * HW : (s + 1) * HW, h * DH : (h + 1) * DH]
    for h in range(HALF):
        for s in range(2):
            packed[h, s, OK0:ROWS, :] = flags
    for step, near in enumerate((near0, near1, near2, near3)):
        h = lax.rem(place[2] + step, HALF)
        for s in range(2):
            near[s] = packed[h, s, :OK0, :]


def project(place, valid, own, other, cot_own, cot_other, gain, weights):
    return pl.pallas_call(
        project_kernel,
        in_specs=[SM, SM] + [VM] * 9,
        out_specs=[VM] * 5,
        out_shape=[jax.ShapeDtypeStruct((HALF, 2, ROWS, DH), BF16)]
        + [jax.ShapeDtypeStruct((2, OK0, DH), BF16)] * 4,
        compiler_params=params(),
        cost_estimate=cost(2 * PAIR * D * 4 * HALF * DH, 7_000_000),
        name="project",
    )(place, valid, own, other, cot_own, cot_other, gain, *weights)


def both(block, row):
    return jnp.concatenate([block[0, row : row + HW, :], block[1, row : row + HW, :]], axis=0)


def near_forward_kernel(near0, near1, near2, near3, kept, result, stats, scores):
    blocks = (near0, near1, near2, near3)
    turned = [turn(both(block, V0)).astype(BF16) for block in blocks]
    for g in range(4):
        cols = slice(g * PAIR, (g + 1) * PAIR)
        query = both(blocks[g], Q0)
        grad_t = turn(both(blocks[g], G0))
        peak = jnp.full((1, PAIR), -jnp.inf, F32)
        for z in range(4):
            block = mm_nt(both(blocks[z], K0), query)
            scores[z * PAIR : (z + 1) * PAIR, :] = block
            peak = jnp.maximum(peak, jnp.max(block, axis=0, keepdims=True))
        peak = peak * SCALE2
        total = jnp.zeros((1, PAIR), F32)
        for b in range(8):
            rows = slice(b * HW, (b + 1) * HW)
            block = jnp.exp2(scores[rows, :] * SCALE2 - peak)
            total = total + jnp.sum(block, axis=0, keepdims=True)
            kept[rows, cols] = block.astype(BF16)
        got = jnp.zeros((DH, PAIR), F32)
        for z in range(4):
            got = got + mm(turned[z], kept[z * PAIR : (z + 1) * PAIR, cols])
        result[:, cols] = got
        delta = jnp.sum(got * grad_t, axis=0, keepdims=True)
        told = jnp.concatenate([peak, total, delta, jnp.zeros((1, PAIR), F32)], axis=0)
        stats[2 * g] = told[:, :HW]
        stats[2 * g + 1] = told[:, HW:]


def near_forward(*blocks):
    return pl.pallas_call(
        near_forward_kernel,
        in_specs=[VM] * 4,
        out_specs=[VM] * 3,
        out_shape=[
            jax.ShapeDtypeStruct((TOKENS, TOKENS), BF16),
            jax.ShapeDtypeStruct((DH, TOKENS), F32),
            jax.ShapeDtypeStruct((8, 4, HW), F32),
        ],
        scratch_shapes=[pltpu.VMEM((TOKENS, PAIR), F32)],
        compiler_params=params(),
        cost_estimate=cost(4 * TOKENS * TOKENS * DH, 4_000_000, TOKENS * TOKENS),
        name="near_forward",
    )(*blocks)


def slot_of_near(place, step, s):
    zh = place[2]
    cam = lax.rem(zh + 4 - step, 4)
    return (zh * 2 + s) * 4 + cam


def far_forward_kernel(place, win, mine, past, close, told, kept, result, keys, values_t, scores):
    width = win[place[0] * HALF + place[1]]
    told[...] = jnp.zeros_like(told)
    for step in range(4):
        for s in range(2):
            told[slot_of_near(place, step, s), 0:4, :] = close[2 * step + s]
    for j in range(GROUP):
        keys[j * HW : (j + 1) * HW, :] = past[j, :HW, :]
        keys[(GROUP + j) * HW : (GROUP + j + 1) * HW, :] = mine[j, K0 : K0 + HW, :]
        values_t[:, j * HW : (j + 1) * HW] = turn(past[j, HW : 2 * HW, :]).astype(BF16)
        values_t[:, (GROUP + j) * HW : (GROUP + j + 1) * HW] = turn(
            mine[j, V0 : V0 + HW, :]
        ).astype(BF16)
    for p in range(GROUP // 2):
        query = jnp.concatenate([mine[2 * p, :HW, :], mine[2 * p + 1, :HW, :]], axis=0)
        grad_t = jnp.concatenate(
            [turn(mine[2 * p, G0 : G0 + HW, :]), turn(mine[2 * p + 1, G0 : G0 + HW, :])], axis=1
        )
        peak = jnp.full((1, PAIR), -jnp.inf, F32)
        for b in range(WIN + 1):
            j = 2 * p + b
            if j < GROUP:
                flag = past[j, 2 * HW : 2 * HW + 1, :].astype(F32)
            else:
                flag = mine[j - GROUP, OK0 : OK0 + 1, :].astype(F32)
            lower = jnp.where((flag > 0.5) & (b >= WIN - width) & (b < WIN), 0.0, -jnp.inf)
            upper = jnp.where((flag > 0.5) & (b >= WIN + 1 - width), 0.0, -jnp.inf)
            bias = jnp.concatenate([lower, upper], axis=1)
            block = mm_nt(keys[j * HW : (j + 1) * HW, :], query) + bias
            scores[b * HW : (b + 1) * HW, :] = block
            peak = jnp.maximum(peak, jnp.max(block, axis=0, keepdims=True))
        peak = jnp.maximum(peak * SCALE2, FLOOR)
        total = jnp.zeros((1, PAIR), F32)
        for b in range(WIN + 1):
            block = jnp.exp2(scores[b * HW : (b + 1) * HW, :] * SCALE2 - peak)
            total = total + jnp.sum(block, axis=0, keepdims=True)
            kept[p, b * HW : (b + 1) * HW, :] = block.astype(BF16)
        got = mm(values_t[:, p * PAIR : p * PAIR + KEYS], kept[p])
        result[:, p * PAIR : (p + 1) * PAIR] = got
        delta = jnp.sum(got * grad_t, axis=0, keepdims=True)
        stats = jnp.concatenate([peak, total, delta, jnp.zeros((1, PAIR), F32)], axis=0)
        told[2 * p * 4 + place[1], 4:8, :] = stats[:, :HW]
        told[(2 * p + 1) * 4 + place[1], 4:8, :] = stats[:, HW:]


def far_forward(place, window, mine, past, close):
    return pl.pallas_call(
        far_forward_kernel,
        in_specs=[SM, SM, VM, VM, VM],
        out_specs=[VM] * 3,
        out_shape=[
            jax.ShapeDtypeStruct((32, 8, HW), F32),
            jax.ShapeDtypeStruct((GROUP // 2, KEYS, PAIR), BF16),
            jax.ShapeDtypeStruct((DH, GROUP * HW), F32),
        ],
        scratch_shapes=[
            pltpu.VMEM((2 * GROUP * HW, DH), BF16),
            pltpu.VMEM((DH, 2 * GROUP * HW), BF16),
            pltpu.VMEM((KEYS, PAIR), F32),
        ],
        compiler_params=params(),
        cost_estimate=cost(16 * KEYS * PAIR * DH, 5_000_000, 4 * KEYS * PAIR),
        name="far_forward",
    )(place, window, mine, past, close)


def merge(this, other):
    top = jnp.maximum(this[0:1], other[0:1])
    here = jnp.exp2(this[0:1] - top)
    there = jnp.exp2(other[0:1] - top)
    inverse = 1.0 / (here * this[1:2] + there * other[1:2])
    here = here * inverse
    delta = here * this[2:3] + there * inverse * other[2:3]
    return here, here * delta


def near_backward_kernel(
    place, near0, near1, near2, near3, kept, result, stats, told,
    back0, back1, back2, back3, grads, grad_all, query_all,
):
    blocks = (near0, near1, near2, near3)
    outs = (back0, back1, back2, back3)
    for g in range(4):
        cols = slice(g * PAIR, (g + 1) * PAIR)
        this = jnp.concatenate([stats[2 * g], stats[2 * g + 1]], axis=1)
        other = jnp.concatenate(
            [told[slot_of_near(place, g, s), 4:8, :] for s in range(2)], axis=1
        )
        weight, delta = merge(this, other)
        grad_t = (turn(both(blocks[g], G0)) * weight).astype(BF16)
        grad_all[:, cols] = grad_t
        query_all[cols, :] = both(blocks[g], Q0)
        attended = (result[:, cols] * weight).T.astype(BF16)
        for s in range(2):
            outs[g][s, :HW, :] = attended[s * HW : (s + 1) * HW]
        for z in range(4):
            rows = slice(z * PAIR, (z + 1) * PAIR)
            d_probs = mm(both(blocks[z], V0), grad_t)
            grads[rows, cols] = (kept[rows, cols].astype(F32) * (d_probs - delta)).astype(BF16)
    for z in range(4):
        rows = slice(z * PAIR, (z + 1) * PAIR)
        d_values = mm_nt(kept[rows, :], grad_all[...]).astype(BF16)
        d_keys = (mm(grads[rows, :], query_all[...]) * SCALE).astype(BF16)
        for s in range(2):
            outs[z][s, 2 * HW : 3 * HW, :] = d_keys[s * HW : (s + 1) * HW]
            outs[z][s, 3 * HW :, :] = d_values[s * HW : (s + 1) * HW]
    keys_t = jnp.concatenate([turn(both(block, K0)).astype(BF16) for block in blocks], axis=1)
    for g in range(4):
        cols = slice(g * PAIR, (g + 1) * PAIR)
        d_query = (mm(keys_t, grads[:, cols]) * SCALE).T.astype(BF16)
        for s in range(2):
            outs[g][s, HW : 2 * HW, :] = d_query[s * HW : (s + 1) * HW]


def near_backward(place, blocks, kept, result, stats, told):
    return pl.pallas_call(
        near_backward_kernel,
        in_specs=[SM] + [VM] * 8,
        out_specs=[VM] * 4,
        out_shape=[jax.ShapeDtypeStruct((2, 4 * HW, DH), BF16)] * 4,
        scratch_shapes=[
            pltpu.VMEM((TOKENS, TOKENS), BF16),
            pltpu.VMEM((DH, TOKENS), BF16),
            pltpu.VMEM((TOKENS, DH), BF16),
        ],
        compiler_params=params(),
        cost_estimate=cost(8 * TOKENS * TOKENS * DH, 5_000_000),
        name="near_backward",
    )(place, *blocks, kept, result, stats, told)


def far_backward_kernel(
    place, mine, past, kept, result, sent, told, own, back, keys_t, values, dk, dv, grads
):
    for j in range(GROUP):
        keys_t[:, j * HW : (j + 1) * HW] = turn(past[j, :HW, :]).astype(BF16)
        keys_t[:, (GROUP + j) * HW : (GROUP + j + 1) * HW] = turn(
            mine[j, K0 : K0 + HW, :]
        ).astype(BF16)
        values[j * HW : (j + 1) * HW, :] = past[j, HW : 2 * HW, :]
        values[(GROUP + j) * HW : (GROUP + j + 1) * HW, :] = mine[j, V0 : V0 + HW, :]
    dk[...] = jnp.zeros_like(dk)
    dv[...] = jnp.zeros_like(dv)
    for p in range(GROUP // 2):
        query = jnp.concatenate([mine[2 * p, :HW, :], mine[2 * p + 1, :HW, :]], axis=0)
        grad_t = jnp.concatenate(
            [turn(mine[2 * p, G0 : G0 + HW, :]), turn(mine[2 * p + 1, G0 : G0 + HW, :])], axis=1
        )
        slots = [(2 * p + i) * 4 + place[1] for i in range(2)]
        this = jnp.concatenate([sent[slot, 4:8, :] for slot in slots], axis=1)
        other = jnp.concatenate([told[slot, 0:4, :] for slot in slots], axis=1)
        weight, delta = merge(this, other)
        grad_t = (grad_t * weight).astype(BF16)
        at = p * PAIR
        attended = (result[:, at : at + PAIR] * weight).T.astype(BF16)
        for lo, size in ((0, 384), (384, 384), (768, 384)):
            rows = slice(lo, lo + size)
            spot = slice(at + lo, at + lo + size)
            d_probs = mm(values[spot, :], grad_t)
            block = kept[p, rows, :]
            d_scores = (block.astype(F32) * (d_probs - delta)).astype(BF16)
            grads[rows, :] = d_scores
            dv[spot, :] += mm_nt(block, grad_t)
            dk[spot, :] += mm(d_scores, query)
        d_query = (mm(keys_t[:, at : at + KEYS], grads[...]) * SCALE).T.astype(BF16)
        for i in range(2):
            own[2 * p + i, :HW, :] = attended[i * HW : (i + 1) * HW]
            own[2 * p + i, HW : 2 * HW, :] = d_query[i * HW : (i + 1) * HW]
    for j in range(GROUP):
        early = slice(j * HW, (j + 1) * HW)
        late = slice((GROUP + j) * HW, (GROUP + j + 1) * HW)
        back[j, :HW, :] = (dk[early, :] * SCALE).astype(BF16)
        back[j, HW:, :] = dv[early, :].astype(BF16)
        own[j, 2 * HW : 3 * HW, :] = (dk[late, :] * SCALE).astype(BF16)
        own[j, 3 * HW :, :] = dv[late, :].astype(BF16)


def far_backward(place, mine, past, kept, result, sent, told):
    return pl.pallas_call(
        far_backward_kernel,
        in_specs=[SM] + [VM] * 6,
        out_specs=[VM, VM],
        out_shape=[
            jax.ShapeDtypeStruct((GROUP, 4 * HW, DH), BF16),
            jax.ShapeDtypeStruct((GROUP, 2 * HW, DH), BF16),
        ],
        scratch_shapes=[
            pltpu.VMEM((DH, 2 * GROUP * HW), BF16),
            pltpu.VMEM((2 * GROUP * HW, DH), BF16),
            pltpu.VMEM((2 * GROUP * HW, DH), F32),
            pltpu.VMEM((2 * GROUP * HW, DH), F32),
            pltpu.VMEM((KEYS, PAIR), BF16),
        ],
        compiler_params=params(),
        cost_estimate=cost(32 * KEYS * PAIR * DH, 6_000_000),
        name="far_backward",
    )(place, mine, past, kept, result, sent, told)


def unproject_kernel(place, near0, near1, near2, near3, far, wq, wk, wv, wo, own, other, close):
    for step, near in enumerate((near0, near1, near2, near3)):
        close[lax.rem(place[2] + step, HALF)] = near[...]
    parts = []
    for part in range(4):
        rows = slice(part * HW, (part + 1) * HW)
        pieces = []
        for h in range(HALF):
            away = jnp.concatenate([far[h, 0, rows, :], far[h, 1, rows, :]], axis=0)
            here = jnp.concatenate([close[h, 0, rows, :], close[h, 1, rows, :]], axis=0)
            pieces.append((away.astype(F32) + here.astype(F32)).astype(BF16))
        parts.append(jnp.concatenate(pieces, axis=1))
    mixed = mm(parts[0], wo[...])
    total = mm_nt(parts[1], wq[...]) + mm_nt(parts[2], wk[...]) + mm_nt(parts[3], wv[...])
    own[0] = mixed[:HW]
    own[1] = total[:HW]
    other[0] = mixed[HW:].astype(BF16)
    other[1] = total[HW:].astype(BF16)


def unproject(place, blocks, far, weights):
    return pl.pallas_call(
        unproject_kernel,
        in_specs=[SM] + [VM] * 9,
        out_specs=[VM, VM],
        out_shape=[jax.ShapeDtypeStruct((2, HW, D), F32), jax.ShapeDtypeStruct((2, HW, D), BF16)],
        scratch_shapes=[pltpu.VMEM((HALF, 2, 4 * HW, DH), BF16)],
        compiler_params=params(),
        cost_estimate=cost(2 * PAIR * D * 4 * HALF * DH, 8_000_000),
        name="unproject",
    )(place, *blocks, far, *weights)


def finish_kernel(tokens, cot, gain, own, other, mixed, out):
    x = tokens[...].astype(F32)
    mixed[...] = (x + (own[0] + other[0].astype(F32))).astype(BF16)
    rinv = lax.rsqrt(jnp.mean(x * x, axis=-1, keepdims=True) + EPS)
    scaled = (own[1] + other[1].astype(F32)) * gain[...]
    mean = jnp.mean(scaled * x, axis=-1, keepdims=True)
    grad = rinv * scaled - x * (rinv * rinv * rinv * mean)
    out[...] = (cot[...].astype(F32) + grad).astype(BF16)


def finish(tokens, cot, gain, own, other):
    return pl.pallas_call(
        finish_kernel,
        in_specs=[VM] * 5,
        out_specs=[VM] * 2,
        out_shape=[jax.ShapeDtypeStruct((HW, D), BF16)] * 2,
        compiler_params=params(),
        cost_estimate=cost(HW * D * 10, 3_000_000),
        name="finish",
    )(tokens, cot, gain, own, other)


LANE = ("x", "zl")


def swap(value):
    return lax.ppermute(value, "core", [(0, 1), (1, 0)])


def turn_ring(value, steps):
    return lax.ppermute(value, "zh", [(i, (i + steps) % 4) for i in range(4)])


def exchange(value, axes):
    return lax.all_to_all(value, axes, 0, 0, tiled=True)


def per_device(tokens, gain, w_qkv, w_out, window, valid, cotangent):
    rows = lax.axis_size("y")
    place = jnp.stack(
        [lax.axis_index(axis) for axis in ("core", "x", "zh")]
    ).astype(jnp.int32)
    tokens = tokens.reshape(HW, D)
    cot = cotangent.reshape(HW, D)
    other_tokens = swap(tokens)
    other_cot = swap(cot)
    tokens, cot, gain, *weights = stage(place, tokens, cot, gain.reshape(1, D), w_qkv, w_out)
    packed, *blocks = project(
        place, valid, tokens, other_tokens, cot, other_cot, gain, weights
    )
    blocks = [blocks[0]] + [turn_ring(blocks[step], step) for step in (1, 2, 3)]
    mine = exchange(packed.reshape(2 * HALF, ROWS, DH), LANE)
    past = lax.ppermute(mine[:, K0:, :], "y", [(i, i + 1) for i in range(rows - 1)])
    near_kept, near_result, close = near_forward(*blocks)
    sent, far_kept, far_result = far_forward(place, window, mine, past, close)
    told = exchange(sent, ("x", "zl", "zh"))
    own, back = far_backward(place, mine, past, far_kept, far_result, sent, told)
    back = lax.ppermute(back, "y", [(i + 1, i) for i in range(rows - 1)])
    returned = near_backward(place, blocks, near_kept, near_result, close, told)
    returned = [returned[0]] + [turn_ring(returned[step], -step) for step in (1, 2, 3)]
    summed = (own[:, 2 * HW :, :].astype(F32) + back.astype(F32)).astype(BF16)
    own = jnp.concatenate([own[:, : 2 * HW, :], summed], axis=1)
    far = exchange(own, LANE).reshape(HALF, 2, 4 * HW, DH)
    out_own, out_other = unproject(place, returned, far, weights)
    mixed, d_tokens = finish(tokens, cot, gain, out_own, swap(out_other))
    return mixed.reshape(1, 1, HW, D), d_tokens.reshape(1, 1, HW, D)


def solution(mesh):
    grid = Mesh(mesh.devices.reshape(4, 4, 2, 4, 2), ("y", "x", "zl", "zh", "core"))
    frames, cams = ("y", "x", "zl"), ("zh", "core")
    split = P(frames, cams, None, None)
    return jax.shard_map(
        per_device,
        mesh=grid,
        in_specs=(split, P(), P(), P(), P(), P(frames), split),
        out_specs=(split, split),
        check_vma=False,
    )
```

```python
import math

import jax
import jax.numpy as jnp
from jax import lax
from jax.experimental import pallas as pl
from jax.experimental.pallas import tpu as pltpu
from jax.sharding import Mesh
from jax.sharding import PartitionSpec as P

D = 1024
H = 8
DH = 128
HW = 128
WIN = 8
EPS = 1e-05

HALF = H // 2
PAIR = 2 * HW
GROUP = 8
SCALE = DH ** (-0.5)
SCALE2 = SCALE * math.log2(math.e)
FLOOR = -3.0e38
F32 = jnp.float32
BF16 = jnp.bfloat16
NT = (((1,), (1,)), ((), ()))
VMEM_LIMIT = 20 * 1024 * 1024
STAGE_LIMIT = 48 * 1024 * 1024

Q0, G0, K0, V0, OK0, ROWS = 0, 128, 256, 384, 512, 528
TOKENS = 8 * HW
KEYS = (WIN + 1) * HW


def params(**kw):
    return pltpu.CompilerParams(vmem_limit_bytes=VMEM_LIMIT, **kw)


def mm(a, b):
    return jnp.dot(a, b, preferred_element_type=F32)


def mm_nt(a, b):
    return lax.dot_general(a, b, NT, preferred_element_type=F32)


def turn(a):
    return a.astype(F32).T


VM = pl.BlockSpec(memory_space=pltpu.VMEM)
SM = pl.BlockSpec(memory_space=pltpu.SMEM)
ANY = pl.BlockSpec(memory_space=pltpu.HBM)


def cost(flops, size, exps=0):
    return pl.CostEstimate(flops=flops, bytes_accessed=size, transcendentals=exps)


def stage_kernel(place, tokens, cot, gain, w_qkv, w_out, own, own_cot, own_gain, wq, wk, wv, out, sems):
    core = place[0]
    copies = [
        pltpu.make_async_copy(tokens, own, sems.at[0]),
        pltpu.make_async_copy(cot, own_cot, sems.at[1]),
        pltpu.make_async_copy(gain, own_gain, sems.at[2]),
        pltpu.make_async_copy(
            w_out.at[pl.ds(pl.multiple_of(core * HALF * DH, HALF * DH), HALF * DH), :],
            out,
            sems.at[3],
        ),
    ]
    for part in range(3):
        start = pl.multiple_of(part * D + core * HALF * DH, HALF * DH)
        copies.append(
            pltpu.make_async_copy(
                w_qkv.at[:, pl.ds(start, HALF * DH)], (wq, wk, wv)[part], sems.at[4 + part]
            )
        )
    for copy in copies:
        copy.start()
    for copy in copies:
        copy.wait()


def stage(place, tokens, cot, gain, w_qkv, w_out):
    return pl.pallas_call(
        stage_kernel,
        in_specs=[SM] + [ANY] * 5,
        out_specs=[VM] * 7,
        out_shape=[
            jax.ShapeDtypeStruct((HW, D), BF16),
            jax.ShapeDtypeStruct((HW, D), BF16),
            jax.ShapeDtypeStruct((1, D), F32),
        ]
        + [jax.ShapeDtypeStruct((D, HALF * DH), BF16)] * 3
        + [jax.ShapeDtypeStruct((HALF * DH, D), BF16)],
        scratch_shapes=[pltpu.SemaphoreType.DMA((7,))],
        compiler_params=pltpu.CompilerParams(vmem_limit_bytes=STAGE_LIMIT),
        cost_estimate=cost(0, 9_000_000),
        name="stage",
    )(place, tokens, cot, gain, w_qkv, w_out)


def project_kernel(
    place, valid, own, other, cot_own, cot_other, gain, wq, wk, wv, wo, packed, near0, near1, near2, near3
):
    x = jnp.concatenate([own[...], other[...]], axis=0).astype(F32)
    rinv = lax.rsqrt(jnp.mean(x * x, axis=-1, keepdims=True) + EPS)
    normed = (x * rinv * gain[...]).astype(BF16)
    cot = jnp.concatenate([cot_own[...], cot_other[...]], axis=0)
    flags = jnp.full((ROWS - OK0, DH), valid[0], jnp.int32).astype(F32).astype(BF16)
    for row in (Q0, K0, V0, G0):
        if row == G0:
            got = mm_nt(cot, wo[...]).astype(BF16)
        else:
            got = mm(normed, {Q0: wq, K0: wk, V0: wv}[row][...]).astype(BF16)
        for h in range(HALF):
            for s in range(2):
                packed[h, s, row : row + HW, :] = got[s * HW : (s + 1) * HW, h * DH : (h + 1) * DH]
    for h in range(HALF):
        for s in range(2):
            packed[h, s, OK0:ROWS, :] = flags
    for step, near in enumerate((near0, near1, near2, near3)):
        h = lax.rem(place[2] + step, HALF)
        for s in range(2):
            near[s] = packed[h, s, :OK0, :]


def project(place, valid, own, other, cot_own, cot_other, gain, weights):
    return pl.pallas_call(
        project_kernel,
        in_specs=[SM, SM] + [VM] * 9,
        out_specs=[VM] * 5,
        out_shape=[jax.ShapeDtypeStruct((HALF, 2, ROWS, DH), BF16)]
        + [jax.ShapeDtypeStruct((2, OK0, DH), BF16)] * 4,
        compiler_params=params(),
        cost_estimate=cost(2 * PAIR * D * 4 * HALF * DH, 7_000_000),
        name="project",
    )(place, valid, own, other, cot_own, cot_other, gain, *weights)


def both(block, row):
    return jnp.concatenate([block[0, row : row + HW, :], block[1, row : row + HW, :]], axis=0)


def near_forward_kernel(near0, near1, near2, near3, kept, result, stats, scores):
    blocks = (near0, near1, near2, near3)
    turned = [turn(both(block, V0)).astype(BF16) for block in blocks]
    for g in range(4):
        cols = slice(g * PAIR, (g + 1) * PAIR)
        query = both(blocks[g], Q0)
        grad_t = turn(both(blocks[g], G0))
        peak = jnp.full((1, PAIR), -jnp.inf, F32)
        for z in range(4):
            block = mm_nt(both(blocks[z], K0), query)
            scores[z * PAIR : (z + 1) * PAIR, :] = block
            peak = jnp.maximum(peak, jnp.max(block, axis=0, keepdims=True))
        peak = peak * SCALE2
        total = jnp.zeros((1, PAIR), F32)
        for b in range(8):
            rows = slice(b * HW, (b + 1) * HW)
            block = jnp.exp2(scores[rows, :] * SCALE2 - peak)
            total = total + jnp.sum(block, axis=0, keepdims=True)
            kept[rows, cols] = block.astype(BF16)
        got = jnp.zeros((DH, PAIR), F32)
        for z in range(4):
            got = got + mm(turned[z], kept[z * PAIR : (z + 1) * PAIR, cols])
        result[:, cols] = got
        delta = jnp.sum(got * grad_t, axis=0, keepdims=True)
        told = jnp.concatenate([peak, total, delta, jnp.zeros((1, PAIR), F32)], axis=0)
        stats[2 * g] = told[:, :HW]
        stats[2 * g + 1] = told[:, HW:]


def near_forward(*blocks):
    return pl.pallas_call(
        near_forward_kernel,
        in_specs=[VM] * 4,
        out_specs=[VM] * 3,
        out_shape=[
            jax.ShapeDtypeStruct((TOKENS, TOKENS), BF16),
            jax.ShapeDtypeStruct((DH, TOKENS), F32),
            jax.ShapeDtypeStruct((8, 4, HW), F32),
        ],
        scratch_shapes=[pltpu.VMEM((TOKENS, PAIR), F32)],
        compiler_params=params(),
        cost_estimate=cost(80 * TOKENS * TOKENS * DH, 4_000_000, TOKENS * TOKENS),
        name="near_forward",
    )(*blocks)


def slot_of_near(place, step, s):
    zh = place[2]
    cam = lax.rem(zh + 4 - step, 4)
    return (zh * 2 + s) * 4 + cam


def far_forward_kernel(place, win, mine, past, close, told, kept, result, keys, values_t, scores):
    width = win[place[0] * HALF + place[1]]
    told[...] = jnp.zeros_like(told)
    for step in range(4):
        for s in range(2):
            told[slot_of_near(place, step, s), 0:4, :] = close[2 * step + s]
    for j in range(GROUP):
        keys[j * HW : (j + 1) * HW, :] = past[j, :HW, :]
        keys[(GROUP + j) * HW : (GROUP + j + 1) * HW, :] = mine[j, K0 : K0 + HW, :]
        values_t[:, j * HW : (j + 1) * HW] = turn(past[j, HW : 2 * HW, :]).astype(BF16)
        values_t[:, (GROUP + j) * HW : (GROUP + j + 1) * HW] = turn(
            mine[j, V0 : V0 + HW, :]
        ).astype(BF16)
    for p in range(GROUP // 2):
        query = jnp.concatenate([mine[2 * p, :HW, :], mine[2 * p + 1, :HW, :]], axis=0)
        grad_t = jnp.concatenate(
            [turn(mine[2 * p, G0 : G0 + HW, :]), turn(mine[2 * p + 1, G0 : G0 + HW, :])], axis=1
        )
        peak = jnp.full((1, PAIR), -jnp.inf, F32)
        for b in range(WIN + 1):
            j = 2 * p + b
            if j < GROUP:
                flag = past[j, 2 * HW : 2 * HW + 1, :].astype(F32)
            else:
                flag = mine[j - GROUP, OK0 : OK0 + 1, :].astype(F32)
            lower = jnp.where((flag > 0.5) & (b >= WIN - width) & (b < WIN), 0.0, -jnp.inf)
            upper = jnp.where((flag > 0.5) & (b >= WIN + 1 - width), 0.0, -jnp.inf)
            bias = jnp.concatenate([lower, upper], axis=1)
            block = mm_nt(keys[j * HW : (j + 1) * HW, :], query) + bias
            scores[b * HW : (b + 1) * HW, :] = block
            peak = jnp.maximum(peak, jnp.max(block, axis=0, keepdims=True))
        peak = jnp.maximum(peak * SCALE2, FLOOR)
        total = jnp.zeros((1, PAIR), F32)
        for b in range(WIN + 1):
            block = jnp.exp2(scores[b * HW : (b + 1) * HW, :] * SCALE2 - peak)
            total = total + jnp.sum(block, axis=0, keepdims=True)
            kept[p, b * HW : (b + 1) * HW, :] = block.astype(BF16)
        got = mm(values_t[:, p * PAIR : p * PAIR + KEYS], kept[p])
        result[:, p * PAIR : (p + 1) * PAIR] = got
        delta = jnp.sum(got * grad_t, axis=0, keepdims=True)
        stats = jnp.concatenate([peak, total, delta, jnp.zeros((1, PAIR), F32)], axis=0)
        told[2 * p * 4 + place[1], 4:8, :] = stats[:, :HW]
        told[(2 * p + 1) * 4 + place[1], 4:8, :] = stats[:, HW:]


def far_forward(place, window, mine, past, close):
    return pl.pallas_call(
        far_forward_kernel,
        in_specs=[SM, SM, VM, VM, VM],
        out_specs=[VM] * 3,
        out_shape=[
            jax.ShapeDtypeStruct((32, 8, HW), F32),
            jax.ShapeDtypeStruct((GROUP // 2, KEYS, PAIR), BF16),
            jax.ShapeDtypeStruct((DH, GROUP * HW), F32),
        ],
        scratch_shapes=[
            pltpu.VMEM((2 * GROUP * HW, DH), BF16),
            pltpu.VMEM((DH, 2 * GROUP * HW), BF16),
            pltpu.VMEM((KEYS, PAIR), F32),
        ],
        compiler_params=params(),
        cost_estimate=cost(16 * KEYS * PAIR * DH, 5_000_000, 4 * KEYS * PAIR),
        name="far_forward",
    )(place, window, mine, past, close)


def merge(this, other):
    top = jnp.maximum(this[0:1], other[0:1])
    here = jnp.exp2(this[0:1] - top)
    there = jnp.exp2(other[0:1] - top)
    inverse = 1.0 / (here * this[1:2] + there * other[1:2])
    here = here * inverse
    delta = here * this[2:3] + there * inverse * other[2:3]
    return here, here * delta


def near_backward_kernel(
    place, near0, near1, near2, near3, kept, result, stats, told,
    back0, back1, back2, back3, grads, grad_all, query_all,
):
    blocks = (near0, near1, near2, near3)
    outs = (back0, back1, back2, back3)
    for g in range(4):
        cols = slice(g * PAIR, (g + 1) * PAIR)
        this = jnp.concatenate([stats[2 * g], stats[2 * g + 1]], axis=1)
        other = jnp.concatenate(
            [told[slot_of_near(place, g, s), 4:8, :] for s in range(2)], axis=1
        )
        weight, delta = merge(this, other)
        grad_t = (turn(both(blocks[g], G0)) * weight).astype(BF16)
        grad_all[:, cols] = grad_t
        query_all[cols, :] = both(blocks[g], Q0)
        attended = (result[:, cols] * weight).T.astype(BF16)
        for s in range(2):
            outs[g][s, :HW, :] = attended[s * HW : (s + 1) * HW]
        for z in range(4):
            rows = slice(z * PAIR, (z + 1) * PAIR)
            d_probs = mm(both(blocks[z], V0), grad_t)
            grads[rows, cols] = (kept[rows, cols].astype(F32) * (d_probs - delta)).astype(BF16)
    for z in range(4):
        rows = slice(z * PAIR, (z + 1) * PAIR)
        d_values = mm_nt(kept[rows, :], grad_all[...]).astype(BF16)
        d_keys = (mm(grads[rows, :], query_all[...]) * SCALE).astype(BF16)
        for s in range(2):
            outs[z][s, 2 * HW : 3 * HW, :] = d_keys[s * HW : (s + 1) * HW]
            outs[z][s, 3 * HW :, :] = d_values[s * HW : (s + 1) * HW]
    keys_t = jnp.concatenate([turn(both(block, K0)).astype(BF16) for block in blocks], axis=1)
    for g in range(4):
        cols = slice(g * PAIR, (g + 1) * PAIR)
        d_query = (mm(keys_t, grads[:, cols]) * SCALE).T.astype(BF16)
        for s in range(2):
            outs[g][s, HW : 2 * HW, :] = d_query[s * HW : (s + 1) * HW]


def near_backward(place, blocks, kept, result, stats, told):
    return pl.pallas_call(
        near_backward_kernel,
        in_specs=[SM] + [VM] * 8,
        out_specs=[VM] * 4,
        out_shape=[jax.ShapeDtypeStruct((2, 4 * HW, DH), BF16)] * 4,
        scratch_shapes=[
            pltpu.VMEM((TOKENS, TOKENS), BF16),
            pltpu.VMEM((DH, TOKENS), BF16),
            pltpu.VMEM((TOKENS, DH), BF16),
        ],
        compiler_params=params(),
        cost_estimate=cost(8 * TOKENS * TOKENS * DH, 5_000_000),
        name="near_backward",
    )(place, *blocks, kept, result, stats, told)


def far_backward_kernel(
    place, mine, past, kept, result, sent, told, own, back, keys_t, values, dk, dv, grads
):
    for j in range(GROUP):
        keys_t[:, j * HW : (j + 1) * HW] = turn(past[j, :HW, :]).astype(BF16)
        keys_t[:, (GROUP + j) * HW : (GROUP + j + 1) * HW] = turn(
            mine[j, K0 : K0 + HW, :]
        ).astype(BF16)
        values[j * HW : (j + 1) * HW, :] = past[j, HW : 2 * HW, :]
        values[(GROUP + j) * HW : (GROUP + j + 1) * HW, :] = mine[j, V0 : V0 + HW, :]
    dk[...] = jnp.zeros_like(dk)
    dv[...] = jnp.zeros_like(dv)
    for p in range(GROUP // 2):
        query = jnp.concatenate([mine[2 * p, :HW, :], mine[2 * p + 1, :HW, :]], axis=0)
        grad_t = jnp.concatenate(
            [turn(mine[2 * p, G0 : G0 + HW, :]), turn(mine[2 * p + 1, G0 : G0 + HW, :])], axis=1
        )
        slots = [(2 * p + i) * 4 + place[1] for i in range(2)]
        this = jnp.concatenate([sent[slot, 4:8, :] for slot in slots], axis=1)
        other = jnp.concatenate([told[slot, 0:4, :] for slot in slots], axis=1)
        weight, delta = merge(this, other)
        grad_t = (grad_t * weight).astype(BF16)
        at = p * PAIR
        attended = (result[:, at : at + PAIR] * weight).T.astype(BF16)
        for lo, size in ((0, 384), (384, 384), (768, 384)):
            rows = slice(lo, lo + size)
            spot = slice(at + lo, at + lo + size)
            d_probs = mm(values[spot, :], grad_t)
            block = kept[p, rows, :]
            d_scores = (block.astype(F32) * (d_probs - delta)).astype(BF16)
            grads[rows, :] = d_scores
            dv[spot, :] += mm_nt(block, grad_t)
            dk[spot, :] += mm(d_scores, query)
        d_query = (mm(keys_t[:, at : at + KEYS], grads[...]) * SCALE).T.astype(BF16)
        for i in range(2):
            own[2 * p + i, :HW, :] = attended[i * HW : (i + 1) * HW]
            own[2 * p + i, HW : 2 * HW, :] = d_query[i * HW : (i + 1) * HW]
    for j in range(GROUP):
        early = slice(j * HW, (j + 1) * HW)
        late = slice((GROUP + j) * HW, (GROUP + j + 1) * HW)
        back[j, :HW, :] = (dk[early, :] * SCALE).astype(BF16)
        back[j, HW:, :] = dv[early, :].astype(BF16)
        own[j, 2 * HW : 3 * HW, :] = (dk[late, :] * SCALE).astype(BF16)
        own[j, 3 * HW :, :] = dv[late, :].astype(BF16)


def far_backward(place, mine, past, kept, result, sent, told):
    return pl.pallas_call(
        far_backward_kernel,
        in_specs=[SM] + [VM] * 6,
        out_specs=[VM, VM],
        out_shape=[
            jax.ShapeDtypeStruct((GROUP, 4 * HW, DH), BF16),
            jax.ShapeDtypeStruct((GROUP, 2 * HW, DH), BF16),
        ],
        scratch_shapes=[
            pltpu.VMEM((DH, 2 * GROUP * HW), BF16),
            pltpu.VMEM((2 * GROUP * HW, DH), BF16),
            pltpu.VMEM((2 * GROUP * HW, DH), F32),
            pltpu.VMEM((2 * GROUP * HW, DH), F32),
            pltpu.VMEM((KEYS, PAIR), BF16),
        ],
        compiler_params=params(),
        cost_estimate=cost(32 * KEYS * PAIR * DH, 6_000_000),
        name="far_backward",
    )(place, mine, past, kept, result, sent, told)


def add_back_kernel(own, back, out):
    out[:, : 2 * HW, :] = own[:, : 2 * HW, :]
    for j in range(GROUP):
        out[j, 2 * HW : 4 * HW, :] = (
            own[j, 2 * HW :, :].astype(F32) + back[j].astype(F32)
        ).astype(BF16)
        out[j, 4 * HW :, :] = jnp.zeros((ROWS - 4 * HW, DH), BF16)


def add_back(own, back):
    return pl.pallas_call(
        add_back_kernel,
        in_specs=[VM] * 2,
        out_specs=VM,
        out_shape=jax.ShapeDtypeStruct((GROUP, ROWS, DH), BF16),
        compiler_params=params(),
        cost_estimate=cost(GROUP * 2 * HW * DH, 2_500_000),
        name="add_back",
    )(own, back)


def unproject_kernel(place, near0, near1, near2, near3, far, wq, wk, wv, wo, own, other, close):
    for step, near in enumerate((near0, near1, near2, near3)):
        close[lax.rem(place[2] + step, HALF)] = near[...]
    parts = []
    for part in range(4):
        rows = slice(part * HW, (part + 1) * HW)
        pieces = []
        for h in range(HALF):
            away = jnp.concatenate([far[h, 0, rows, :], far[h, 1, rows, :]], axis=0)
            here = jnp.concatenate([close[h, 0, rows, :], close[h, 1, rows, :]], axis=0)
            pieces.append((away.astype(F32) + here.astype(F32)).astype(BF16))
        parts.append(jnp.concatenate(pieces, axis=1))
    mixed = mm(parts[0], wo[...])
    total = mm_nt(parts[1], wq[...]) + mm_nt(parts[2], wk[...]) + mm_nt(parts[3], wv[...])
    own[0] = mixed[:HW]
    own[1] = total[:HW]
    other[0] = mixed[HW:].astype(BF16)
    other[1] = total[HW:].astype(BF16)


def unproject(place, blocks, far, weights):
    return pl.pallas_call(
        unproject_kernel,
        in_specs=[SM] + [VM] * 9,
        out_specs=[VM, VM],
        out_shape=[jax.ShapeDtypeStruct((2, HW, D), F32), jax.ShapeDtypeStruct((2, HW, D), BF16)],
        scratch_shapes=[pltpu.VMEM((HALF, 2, 4 * HW, DH), BF16)],
        compiler_params=params(),
        cost_estimate=cost(2 * PAIR * D * 4 * HALF * DH, 8_000_000),
        name="unproject",
    )(place, *blocks, far, *weights)


def finish_kernel(tokens, cot, gain, own, other, mixed, out):
    x = tokens[...].astype(F32)
    mixed[...] = (x + (own[0] + other[0].astype(F32))).astype(BF16)
    rinv = lax.rsqrt(jnp.mean(x * x, axis=-1, keepdims=True) + EPS)
    scaled = (own[1] + other[1].astype(F32)) * gain[...]
    mean = jnp.mean(scaled * x, axis=-1, keepdims=True)
    grad = rinv * scaled - x * (rinv * rinv * rinv * mean)
    out[...] = (cot[...].astype(F32) + grad).astype(BF16)


def finish(tokens, cot, gain, own, other):
    return pl.pallas_call(
        finish_kernel,
        in_specs=[VM] * 5,
        out_specs=[VM] * 2,
        out_shape=[jax.ShapeDtypeStruct((HW, D), BF16)] * 2,
        compiler_params=params(),
        cost_estimate=cost(HW * D * 10, 3_000_000),
        name="finish",
    )(tokens, cot, gain, own, other)


LANE = ("x", "zl")


def swap(value):
    return lax.ppermute(value, "core", [(0, 1), (1, 0)])


def turn_ring(value, steps):
    return lax.ppermute(value, "zh", [(i, (i + steps) % 4) for i in range(4)])


def exchange(value, axes):
    return lax.all_to_all(value, axes, 0, 0, tiled=True)


def per_device(tokens, gain, w_qkv, w_out, window, valid, cotangent):
    rows = lax.axis_size("y")
    place = jnp.stack(
        [lax.axis_index(axis) for axis in ("core", "x", "zh")]
    ).astype(jnp.int32)
    tokens = tokens.reshape(HW, D)
    cot = cotangent.reshape(HW, D)
    other_tokens = swap(tokens)
    other_cot = swap(cot)
    tokens, cot, gain, *weights = stage(place, tokens, cot, gain.reshape(1, D), w_qkv, w_out)
    packed, *blocks = project(
        place, valid, tokens, other_tokens, cot, other_cot, gain, weights
    )
    blocks = [blocks[0]] + [turn_ring(blocks[step], step) for step in (1, 2, 3)]
    mine = exchange(packed.reshape(2 * HALF, ROWS, DH), LANE)
    past = lax.ppermute(mine[:, K0:, :], "y", [(i, i + 1) for i in range(rows - 1)])
    near_kept, near_result, close = near_forward(*blocks)
    sent, far_kept, far_result = far_forward(place, window, mine, past, close)
    told = exchange(sent, ("x", "zl", "zh"))
    own, back = far_backward(place, mine, past, far_kept, far_result, sent, told)
    back = lax.ppermute(back, "y", [(i + 1, i) for i in range(rows - 1)])
    returned = near_backward(place, blocks, near_kept, near_result, close, told)
    own, returned = lax.optimization_barrier((own, returned))
    returned = [returned[0]] + [turn_ring(returned[step], -step) for step in (1, 2, 3)]
    own = add_back(own, back)
    far = exchange(own, LANE).reshape(HALF, 2, ROWS, DH)
    out_own, out_other = unproject(place, returned, far, weights)
    mixed, d_tokens = finish(tokens, cot, gain, out_own, swap(out_other))
    return mixed.reshape(1, 1, HW, D), d_tokens.reshape(1, 1, HW, D)


def solution(mesh):
    grid = Mesh(mesh.devices.reshape(4, 4, 2, 4, 2), ("y", "x", "zl", "zh", "core"))
    frames, cams = ("y", "x", "zl"), ("zh", "core")
    split = P(frames, cams, None, None)
    return jax.shard_map(
        per_device,
        mesh=grid,
        in_specs=(split, P(), P(), P(), P(), P(frames), split),
        out_specs=(split, split),
        check_vma=False,
    )
```

```python
import math

import jax
import jax.numpy as jnp
from jax import lax
from jax.experimental import pallas as pl
from jax.experimental.pallas import tpu as pltpu
from jax.sharding import Mesh
from jax.sharding import PartitionSpec as P

D = 1024
H = 8
DH = 128
HW = 128
WIN = 8
EPS = 1e-05

HALF = H // 2
PAIR = 2 * HW
GROUP = 8
SCALE = DH ** (-0.5)
SCALE2 = SCALE * math.log2(math.e)
FLOOR = -3.0e38
F32 = jnp.float32
BF16 = jnp.bfloat16
NT = (((1,), (1,)), ((), ()))
VMEM_LIMIT = 20 * 1024 * 1024
STAGE_LIMIT = 48 * 1024 * 1024

Q0, G0, K0, V0, OK0, ROWS = 0, 128, 256, 384, 512, 528
TOKENS = 8 * HW
KEYS = (WIN + 1) * HW


def params(**kw):
    return pltpu.CompilerParams(vmem_limit_bytes=VMEM_LIMIT, **kw)


def mm(a, b):
    return jnp.dot(a, b, preferred_element_type=F32)


def mm_nt(a, b):
    return lax.dot_general(a, b, NT, preferred_element_type=F32)


def turn(a):
    return a.astype(F32).T


VM = pl.BlockSpec(memory_space=pltpu.VMEM)
SM = pl.BlockSpec(memory_space=pltpu.SMEM)
ANY = pl.BlockSpec(memory_space=pltpu.HBM)


def cost(flops, size, exps=0):
    return pl.CostEstimate(flops=flops, bytes_accessed=size, transcendentals=exps)


def stage_kernel(place, tokens, cot, gain, w_qkv, w_out, own, own_cot, own_gain, wq, wk, wv, out, sems):
    core = place[0]
    copies = [
        pltpu.make_async_copy(tokens, own, sems.at[0]),
        pltpu.make_async_copy(cot, own_cot, sems.at[1]),
        pltpu.make_async_copy(gain, own_gain, sems.at[2]),
        pltpu.make_async_copy(
            w_out.at[pl.ds(pl.multiple_of(core * HALF * DH, HALF * DH), HALF * DH), :],
            out,
            sems.at[3],
        ),
    ]
    for part in range(3):
        start = pl.multiple_of(part * D + core * HALF * DH, HALF * DH)
        copies.append(
            pltpu.make_async_copy(
                w_qkv.at[:, pl.ds(start, HALF * DH)], (wq, wk, wv)[part], sems.at[4 + part]
            )
        )
    for copy in copies:
        copy.start()
    for copy in copies:
        copy.wait()


def stage(place, tokens, cot, gain, w_qkv, w_out):
    return pl.pallas_call(
        stage_kernel,
        in_specs=[SM] + [ANY] * 5,
        out_specs=[VM] * 7,
        out_shape=[
            jax.ShapeDtypeStruct((HW, D), BF16),
            jax.ShapeDtypeStruct((HW, D), BF16),
            jax.ShapeDtypeStruct((1, D), F32),
        ]
        + [jax.ShapeDtypeStruct((D, HALF * DH), BF16)] * 3
        + [jax.ShapeDtypeStruct((HALF * DH, D), BF16)],
        scratch_shapes=[pltpu.SemaphoreType.DMA((7,))],
        compiler_params=pltpu.CompilerParams(vmem_limit_bytes=STAGE_LIMIT),
        cost_estimate=cost(0, 9_000_000),
        name="stage",
    )(place, tokens, cot, gain, w_qkv, w_out)


def project_kernel(
    place, valid, own, other, cot_own, cot_other, gain, wq, wk, wv, wo, packed, near0, near1, near2, near3
):
    x = jnp.concatenate([own[...], other[...]], axis=0).astype(F32)
    rinv = lax.rsqrt(jnp.mean(x * x, axis=-1, keepdims=True) + EPS)
    normed = (x * rinv * gain[...]).astype(BF16)
    cot = jnp.concatenate([cot_own[...], cot_other[...]], axis=0)
    flags = jnp.full((ROWS - OK0, DH), valid[0], jnp.int32).astype(F32).astype(BF16)
    for row in (Q0, K0, V0, G0):
        if row == G0:
            got = mm_nt(cot, wo[...]).astype(BF16)
        else:
            got = mm(normed, {Q0: wq, K0: wk, V0: wv}[row][...]).astype(BF16)
        for h in range(HALF):
            for s in range(2):
                packed[h, s, row : row + HW, :] = got[s * HW : (s + 1) * HW, h * DH : (h + 1) * DH]
    for h in range(HALF):
        for s in range(2):
            packed[h, s, OK0:ROWS, :] = flags
    for step, near in enumerate((near0, near1, near2, near3)):
        h = lax.rem(place[2] + step, HALF)
        for s in range(2):
            near[s] = packed[h, s, :OK0, :]


def project(place, valid, own, other, cot_own, cot_other, gain, weights):
    return pl.pallas_call(
        project_kernel,
        in_specs=[SM, SM] + [VM] * 9,
        out_specs=[VM] * 5,
        out_shape=[jax.ShapeDtypeStruct((HALF, 2, ROWS, DH), BF16)]
        + [jax.ShapeDtypeStruct((2, OK0, DH), BF16)] * 4,
        compiler_params=params(),
        cost_estimate=cost(2 * PAIR * D * 4 * HALF * DH, 7_000_000),
        name="project",
    )(place, valid, own, other, cot_own, cot_other, gain, *weights)


def both(block, row):
    return jnp.concatenate([block[0, row : row + HW, :], block[1, row : row + HW, :]], axis=0)


def near_forward_kernel(near0, near1, near2, near3, kept, result, stats, scores):
    blocks = (near0, near1, near2, near3)
    turned = [turn(both(block, V0)).astype(BF16) for block in blocks]
    for g in range(4):
        cols = slice(g * PAIR, (g + 1) * PAIR)
        query = both(blocks[g], Q0)
        grad_t = turn(both(blocks[g], G0))
        peak = jnp.full((1, PAIR), -jnp.inf, F32)
        for z in range(4):
            block = mm_nt(both(blocks[z], K0), query)
            scores[z * PAIR : (z + 1) * PAIR, :] = block
            peak = jnp.maximum(peak, jnp.max(block, axis=0, keepdims=True))
        peak = peak * SCALE2
        total = jnp.zeros((1, PAIR), F32)
        for b in range(8):
            rows = slice(b * HW, (b + 1) * HW)
            block = jnp.exp2(scores[rows, :] * SCALE2 - peak)
            total = total + jnp.sum(block, axis=0, keepdims=True)
            kept[rows, cols] = block.astype(BF16)
        got = jnp.zeros((DH, PAIR), F32)
        for z in range(4):
            got = got + mm(turned[z], kept[z * PAIR : (z + 1) * PAIR, cols])
        result[:, cols] = got
        delta = jnp.sum(got * grad_t, axis=0, keepdims=True)
        told = jnp.concatenate([peak, total, delta, jnp.zeros((1, PAIR), F32)], axis=0)
        stats[2 * g] = told[:, :HW]
        stats[2 * g + 1] = told[:, HW:]


def near_forward(*blocks):
    return pl.pallas_call(
        near_forward_kernel,
        in_specs=[VM] * 4,
        out_specs=[VM] * 3,
        out_shape=[
            jax.ShapeDtypeStruct((TOKENS, TOKENS), BF16),
            jax.ShapeDtypeStruct((DH, TOKENS), F32),
            jax.ShapeDtypeStruct((8, 4, HW), F32),
        ],
        scratch_shapes=[pltpu.VMEM((TOKENS, PAIR), F32)],
        compiler_params=params(),
        cost_estimate=cost(80 * TOKENS * TOKENS * DH, 4_000_000, TOKENS * TOKENS),
        name="near_forward",
    )(*blocks)


def slot_of_near(place, step, s):
    zh = place[2]
    cam = lax.rem(zh + 4 - step, 4)
    return (zh * 2 + s) * 4 + cam


def far_forward_kernel(place, win, mine, past, close, told, kept, result, keys, values_t, scores):
    width = win[place[0] * HALF + place[1]]
    told[...] = jnp.zeros_like(told)
    for step in range(4):
        for s in range(2):
            told[slot_of_near(place, step, s), 0:4, :] = close[2 * step + s]
    for j in range(GROUP):
        keys[j * HW : (j + 1) * HW, :] = past[j, :HW, :]
        keys[(GROUP + j) * HW : (GROUP + j + 1) * HW, :] = mine[j, K0 : K0 + HW, :]
        values_t[:, j * HW : (j + 1) * HW] = turn(past[j, HW : 2 * HW, :]).astype(BF16)
        values_t[:, (GROUP + j) * HW : (GROUP + j + 1) * HW] = turn(
            mine[j, V0 : V0 + HW, :]
        ).astype(BF16)
    for p in range(GROUP // 2):
        query = jnp.concatenate([mine[2 * p, :HW, :], mine[2 * p + 1, :HW, :]], axis=0)
        grad_t = jnp.concatenate(
            [turn(mine[2 * p, G0 : G0 + HW, :]), turn(mine[2 * p + 1, G0 : G0 + HW, :])], axis=1
        )
        peak = jnp.full((1, PAIR), -jnp.inf, F32)
        for b in range(WIN + 1):
            j = 2 * p + b
            if j < GROUP:
                flag = past[j, 2 * HW : 2 * HW + 1, :].astype(F32)
            else:
                flag = mine[j - GROUP, OK0 : OK0 + 1, :].astype(F32)
            lower = jnp.where((flag > 0.5) & (b >= WIN - width) & (b < WIN), 0.0, -jnp.inf)
            upper = jnp.where((flag > 0.5) & (b >= WIN + 1 - width), 0.0, -jnp.inf)
            bias = jnp.concatenate([lower, upper], axis=1)
            block = mm_nt(keys[j * HW : (j + 1) * HW, :], query) + bias
            scores[b * HW : (b + 1) * HW, :] = block
            peak = jnp.maximum(peak, jnp.max(block, axis=0, keepdims=True))
        peak = jnp.maximum(peak * SCALE2, FLOOR)
        total = jnp.zeros((1, PAIR), F32)
        for b in range(WIN + 1):
            block = jnp.exp2(scores[b * HW : (b + 1) * HW, :] * SCALE2 - peak)
            total = total + jnp.sum(block, axis=0, keepdims=True)
            kept[p, b * HW : (b + 1) * HW, :] = block.astype(BF16)
        got = mm(values_t[:, p * PAIR : p * PAIR + KEYS], kept[p])
        result[:, p * PAIR : (p + 1) * PAIR] = got
        delta = jnp.sum(got * grad_t, axis=0, keepdims=True)
        stats = jnp.concatenate([peak, total, delta, jnp.zeros((1, PAIR), F32)], axis=0)
        told[2 * p * 4 + place[1], 4:8, :] = stats[:, :HW]
        told[(2 * p + 1) * 4 + place[1], 4:8, :] = stats[:, HW:]


def far_forward(place, window, mine, past, close):
    return pl.pallas_call(
        far_forward_kernel,
        in_specs=[SM, SM, VM, VM, VM],
        out_specs=[VM] * 3,
        out_shape=[
            jax.ShapeDtypeStruct((32, 8, HW), F32),
            jax.ShapeDtypeStruct((GROUP // 2, KEYS, PAIR), BF16),
            jax.ShapeDtypeStruct((DH, GROUP * HW), F32),
        ],
        scratch_shapes=[
            pltpu.VMEM((2 * GROUP * HW, DH), BF16),
            pltpu.VMEM((DH, 2 * GROUP * HW), BF16),
            pltpu.VMEM((KEYS, PAIR), F32),
        ],
        compiler_params=params(),
        cost_estimate=cost(16 * KEYS * PAIR * DH, 5_000_000, 4 * KEYS * PAIR),
        name="far_forward",
    )(place, window, mine, past, close)


def merge(this, other):
    top = jnp.maximum(this[0:1], other[0:1])
    here = jnp.exp2(this[0:1] - top)
    there = jnp.exp2(other[0:1] - top)
    inverse = 1.0 / (here * this[1:2] + there * other[1:2])
    here = here * inverse
    delta = here * this[2:3] + there * inverse * other[2:3]
    return here, here * delta


def near_backward_kernel(
    place, near0, near1, near2, near3, kept, result, stats, told,
    back0, back1, back2, back3, grads, grad_all, query_all,
):
    blocks = (near0, near1, near2, near3)
    outs = (back0, back1, back2, back3)
    for g in range(4):
        cols = slice(g * PAIR, (g + 1) * PAIR)
        this = jnp.concatenate([stats[2 * g], stats[2 * g + 1]], axis=1)
        other = jnp.concatenate(
            [told[slot_of_near(place, g, s), 4:8, :] for s in range(2)], axis=1
        )
        weight, delta = merge(this, other)
        grad_t = (turn(both(blocks[g], G0)) * weight).astype(BF16)
        grad_all[:, cols] = grad_t
        query_all[cols, :] = both(blocks[g], Q0)
        attended = (result[:, cols] * weight).T.astype(BF16)
        for s in range(2):
            outs[g][s, :HW, :] = attended[s * HW : (s + 1) * HW]
        for z in range(4):
            rows = slice(z * PAIR, (z + 1) * PAIR)
            d_probs = mm(both(blocks[z], V0), grad_t)
            grads[rows, cols] = (kept[rows, cols].astype(F32) * (d_probs - delta)).astype(BF16)
    for z in range(4):
        rows = slice(z * PAIR, (z + 1) * PAIR)
        d_values = mm_nt(kept[rows, :], grad_all[...]).astype(BF16)
        d_keys = (mm(grads[rows, :], query_all[...]) * SCALE).astype(BF16)
        for s in range(2):
            outs[z][s, 2 * HW : 3 * HW, :] = d_keys[s * HW : (s + 1) * HW]
            outs[z][s, 3 * HW :, :] = d_values[s * HW : (s + 1) * HW]
    keys_t = jnp.concatenate([turn(both(block, K0)).astype(BF16) for block in blocks], axis=1)
    for g in range(4):
        cols = slice(g * PAIR, (g + 1) * PAIR)
        d_query = (mm(keys_t, grads[:, cols]) * SCALE).T.astype(BF16)
        for s in range(2):
            outs[g][s, HW : 2 * HW, :] = d_query[s * HW : (s + 1) * HW]


def near_backward(place, blocks, kept, result, stats, told):
    return pl.pallas_call(
        near_backward_kernel,
        in_specs=[SM] + [VM] * 8,
        out_specs=[VM] * 4,
        out_shape=[jax.ShapeDtypeStruct((2, 4 * HW, DH), BF16)] * 4,
        scratch_shapes=[
            pltpu.VMEM((TOKENS, TOKENS), BF16),
            pltpu.VMEM((DH, TOKENS), BF16),
            pltpu.VMEM((TOKENS, DH), BF16),
        ],
        compiler_params=params(),
        cost_estimate=cost(8 * TOKENS * TOKENS * DH, 5_000_000),
        name="near_backward",
    )(place, *blocks, kept, result, stats, told)


def far_backward_kernel(
    place, mine, past, kept, result, sent, told, own, back, keys_t, values, dk, dv, grads
):
    for j in range(GROUP):
        keys_t[:, j * HW : (j + 1) * HW] = turn(past[j, :HW, :]).astype(BF16)
        keys_t[:, (GROUP + j) * HW : (GROUP + j + 1) * HW] = turn(
            mine[j, K0 : K0 + HW, :]
        ).astype(BF16)
        values[j * HW : (j + 1) * HW, :] = past[j, HW : 2 * HW, :]
        values[(GROUP + j) * HW : (GROUP + j + 1) * HW, :] = mine[j, V0 : V0 + HW, :]
    dk[...] = jnp.zeros_like(dk)
    dv[...] = jnp.zeros_like(dv)
    for p in range(GROUP // 2):
        query = jnp.concatenate([mine[2 * p, :HW, :], mine[2 * p + 1, :HW, :]], axis=0)
        grad_t = jnp.concatenate(
            [turn(mine[2 * p, G0 : G0 + HW, :]), turn(mine[2 * p + 1, G0 : G0 + HW, :])], axis=1
        )
        slots = [(2 * p + i) * 4 + place[1] for i in range(2)]
        this = jnp.concatenate([sent[slot, 4:8, :] for slot in slots], axis=1)
        other = jnp.concatenate([told[slot, 0:4, :] for slot in slots], axis=1)
        weight, delta = merge(this, other)
        grad_t = (grad_t * weight).astype(BF16)
        at = p * PAIR
        attended = (result[:, at : at + PAIR] * weight).T.astype(BF16)
        for lo, size in ((0, 384), (384, 384), (768, 384)):
            rows = slice(lo, lo + size)
            spot = slice(at + lo, at + lo + size)
            d_probs = mm(values[spot, :], grad_t)
            block = kept[p, rows, :]
            d_scores = (block.astype(F32) * (d_probs - delta)).astype(BF16)
            grads[rows, :] = d_scores
            dv[spot, :] += mm_nt(block, grad_t)
            dk[spot, :] += mm(d_scores, query)
        d_query = (mm(keys_t[:, at : at + KEYS], grads[...]) * SCALE).T.astype(BF16)
        for i in range(2):
            own[2 * p + i, :HW, :] = attended[i * HW : (i + 1) * HW]
            own[2 * p + i, HW : 2 * HW, :] = d_query[i * HW : (i + 1) * HW]
    for j in range(GROUP):
        early = slice(j * HW, (j + 1) * HW)
        late = slice((GROUP + j) * HW, (GROUP + j + 1) * HW)
        back[j, :HW, :] = (dk[early, :] * SCALE).astype(BF16)
        back[j, HW:, :] = dv[early, :].astype(BF16)
        own[j, 2 * HW : 3 * HW, :] = (dk[late, :] * SCALE).astype(BF16)
        own[j, 3 * HW :, :] = dv[late, :].astype(BF16)


def far_backward(place, mine, past, kept, result, sent, told):
    return pl.pallas_call(
        far_backward_kernel,
        in_specs=[SM] + [VM] * 6,
        out_specs=[VM, VM],
        out_shape=[
            jax.ShapeDtypeStruct((GROUP, 4 * HW, DH), BF16),
            jax.ShapeDtypeStruct((GROUP, 2 * HW, DH), BF16),
        ],
        scratch_shapes=[
            pltpu.VMEM((DH, 2 * GROUP * HW), BF16),
            pltpu.VMEM((2 * GROUP * HW, DH), BF16),
            pltpu.VMEM((2 * GROUP * HW, DH), F32),
            pltpu.VMEM((2 * GROUP * HW, DH), F32),
            pltpu.VMEM((KEYS, PAIR), BF16),
        ],
        compiler_params=params(),
        cost_estimate=cost(32 * KEYS * PAIR * DH, 6_000_000),
        name="far_backward",
    )(place, mine, past, kept, result, sent, told)


def add_back_kernel(own, back, out):
    out[:, : 2 * HW, :] = own[:, : 2 * HW, :]
    for j in range(GROUP):
        out[j, 2 * HW : 4 * HW, :] = (
            own[j, 2 * HW :, :].astype(F32) + back[j].astype(F32)
        ).astype(BF16)
        out[j, 4 * HW :, :] = jnp.zeros((ROWS - 4 * HW, DH), BF16)


def add_back(own, back):
    return pl.pallas_call(
        add_back_kernel,
        in_specs=[VM] * 2,
        out_specs=VM,
        out_shape=jax.ShapeDtypeStruct((GROUP, ROWS, DH), BF16),
        compiler_params=params(),
        cost_estimate=cost(GROUP * 2 * HW * DH, 2_500_000),
        name="add_back",
    )(own, back)


def unproject_kernel(place, near0, near1, near2, near3, far, wq, wk, wv, wo, own, other, close):
    for step, near in enumerate((near0, near1, near2, near3)):
        close[lax.rem(place[2] + step, HALF)] = near[...]
    parts = []
    for part in range(4):
        rows = slice(part * HW, (part + 1) * HW)
        pieces = []
        for h in range(HALF):
            away = jnp.concatenate([far[h, 0, rows, :], far[h, 1, rows, :]], axis=0)
            here = jnp.concatenate([close[h, 0, rows, :], close[h, 1, rows, :]], axis=0)
            pieces.append((away.astype(F32) + here.astype(F32)).astype(BF16))
        parts.append(jnp.concatenate(pieces, axis=1))
    mixed = mm(parts[0], wo[...])
    total = mm_nt(parts[1], wq[...]) + mm_nt(parts[2], wk[...]) + mm_nt(parts[3], wv[...])
    own[0] = mixed[:HW]
    own[1] = total[:HW]
    other[0] = mixed[HW:].astype(BF16)
    other[1] = total[HW:].astype(BF16)


def unproject(place, blocks, far, weights):
    return pl.pallas_call(
        unproject_kernel,
        in_specs=[SM] + [VM] * 9,
        out_specs=[VM, VM],
        out_shape=[jax.ShapeDtypeStruct((2, HW, D), F32), jax.ShapeDtypeStruct((2, HW, D), BF16)],
        scratch_shapes=[pltpu.VMEM((HALF, 2, 4 * HW, DH), BF16)],
        compiler_params=params(),
        cost_estimate=cost(2 * PAIR * D * 4 * HALF * DH, 8_000_000),
        name="unproject",
    )(place, *blocks, far, *weights)


def finish_kernel(tokens, cot, gain, own, other, mixed, out):
    x = tokens[...].astype(F32)
    mixed[...] = (x + (own[0] + other[0].astype(F32))).astype(BF16)
    rinv = lax.rsqrt(jnp.mean(x * x, axis=-1, keepdims=True) + EPS)
    scaled = (own[1] + other[1].astype(F32)) * gain[...]
    mean = jnp.mean(scaled * x, axis=-1, keepdims=True)
    grad = rinv * scaled - x * (rinv * rinv * rinv * mean)
    out[...] = (cot[...].astype(F32) + grad).astype(BF16)


def finish(tokens, cot, gain, own, other):
    return pl.pallas_call(
        finish_kernel,
        in_specs=[VM] * 5,
        out_specs=[VM] * 2,
        out_shape=[jax.ShapeDtypeStruct((HW, D), BF16)] * 2,
        compiler_params=params(),
        cost_estimate=cost(HW * D * 10, 3_000_000),
        name="finish",
    )(tokens, cot, gain, own, other)


LANE = ("x", "zl")


def swap(value):
    return lax.ppermute(value, "core", [(0, 1), (1, 0)])


def turn_ring(value, steps):
    return lax.ppermute(value, "zh", [(i, (i + steps) % 4) for i in range(4)])


def exchange(value, axes):
    return lax.all_to_all(value, axes, 0, 0, tiled=True)


def exchange_alone(value, go):
    return lax.cond(go, lambda v: exchange(v, LANE), jnp.zeros_like, value)


def per_device(tokens, gain, w_qkv, w_out, window, valid, cotangent):
    rows = lax.axis_size("y")
    place = jnp.stack(
        [lax.axis_index(axis) for axis in ("core", "x", "zh")]
    ).astype(jnp.int32)
    go = window[0] > 0
    tokens = tokens.reshape(HW, D)
    cot = cotangent.reshape(HW, D)
    other_tokens = swap(tokens)
    other_cot = swap(cot)
    tokens, cot, gain, *weights = stage(place, tokens, cot, gain.reshape(1, D), w_qkv, w_out)
    packed, *blocks = project(
        place, valid, tokens, other_tokens, cot, other_cot, gain, weights
    )
    blocks = [blocks[0]] + [turn_ring(blocks[step], step) for step in (1, 2, 3)]
    mine = exchange_alone(packed.reshape(2 * HALF, ROWS, DH), go)
    past = lax.ppermute(mine[:, K0:, :], "y", [(i, i + 1) for i in range(rows - 1)])
    near_kept, near_result, close = near_forward(*blocks)
    sent, far_kept, far_result = far_forward(place, window, mine, past, close)
    told = exchange(sent, ("x", "zl", "zh"))
    own, back = far_backward(place, mine, past, far_kept, far_result, sent, told)
    back = lax.ppermute(back, "y", [(i + 1, i) for i in range(rows - 1)])
    returned = near_backward(place, blocks, near_kept, near_result, close, told)
    own, returned = lax.optimization_barrier((own, returned))
    returned = [returned[0]] + [turn_ring(returned[step], -step) for step in (1, 2, 3)]
    own = add_back(own, back)
    far = exchange_alone(own, go).reshape(HALF, 2, ROWS, DH)
    out_own, out_other = unproject(place, returned, far, weights)
    mixed, d_tokens = finish(tokens, cot, gain, out_own, swap(out_other))
    return mixed.reshape(1, 1, HW, D), d_tokens.reshape(1, 1, HW, D)


def solution(mesh):
    grid = Mesh(mesh.devices.reshape(4, 4, 2, 4, 2), ("y", "x", "zl", "zh", "core"))
    frames, cams = ("y", "x", "zl"), ("zh", "core")
    split = P(frames, cams, None, None)
    return jax.shard_map(
        per_device,
        mesh=grid,
        in_specs=(split, P(), P(), P(), P(), P(frames), split),
        out_specs=(split, split),
        check_vma=False,
    )
```

```python
import math

import jax
import jax.numpy as jnp
from jax import lax
from jax.experimental import pallas as pl
from jax.experimental.pallas import tpu as pltpu
from jax.sharding import Mesh
from jax.sharding import PartitionSpec as P

D = 1024
H = 8
DH = 128
HW = 128
WIN = 8
EPS = 1e-05

HALF = H // 2
PAIR = 2 * HW
GROUP = 8
SCALE = DH ** (-0.5)
SCALE2 = SCALE * math.log2(math.e)
FLOOR = -3.0e38
F32 = jnp.float32
BF16 = jnp.bfloat16
NT = (((1,), (1,)), ((), ()))
VMEM_LIMIT = 20 * 1024 * 1024
STAGE_LIMIT = 48 * 1024 * 1024

Q0, G0, K0, V0, OK0, ROWS = 0, 128, 256, 384, 512, 528
TOKENS = 8 * HW
KEYS = (WIN + 1) * HW


def params(**kw):
    return pltpu.CompilerParams(vmem_limit_bytes=VMEM_LIMIT, **kw)


def mm(a, b):
    return jnp.dot(a, b, preferred_element_type=F32)


def mm_nt(a, b):
    return lax.dot_general(a, b, NT, preferred_element_type=F32)


def turn(a):
    return a.astype(F32).T


VM = pl.BlockSpec(memory_space=pltpu.VMEM)
SM = pl.BlockSpec(memory_space=pltpu.SMEM)
ANY = pl.BlockSpec(memory_space=pltpu.HBM)


def cost(flops, size, exps=0):
    return pl.CostEstimate(flops=flops, bytes_accessed=size, transcendentals=exps)


def stage_kernel(place, w_qkv, w_out, wq, wk, wv, out, sems):
    core = place[0]
    copies = [
        pltpu.make_async_copy(
            w_out.at[pl.ds(pl.multiple_of(core * HALF * DH, HALF * DH), HALF * DH), :],
            out,
            sems.at[3],
        ),
    ]
    for part in range(3):
        start = pl.multiple_of(part * D + core * HALF * DH, HALF * DH)
        copies.append(
            pltpu.make_async_copy(
                w_qkv.at[:, pl.ds(start, HALF * DH)], (wq, wk, wv)[part], sems.at[part]
            )
        )
    for copy in copies:
        copy.start()
    for copy in copies:
        copy.wait()


def stage(place, w_qkv, w_out):
    return pl.pallas_call(
        stage_kernel,
        in_specs=[SM] + [ANY] * 2,
        out_specs=[VM] * 4,
        out_shape=[jax.ShapeDtypeStruct((D, HALF * DH), BF16)] * 3
        + [jax.ShapeDtypeStruct((HALF * DH, D), BF16)],
        scratch_shapes=[pltpu.SemaphoreType.DMA((4,))],
        compiler_params=pltpu.CompilerParams(vmem_limit_bytes=STAGE_LIMIT),
        cost_estimate=cost(0, 9_000_000),
        name="stage",
    )(place, w_qkv, w_out)


def slot_of_head(place, h):
    return lax.rem(h + HALF - place[2], HALF)


def head_here(place, step=0):
    return lax.rem(place[1] + place[2] + step, HALF)


def project_kernel(
    place, valid, own, other, cot_own, cot_other, gain, wq, wk, wv, wo, packed, near0, near1, near2, near3
):
    x = jnp.concatenate([own[...], other[...]], axis=0).astype(F32)
    rinv = lax.rsqrt(jnp.mean(x * x, axis=-1, keepdims=True) + EPS)
    normed = (x * rinv * gain[...]).astype(BF16)
    cot = jnp.concatenate([cot_own[...], cot_other[...]], axis=0)
    flags = jnp.full((ROWS - OK0, DH), valid[0], jnp.int32).astype(F32).astype(BF16)
    for row in (Q0, K0, V0, G0):
        if row == G0:
            got = mm_nt(cot, wo[...]).astype(BF16)
        else:
            got = mm(normed, {Q0: wq, K0: wk, V0: wv}[row][...]).astype(BF16)
        for h in range(HALF):
            for s in range(2):
                packed[slot_of_head(place, h), s, row : row + HW, :] = (
                    got[s * HW : (s + 1) * HW, h * DH : (h + 1) * DH]
                )
    for h in range(HALF):
        for s in range(2):
            packed[h, s, OK0:ROWS, :] = flags
    for step, near in enumerate((near0, near1, near2, near3)):
        slot = lax.rem(place[1] + step, HALF)
        for s in range(2):
            near[s] = packed[slot, s, :OK0, :]


def project(place, valid, own, other, cot_own, cot_other, gain, weights):
    return pl.pallas_call(
        project_kernel,
        in_specs=[SM, SM] + [VM] * 9,
        out_specs=[VM] * 5,
        out_shape=[jax.ShapeDtypeStruct((HALF, 2, ROWS, DH), BF16)]
        + [jax.ShapeDtypeStruct((2, OK0, DH), BF16)] * 4,
        compiler_params=params(),
        cost_estimate=cost(2 * PAIR * D * 4 * HALF * DH, 7_000_000),
        name="project",
    )(place, valid, own, other, cot_own, cot_other, gain, *weights)


def both(block, row):
    return jnp.concatenate([block[0, row : row + HW, :], block[1, row : row + HW, :]], axis=0)


def near_forward_kernel(near0, near1, near2, near3, kept, result, stats, scores):
    blocks = (near0, near1, near2, near3)
    turned = [turn(both(block, V0)).astype(BF16) for block in blocks]
    for g in range(4):
        cols = slice(g * PAIR, (g + 1) * PAIR)
        query = both(blocks[g], Q0)
        grad_t = turn(both(blocks[g], G0))
        peak = jnp.full((1, PAIR), -jnp.inf, F32)
        for z in range(4):
            block = mm_nt(both(blocks[z], K0), query)
            scores[z * PAIR : (z + 1) * PAIR, :] = block
            peak = jnp.maximum(peak, jnp.max(block, axis=0, keepdims=True))
        peak = peak * SCALE2
        total = jnp.zeros((1, PAIR), F32)
        for b in range(8):
            rows = slice(b * HW, (b + 1) * HW)
            block = jnp.exp2(scores[rows, :] * SCALE2 - peak)
            total = total + jnp.sum(block, axis=0, keepdims=True)
            kept[rows, cols] = block.astype(BF16)
        got = jnp.zeros((DH, PAIR), F32)
        for z in range(4):
            got = got + mm(turned[z], kept[z * PAIR : (z + 1) * PAIR, cols])
        result[:, cols] = got
        delta = jnp.sum(got * grad_t, axis=0, keepdims=True)
        told = jnp.concatenate([peak, total, delta, jnp.zeros((1, PAIR), F32)], axis=0)
        stats[2 * g] = told[:, :HW]
        stats[2 * g + 1] = told[:, HW:]


def near_forward(*blocks):
    return pl.pallas_call(
        near_forward_kernel,
        in_specs=[VM] * 4,
        out_specs=[VM] * 3,
        out_shape=[
            jax.ShapeDtypeStruct((TOKENS, TOKENS), BF16),
            jax.ShapeDtypeStruct((DH, TOKENS), F32),
            jax.ShapeDtypeStruct((8, 4, HW), F32),
        ],
        scratch_shapes=[pltpu.VMEM((TOKENS, PAIR), F32)],
        compiler_params=params(),
        cost_estimate=cost(80 * TOKENS * TOKENS * DH, 4_000_000, TOKENS * TOKENS),
        name="near_forward",
    )(*blocks)


def slot_of_near(place, step, s):
    return lax.rem(place[1] + step, 4) * 2 + s


def far_forward_kernel(place, win, mine, past, close, told, kept, result, keys, values_t, scores):
    width = win[place[0] * HALF + head_here(place)]
    for step in range(4):
        for s in range(2):
            told[slot_of_near(place, step, s), 0:4, :] = close[2 * step + s]
    for j in range(GROUP):
        keys[j * HW : (j + 1) * HW, :] = past[j, :HW, :]
        keys[(GROUP + j) * HW : (GROUP + j + 1) * HW, :] = mine[j, K0 : K0 + HW, :]
        values_t[:, j * HW : (j + 1) * HW] = turn(past[j, HW : 2 * HW, :]).astype(BF16)
        values_t[:, (GROUP + j) * HW : (GROUP + j + 1) * HW] = turn(
            mine[j, V0 : V0 + HW, :]
        ).astype(BF16)
    for p in range(GROUP // 2):
        query = jnp.concatenate([mine[2 * p, :HW, :], mine[2 * p + 1, :HW, :]], axis=0)
        grad_t = jnp.concatenate(
            [turn(mine[2 * p, G0 : G0 + HW, :]), turn(mine[2 * p + 1, G0 : G0 + HW, :])], axis=1
        )
        peak = jnp.full((1, PAIR), -jnp.inf, F32)
        for b in range(WIN + 1):
            j = 2 * p + b
            if j < GROUP:
                flag = past[j, 2 * HW : 2 * HW + 1, :].astype(F32)
            else:
                flag = mine[j - GROUP, OK0 : OK0 + 1, :].astype(F32)
            lower = jnp.where((flag > 0.5) & (b >= WIN - width) & (b < WIN), 0.0, -jnp.inf)
            upper = jnp.where((flag > 0.5) & (b >= WIN + 1 - width), 0.0, -jnp.inf)
            bias = jnp.concatenate([lower, upper], axis=1)
            block = mm_nt(keys[j * HW : (j + 1) * HW, :], query) + bias
            scores[b * HW : (b + 1) * HW, :] = block
            peak = jnp.maximum(peak, jnp.max(block, axis=0, keepdims=True))
        peak = jnp.maximum(peak * SCALE2, FLOOR)
        total = jnp.zeros((1, PAIR), F32)
        for b in range(WIN + 1):
            block = jnp.exp2(scores[b * HW : (b + 1) * HW, :] * SCALE2 - peak)
            total = total + jnp.sum(block, axis=0, keepdims=True)
            kept[p, b * HW : (b + 1) * HW, :] = block.astype(BF16)
        got = mm(values_t[:, p * PAIR : p * PAIR + KEYS], kept[p])
        result[:, p * PAIR : (p + 1) * PAIR] = got
        delta = jnp.sum(got * grad_t, axis=0, keepdims=True)
        stats = jnp.concatenate([peak, total, delta, jnp.zeros((1, PAIR), F32)], axis=0)
        told[2 * p, 4:8, :] = stats[:, :HW]
        told[2 * p + 1, 4:8, :] = stats[:, HW:]


def far_forward(place, window, mine, past, close):
    return pl.pallas_call(
        far_forward_kernel,
        in_specs=[SM, SM, VM, VM, VM],
        out_specs=[VM] * 3,
        out_shape=[
            jax.ShapeDtypeStruct((GROUP, 8, HW), F32),
            jax.ShapeDtypeStruct((GROUP // 2, KEYS, PAIR), BF16),
            jax.ShapeDtypeStruct((DH, GROUP * HW), F32),
        ],
        scratch_shapes=[
            pltpu.VMEM((2 * GROUP * HW, DH), BF16),
            pltpu.VMEM((DH, 2 * GROUP * HW), BF16),
            pltpu.VMEM((KEYS, PAIR), F32),
        ],
        compiler_params=params(),
        cost_estimate=cost(16 * KEYS * PAIR * DH, 5_000_000, 4 * KEYS * PAIR),
        name="far_forward",
    )(place, window, mine, past, close)


def merge(this, other):
    top = jnp.maximum(this[0:1], other[0:1])
    here = jnp.exp2(this[0:1] - top)
    there = jnp.exp2(other[0:1] - top)
    inverse = 1.0 / (here * this[1:2] + there * other[1:2])
    here = here * inverse
    delta = here * this[2:3] + there * inverse * other[2:3]
    return here, here * delta


def near_backward_kernel(
    place, near0, near1, near2, near3, kept, result, stats, told,
    back0, back1, back2, back3, grads, grad_all, query_all,
):
    blocks = (near0, near1, near2, near3)
    outs = (back0, back1, back2, back3)
    for g in range(4):
        cols = slice(g * PAIR, (g + 1) * PAIR)
        this = jnp.concatenate([stats[2 * g], stats[2 * g + 1]], axis=1)
        other = jnp.concatenate(
            [told[slot_of_near(place, g, s), 4:8, :] for s in range(2)], axis=1
        )
        weight, delta = merge(this, other)
        grad_t = (turn(both(blocks[g], G0)) * weight).astype(BF16)
        grad_all[:, cols] = grad_t
        query_all[cols, :] = both(blocks[g], Q0)
        attended = (result[:, cols] * weight).T.astype(BF16)
        for s in range(2):
            outs[g][s, :HW, :] = attended[s * HW : (s + 1) * HW]
        for z in range(4):
            rows = slice(z * PAIR, (z + 1) * PAIR)
            d_probs = mm(both(blocks[z], V0), grad_t)
            grads[rows, cols] = (kept[rows, cols].astype(F32) * (d_probs - delta)).astype(BF16)
    for z in range(4):
        rows = slice(z * PAIR, (z + 1) * PAIR)
        d_values = mm_nt(kept[rows, :], grad_all[...]).astype(BF16)
        d_keys = (mm(grads[rows, :], query_all[...]) * SCALE).astype(BF16)
        for s in range(2):
            outs[z][s, 2 * HW : 3 * HW, :] = d_keys[s * HW : (s + 1) * HW]
            outs[z][s, 3 * HW :, :] = d_values[s * HW : (s + 1) * HW]
    keys_t = jnp.concatenate([turn(both(block, K0)).astype(BF16) for block in blocks], axis=1)
    for g in range(4):
        cols = slice(g * PAIR, (g + 1) * PAIR)
        d_query = (mm(keys_t, grads[:, cols]) * SCALE).T.astype(BF16)
        for s in range(2):
            outs[g][s, HW : 2 * HW, :] = d_query[s * HW : (s + 1) * HW]


def near_backward(place, blocks, kept, result, stats, told):
    return pl.pallas_call(
        near_backward_kernel,
        in_specs=[SM] + [VM] * 8,
        out_specs=[VM] * 4,
        out_shape=[jax.ShapeDtypeStruct((2, 4 * HW, DH), BF16)] * 4,
        scratch_shapes=[
            pltpu.VMEM((TOKENS, TOKENS), BF16),
            pltpu.VMEM((DH, TOKENS), BF16),
            pltpu.VMEM((TOKENS, DH), BF16),
        ],
        compiler_params=params(),
        cost_estimate=cost(8 * TOKENS * TOKENS * DH, 5_000_000),
        name="near_backward",
    )(place, *blocks, kept, result, stats, told)


def far_backward_kernel(
    place, mine, past, kept, result, sent, told, own, back, keys_t, values, dk, dv, grads
):
    for j in range(GROUP):
        keys_t[:, j * HW : (j + 1) * HW] = turn(past[j, :HW, :]).astype(BF16)
        keys_t[:, (GROUP + j) * HW : (GROUP + j + 1) * HW] = turn(
            mine[j, K0 : K0 + HW, :]
        ).astype(BF16)
        values[j * HW : (j + 1) * HW, :] = past[j, HW : 2 * HW, :]
        values[(GROUP + j) * HW : (GROUP + j + 1) * HW, :] = mine[j, V0 : V0 + HW, :]
    dk[...] = jnp.zeros_like(dk)
    dv[...] = jnp.zeros_like(dv)
    for p in range(GROUP // 2):
        query = jnp.concatenate([mine[2 * p, :HW, :], mine[2 * p + 1, :HW, :]], axis=0)
        grad_t = jnp.concatenate(
            [turn(mine[2 * p, G0 : G0 + HW, :]), turn(mine[2 * p + 1, G0 : G0 + HW, :])], axis=1
        )
        this = jnp.concatenate([sent[2 * p, 4:8, :], sent[2 * p + 1, 4:8, :]], axis=1)
        other = jnp.concatenate([told[2 * p, 0:4, :], told[2 * p + 1, 0:4, :]], axis=1)
        weight, delta = merge(this, other)
        grad_t = (grad_t * weight).astype(BF16)
        at = p * PAIR
        attended = (result[:, at : at + PAIR] * weight).T.astype(BF16)
        for lo, size in ((0, 384), (384, 384), (768, 384)):
            rows = slice(lo, lo + size)
            spot = slice(at + lo, at + lo + size)
            d_probs = mm(values[spot, :], grad_t)
            block = kept[p, rows, :]
            d_scores = (block.astype(F32) * (d_probs - delta)).astype(BF16)
            grads[rows, :] = d_scores
            dv[spot, :] += mm_nt(block, grad_t)
            dk[spot, :] += mm(d_scores, query)
        d_query = (mm(keys_t[:, at : at + KEYS], grads[...]) * SCALE).T.astype(BF16)
        for i in range(2):
            own[2 * p + i, :HW, :] = attended[i * HW : (i + 1) * HW]
            own[2 * p + i, HW : 2 * HW, :] = d_query[i * HW : (i + 1) * HW]
    for j in range(GROUP):
        early = slice(j * HW, (j + 1) * HW)
        late = slice((GROUP + j) * HW, (GROUP + j + 1) * HW)
        back[j, :HW, :] = (dk[early, :] * SCALE).astype(BF16)
        back[j, HW:, :] = dv[early, :].astype(BF16)
        own[j, 2 * HW : 3 * HW, :] = (dk[late, :] * SCALE).astype(BF16)
        own[j, 3 * HW :, :] = dv[late, :].astype(BF16)


def far_backward(place, mine, past, kept, result, sent, told):
    return pl.pallas_call(
        far_backward_kernel,
        in_specs=[SM] + [VM] * 6,
        out_specs=[VM, VM],
        out_shape=[
            jax.ShapeDtypeStruct((GROUP, 4 * HW, DH), BF16),
            jax.ShapeDtypeStruct((GROUP, 2 * HW, DH), BF16),
        ],
        scratch_shapes=[
            pltpu.VMEM((DH, 2 * GROUP * HW), BF16),
            pltpu.VMEM((2 * GROUP * HW, DH), BF16),
            pltpu.VMEM((2 * GROUP * HW, DH), F32),
            pltpu.VMEM((2 * GROUP * HW, DH), F32),
            pltpu.VMEM((KEYS, PAIR), BF16),
        ],
        compiler_params=params(),
        cost_estimate=cost(32 * KEYS * PAIR * DH, 6_000_000),
        name="far_backward",
    )(place, mine, past, kept, result, sent, told)


def add_back_kernel(own, back, out):
    out[:, : 2 * HW, :] = own[:, : 2 * HW, :]
    for j in range(GROUP):
        out[j, 2 * HW : 4 * HW, :] = (
            own[j, 2 * HW :, :].astype(F32) + back[j].astype(F32)
        ).astype(BF16)
        out[j, 4 * HW :, :] = jnp.zeros((ROWS - 4 * HW, DH), BF16)


def add_back(own, back):
    return pl.pallas_call(
        add_back_kernel,
        in_specs=[VM] * 2,
        out_specs=VM,
        out_shape=jax.ShapeDtypeStruct((GROUP, ROWS, DH), BF16),
        compiler_params=params(),
        cost_estimate=cost(GROUP * 2 * HW * DH, 2_500_000),
        name="add_back",
    )(own, back)


def unproject_kernel(place, near0, near1, near2, near3, far, wq, wk, wv, wo, own, other, close):
    for step, near in enumerate((near0, near1, near2, near3)):
        close[head_here(place, step)] = near[...]
    parts = []
    for part in range(4):
        rows = slice(part * HW, (part + 1) * HW)
        pieces = []
        for h in range(HALF):
            slot = slot_of_head(place, h)
            away = jnp.concatenate([far[slot, 0, rows, :], far[slot, 1, rows, :]], axis=0)
            here = jnp.concatenate([close[h, 0, rows, :], close[h, 1, rows, :]], axis=0)
            pieces.append((away.astype(F32) + here.astype(F32)).astype(BF16))
        parts.append(jnp.concatenate(pieces, axis=1))
    mixed = mm(parts[0], wo[...])
    total = mm_nt(parts[1], wq[...]) + mm_nt(parts[2], wk[...]) + mm_nt(parts[3], wv[...])
    own[0] = mixed[:HW]
    own[1] = total[:HW]
    other[0] = mixed[HW:].astype(BF16)
    other[1] = total[HW:].astype(BF16)


def unproject(place, blocks, far, w_qkv, w_out):
    whole = lambda shape: pl.BlockSpec(shape, lambda i, place: (0,) * len(shape))
    part = lambda at: pl.BlockSpec((D, HALF * DH), lambda i, place: (0, at * 2 + place[0]))
    return pl.pallas_call(
        unproject_kernel,
        grid_spec=pltpu.PrefetchScalarGridSpec(
            num_scalar_prefetch=1,
            grid=(1,),
            in_specs=[whole((2, 4 * HW, DH))] * 4
            + [whole((HALF, 2, ROWS, DH)), part(0), part(1), part(2)]
            + [pl.BlockSpec((HALF * DH, D), lambda i, place: (place[0], 0))],
            out_specs=[whole((2, HW, D))] * 2,
            scratch_shapes=[pltpu.VMEM((HALF, 2, 4 * HW, DH), BF16)],
        ),
        out_shape=[jax.ShapeDtypeStruct((2, HW, D), F32), jax.ShapeDtypeStruct((2, HW, D), BF16)],
        compiler_params=pltpu.CompilerParams(vmem_limit_bytes=50 * 1024 * 1024),
        cost_estimate=cost(2 * PAIR * D * 4 * HALF * DH, 8_000_000),
        name="unproject",
    )(place, *blocks, far, w_qkv, w_qkv, w_qkv, w_out)


def finish_kernel(tokens, cot, gain, own, other, mixed, out):
    x = tokens[...].astype(F32)
    mixed[...] = (x + (own[0] + other[0].astype(F32))).astype(BF16)
    rinv = lax.rsqrt(jnp.mean(x * x, axis=-1, keepdims=True) + EPS)
    scaled = (own[1] + other[1].astype(F32)) * gain[...]
    mean = jnp.mean(scaled * x, axis=-1, keepdims=True)
    grad = rinv * scaled - x * (rinv * rinv * rinv * mean)
    out[...] = (cot[...].astype(F32) + grad).astype(BF16)


def finish(tokens, cot, gain, own, other):
    return pl.pallas_call(
        finish_kernel,
        in_specs=[VM] * 5,
        out_specs=[VM] * 2,
        out_shape=[jax.ShapeDtypeStruct((HW, D), BF16)] * 2,
        compiler_params=params(),
        cost_estimate=cost(HW * D * 10, 3_000_000),
        name="finish",
    )(tokens, cot, gain, own, other)


LANE = ("x", "zl")
SAME_HEAD = [
    [(x * 2 + zl) * 4 + (h + 4 - x) % 4 for x in range(4) for zl in range(2)] for h in range(4)
]


def swap(value):
    return lax.ppermute(value, "core", [(0, 1), (1, 0)])


def turn_ring(value, steps):
    return lax.ppermute(value, "zh", [(i, (i + steps) % 4) for i in range(4)])


def exchange(value, axes, groups=None):
    return lax.all_to_all(value, axes, 0, 0, axis_index_groups=groups, tiled=True)


def exchange_alone(value, go):
    return lax.cond(go, lambda v: exchange(v, LANE), jnp.zeros_like, value)


def per_device(tokens, gain, w_qkv, w_out, window, valid, cotangent):
    rows = lax.axis_size("y")
    place = jnp.stack(
        [lax.axis_index(axis) for axis in ("core", "x", "zh")]
    ).astype(jnp.int32)
    go = window[0] > 0
    tokens = tokens.reshape(HW, D)
    cot = cotangent.reshape(HW, D)
    other_tokens = swap(tokens)
    other_cot = swap(cot)
    gain = gain.reshape(1, D)
    weights = stage(place, w_qkv, w_out)
    packed, *blocks = project(
        place, valid, tokens, other_tokens, cot, other_cot, gain, weights
    )
    blocks = [blocks[0]] + [turn_ring(blocks[step], step) for step in (1, 2, 3)]
    mine = exchange(packed.reshape(2 * HALF, ROWS, DH), LANE)
    past = lax.ppermute(mine[:, K0:, :], "y", [(i, i + 1) for i in range(rows - 1)])
    near_kept, near_result, close = near_forward(*blocks)
    sent, far_kept, far_result = far_forward(place, window, mine, past, close)
    told = exchange(sent, ("x", "zl", "zh"), SAME_HEAD)
    own, back = far_backward(place, mine, past, far_kept, far_result, sent, told)
    back = lax.ppermute(back, "y", [(i + 1, i) for i in range(rows - 1)])
    returned = near_backward(place, blocks, near_kept, near_result, close, told)
    own, returned = lax.optimization_barrier((own, returned))
    returned = [returned[0]] + [turn_ring(returned[step], -step) for step in (1, 2, 3)]
    own = add_back(own, back)
    far = exchange_alone(own, go).reshape(HALF, 2, ROWS, DH)
    out_own, out_other = unproject(place, returned, far, w_qkv, w_out)
    mixed, d_tokens = finish(tokens, cot, gain, out_own, swap(out_other))
    return mixed.reshape(1, 1, HW, D), d_tokens.reshape(1, 1, HW, D)


def solution(mesh):
    grid = Mesh(mesh.devices.reshape(4, 4, 2, 4, 2), ("y", "x", "zl", "zh", "core"))
    frames, cams = ("y", "x", "zl"), ("zh", "core")
    split = P(frames, cams, None, None)
    return jax.shard_map(
        per_device,
        mesh=grid,
        in_specs=(split, P(), P(), P(), P(), P(frames), split),
        out_specs=(split, split),
        check_vma=False,
    )
```

```python
import math

import jax
import jax.numpy as jnp
from jax import lax
from jax.experimental import pallas as pl
from jax.experimental.pallas import tpu as pltpu
from jax.sharding import Mesh
from jax.sharding import PartitionSpec as P

D = 1024
H = 8
DH = 128
HW = 128
WIN = 8
EPS = 1e-05

HALF = H // 2
PAIR = 2 * HW
GROUP = 8
SCALE = DH ** (-0.5)
SCALE2 = SCALE * math.log2(math.e)
FLOOR = -3.0e38
F32 = jnp.float32
BF16 = jnp.bfloat16
NT = (((1,), (1,)), ((), ()))
VMEM_LIMIT = 20 * 1024 * 1024
STAGE_LIMIT = 48 * 1024 * 1024

Q0, G0, K0, V0, OK0, ROWS = 0, 128, 256, 384, 512, 528
TOKENS = 8 * HW
KEYS = (WIN + 1) * HW


def params(**kw):
    return pltpu.CompilerParams(vmem_limit_bytes=VMEM_LIMIT, **kw)


def mm(a, b):
    return jnp.dot(a, b, preferred_element_type=F32)


def mm_nt(a, b):
    return lax.dot_general(a, b, NT, preferred_element_type=F32)


def turn(a):
    return a.astype(F32).T


VM = pl.BlockSpec(memory_space=pltpu.VMEM)
SM = pl.BlockSpec(memory_space=pltpu.SMEM)
ANY = pl.BlockSpec(memory_space=pltpu.HBM)


def cost(flops, size, exps=0):
    return pl.CostEstimate(flops=flops, bytes_accessed=size, transcendentals=exps)


def weight_copies(place, w_qkv, w_out, parts, out, sems):
    begin = pl.multiple_of(place[0] * HALF * DH, HALF * DH)
    copies = [
        pltpu.make_async_copy(
            w_qkv.at[:, pl.ds(pl.multiple_of(begin + part * D, HALF * DH), HALF * DH)],
            parts[part],
            sems.at[part],
        )
        for part in range(3)
    ]
    copies.append(
        pltpu.make_async_copy(w_out.at[pl.ds(begin, HALF * DH), :], out, sems.at[3])
    )
    return copies


def stage_kernel(place, w_qkv, w_out, wq, wk, wv, out, sems):
    copies = weight_copies(place, w_qkv, w_out, (wq, wk, wv), out, sems)
    for copy in copies:
        copy.start()
    for copy in copies:
        copy.wait()


def stage(place, w_qkv, w_out):
    return pl.pallas_call(
        stage_kernel,
        in_specs=[SM] + [ANY] * 2,
        out_specs=[VM] * 4,
        out_shape=[jax.ShapeDtypeStruct((D, HALF * DH), BF16)] * 3
        + [jax.ShapeDtypeStruct((HALF * DH, D), BF16)],
        scratch_shapes=[pltpu.SemaphoreType.DMA((4,))],
        compiler_params=pltpu.CompilerParams(vmem_limit_bytes=STAGE_LIMIT),
        cost_estimate=cost(0, 9_000_000),
        name="stage",
    )(place, w_qkv, w_out)


STEPS = (0, 2, 1, 3)


def slot_of_head(place, h):
    return lax.rem(h + HALF - place[2], HALF)


def head_here(place, step=0):
    return lax.rem(place[1] + place[2] + step, HALF)


def project_kernel(
    place, valid, own, other, cot_own, cot_other, gain, wq, wk, wv, wo, packed, near0, near1, near2, near3
):
    x = jnp.concatenate([own[...], other[...]], axis=0).astype(F32)
    rinv = lax.rsqrt(jnp.mean(x * x, axis=-1, keepdims=True) + EPS)
    normed = (x * rinv * gain[...]).astype(BF16)
    cot = jnp.concatenate([cot_own[...], cot_other[...]], axis=0)
    flags = jnp.full((ROWS - OK0, DH), valid[0], jnp.int32).astype(F32).astype(BF16)
    for row in (Q0, K0, V0, G0):
        if row == G0:
            got = mm_nt(cot, wo[...]).astype(BF16)
        else:
            got = mm(normed, {Q0: wq, K0: wk, V0: wv}[row][...]).astype(BF16)
        for h in range(HALF):
            for s in range(2):
                packed[slot_of_head(place, h), s, row : row + HW, :] = (
                    got[s * HW : (s + 1) * HW, h * DH : (h + 1) * DH]
                )
    for h in range(HALF):
        for s in range(2):
            packed[h, s, OK0:ROWS, :] = flags
    for step, near in zip(STEPS, (near0, near1, near2, near3)):
        slot = lax.rem(place[1] + step, HALF)
        for s in range(2):
            near[s] = packed[slot, s, :OK0, :]


def project(place, valid, own, other, cot_own, cot_other, gain, weights):
    return pl.pallas_call(
        project_kernel,
        in_specs=[SM, SM] + [VM] * 9,
        out_specs=[VM] * 5,
        out_shape=[jax.ShapeDtypeStruct((HALF, 2, ROWS, DH), BF16)]
        + [jax.ShapeDtypeStruct((2, OK0, DH), BF16)] * 4,
        compiler_params=params(),
        cost_estimate=cost(2 * PAIR * D * 4 * HALF * DH, 7_000_000),
        name="project",
    )(place, valid, own, other, cot_own, cot_other, gain, *weights)


def both(block, row):
    return jnp.concatenate([block[0, row : row + HW, :], block[1, row : row + HW, :]], axis=0)


def near_forward_kernel(near0, near1, near2, near3, kept, result, stats, scores):
    blocks = (near0, near1, near2, near3)
    turned = [turn(both(block, V0)).astype(BF16) for block in blocks]
    for g in range(4):
        cols = slice(g * PAIR, (g + 1) * PAIR)
        query = both(blocks[g], Q0)
        grad_t = turn(both(blocks[g], G0))
        peak = jnp.full((1, PAIR), -jnp.inf, F32)
        for z in range(4):
            block = mm_nt(both(blocks[z], K0), query)
            scores[z * PAIR : (z + 1) * PAIR, :] = block
            peak = jnp.maximum(peak, jnp.max(block, axis=0, keepdims=True))
        peak = peak * SCALE2
        total = jnp.zeros((1, PAIR), F32)
        for b in range(8):
            rows = slice(b * HW, (b + 1) * HW)
            block = jnp.exp2(scores[rows, :] * SCALE2 - peak)
            total = total + jnp.sum(block, axis=0, keepdims=True)
            kept[rows, cols] = block.astype(BF16)
        got = jnp.zeros((DH, PAIR), F32)
        for z in range(4):
            got = got + mm(turned[z], kept[z * PAIR : (z + 1) * PAIR, cols])
        result[:, cols] = got
        delta = jnp.sum(got * grad_t, axis=0, keepdims=True)
        told = jnp.concatenate([peak, total, delta, jnp.zeros((1, PAIR), F32)], axis=0)
        stats[2 * g] = told[:, :HW]
        stats[2 * g + 1] = told[:, HW:]


def near_forward(*blocks):
    return pl.pallas_call(
        near_forward_kernel,
        in_specs=[VM] * 4,
        out_specs=[VM] * 3,
        out_shape=[
            jax.ShapeDtypeStruct((TOKENS, TOKENS), BF16),
            jax.ShapeDtypeStruct((DH, TOKENS), F32),
            jax.ShapeDtypeStruct((8, 4, HW), F32),
        ],
        scratch_shapes=[pltpu.VMEM((TOKENS, PAIR), F32)],
        compiler_params=params(),
        cost_estimate=cost(80 * TOKENS * TOKENS * DH, 4_000_000, TOKENS * TOKENS),
        name="near_forward",
    )(*blocks)


def slot_of_near(place, step, s):
    return lax.rem(place[1] + step, 4) * 2 + s


def far_forward_kernel(place, win, mine, past, close, told, kept, result, keys, values_t, scores):
    width = win[place[0] * HALF + head_here(place)]
    for g in range(4):
        for s in range(2):
            told[slot_of_near(place, STEPS[g], s), 0:4, :] = close[2 * g + s]
    for j in range(GROUP):
        keys[j * HW : (j + 1) * HW, :] = past[j, :HW, :]
        keys[(GROUP + j) * HW : (GROUP + j + 1) * HW, :] = mine[j, K0 : K0 + HW, :]
        values_t[:, j * HW : (j + 1) * HW] = turn(past[j, HW : 2 * HW, :]).astype(BF16)
        values_t[:, (GROUP + j) * HW : (GROUP + j + 1) * HW] = turn(
            mine[j, V0 : V0 + HW, :]
        ).astype(BF16)
    for p in range(GROUP // 2):
        query = jnp.concatenate([mine[2 * p, :HW, :], mine[2 * p + 1, :HW, :]], axis=0)
        grad_t = jnp.concatenate(
            [turn(mine[2 * p, G0 : G0 + HW, :]), turn(mine[2 * p + 1, G0 : G0 + HW, :])], axis=1
        )
        peak = jnp.full((1, PAIR), -jnp.inf, F32)
        for b in range(WIN + 1):
            j = 2 * p + b
            if j < GROUP:
                flag = past[j, 2 * HW : 2 * HW + 1, :].astype(F32)
            else:
                flag = mine[j - GROUP, OK0 : OK0 + 1, :].astype(F32)
            lower = jnp.where((flag > 0.5) & (b >= WIN - width) & (b < WIN), 0.0, -jnp.inf)
            upper = jnp.where((flag > 0.5) & (b >= WIN + 1 - width), 0.0, -jnp.inf)
            bias = jnp.concatenate([lower, upper], axis=1)
            block = mm_nt(keys[j * HW : (j + 1) * HW, :], query) + bias
            scores[b * HW : (b + 1) * HW, :] = block
            peak = jnp.maximum(peak, jnp.max(block, axis=0, keepdims=True))
        peak = jnp.maximum(peak * SCALE2, FLOOR)
        total = jnp.zeros((1, PAIR), F32)
        for b in range(WIN + 1):
            block = jnp.exp2(scores[b * HW : (b + 1) * HW, :] * SCALE2 - peak)
            total = total + jnp.sum(block, axis=0, keepdims=True)
            kept[p, b * HW : (b + 1) * HW, :] = block.astype(BF16)
        got = mm(values_t[:, p * PAIR : p * PAIR + KEYS], kept[p])
        result[:, p * PAIR : (p + 1) * PAIR] = got
        delta = jnp.sum(got * grad_t, axis=0, keepdims=True)
        stats = jnp.concatenate([peak, total, delta, jnp.zeros((1, PAIR), F32)], axis=0)
        told[2 * p, 4:8, :] = stats[:, :HW]
        told[2 * p + 1, 4:8, :] = stats[:, HW:]


def far_forward(place, window, mine, past, close):
    return pl.pallas_call(
        far_forward_kernel,
        in_specs=[SM, SM, VM, VM, VM],
        out_specs=[VM] * 3,
        out_shape=[
            jax.ShapeDtypeStruct((GROUP, 8, HW), F32),
            jax.ShapeDtypeStruct((GROUP // 2, KEYS, PAIR), BF16),
            jax.ShapeDtypeStruct((DH, GROUP * HW), F32),
        ],
        scratch_shapes=[
            pltpu.VMEM((2 * GROUP * HW, DH), BF16),
            pltpu.VMEM((DH, 2 * GROUP * HW), BF16),
            pltpu.VMEM((KEYS, PAIR), F32),
        ],
        compiler_params=params(),
        cost_estimate=cost(16 * KEYS * PAIR * DH, 5_000_000, 4 * KEYS * PAIR),
        name="far_forward",
    )(place, window, mine, past, close)


def merge(this, other):
    top = jnp.maximum(this[0:1], other[0:1])
    here = jnp.exp2(this[0:1] - top)
    there = jnp.exp2(other[0:1] - top)
    inverse = 1.0 / (here * this[1:2] + there * other[1:2])
    here = here * inverse
    delta = here * this[2:3] + there * inverse * other[2:3]
    return here, here * delta


def near_backward_kernel(
    place, near0, near1, near2, near3, kept, result, stats, told,
    back0, back1, back2, back3, grads, grad_all, query_all,
):
    blocks = (near0, near1, near2, near3)
    outs = (back0, back1, back2, back3)
    for g in range(4):
        cols = slice(g * PAIR, (g + 1) * PAIR)
        this = jnp.concatenate([stats[2 * g], stats[2 * g + 1]], axis=1)
        other = jnp.concatenate(
            [told[slot_of_near(place, STEPS[g], s), 4:8, :] for s in range(2)], axis=1
        )
        weight, delta = merge(this, other)
        grad_t = (turn(both(blocks[g], G0)) * weight).astype(BF16)
        grad_all[:, cols] = grad_t
        query_all[cols, :] = both(blocks[g], Q0)
        attended = (result[:, cols] * weight).T.astype(BF16)
        for s in range(2):
            outs[g][s, :HW, :] = attended[s * HW : (s + 1) * HW]
        for z in range(4):
            rows = slice(z * PAIR, (z + 1) * PAIR)
            d_probs = mm(both(blocks[z], V0), grad_t)
            grads[rows, cols] = (kept[rows, cols].astype(F32) * (d_probs - delta)).astype(BF16)
    for z in range(4):
        rows = slice(z * PAIR, (z + 1) * PAIR)
        d_values = mm_nt(kept[rows, :], grad_all[...]).astype(BF16)
        d_keys = (mm(grads[rows, :], query_all[...]) * SCALE).astype(BF16)
        for s in range(2):
            outs[z][s, 2 * HW : 3 * HW, :] = d_keys[s * HW : (s + 1) * HW]
            outs[z][s, 3 * HW :, :] = d_values[s * HW : (s + 1) * HW]
    keys_t = jnp.concatenate([turn(both(block, K0)).astype(BF16) for block in blocks], axis=1)
    for g in range(4):
        cols = slice(g * PAIR, (g + 1) * PAIR)
        d_query = (mm(keys_t, grads[:, cols]) * SCALE).T.astype(BF16)
        for s in range(2):
            outs[g][s, HW : 2 * HW, :] = d_query[s * HW : (s + 1) * HW]


def near_backward(place, blocks, kept, result, stats, told):
    return pl.pallas_call(
        near_backward_kernel,
        in_specs=[SM] + [VM] * 8,
        out_specs=[VM] * 4,
        out_shape=[jax.ShapeDtypeStruct((2, 4 * HW, DH), BF16)] * 4,
        scratch_shapes=[
            pltpu.VMEM((TOKENS, TOKENS), BF16),
            pltpu.VMEM((DH, TOKENS), BF16),
            pltpu.VMEM((TOKENS, DH), BF16),
        ],
        compiler_params=params(),
        cost_estimate=cost(8 * TOKENS * TOKENS * DH, 5_000_000),
        name="near_backward",
    )(place, *blocks, kept, result, stats, told)


def far_backward_kernel(
    place, mine, past, kept, result, sent, told, own, back, keys_t, values, dk, dv, grads
):
    for j in range(GROUP):
        keys_t[:, j * HW : (j + 1) * HW] = turn(past[j, :HW, :]).astype(BF16)
        keys_t[:, (GROUP + j) * HW : (GROUP + j + 1) * HW] = turn(
            mine[j, K0 : K0 + HW, :]
        ).astype(BF16)
        values[j * HW : (j + 1) * HW, :] = past[j, HW : 2 * HW, :]
        values[(GROUP + j) * HW : (GROUP + j + 1) * HW, :] = mine[j, V0 : V0 + HW, :]
    dk[...] = jnp.zeros_like(dk)
    dv[...] = jnp.zeros_like(dv)
    for p in range(GROUP // 2):
        query = jnp.concatenate([mine[2 * p, :HW, :], mine[2 * p + 1, :HW, :]], axis=0)
        grad_t = jnp.concatenate(
            [turn(mine[2 * p, G0 : G0 + HW, :]), turn(mine[2 * p + 1, G0 : G0 + HW, :])], axis=1
        )
        this = jnp.concatenate([sent[2 * p, 4:8, :], sent[2 * p + 1, 4:8, :]], axis=1)
        other = jnp.concatenate([told[2 * p, 0:4, :], told[2 * p + 1, 0:4, :]], axis=1)
        weight, delta = merge(this, other)
        grad_t = (grad_t * weight).astype(BF16)
        at = p * PAIR
        attended = (result[:, at : at + PAIR] * weight).T.astype(BF16)
        for lo, size in ((0, 384), (384, 384), (768, 384)):
            rows = slice(lo, lo + size)
            spot = slice(at + lo, at + lo + size)
            d_probs = mm(values[spot, :], grad_t)
            block = kept[p, rows, :]
            d_scores = (block.astype(F32) * (d_probs - delta)).astype(BF16)
            grads[rows, :] = d_scores
            dv[spot, :] += mm_nt(block, grad_t)
            dk[spot, :] += mm(d_scores, query)
        d_query = (mm(keys_t[:, at : at + KEYS], grads[...]) * SCALE).T.astype(BF16)
        for i in range(2):
            own[2 * p + i, :HW, :] = attended[i * HW : (i + 1) * HW]
            own[2 * p + i, HW : 2 * HW, :] = d_query[i * HW : (i + 1) * HW]
    for j in range(GROUP):
        early = slice(j * HW, (j + 1) * HW)
        late = slice((GROUP + j) * HW, (GROUP + j + 1) * HW)
        back[j, :HW, :] = (dk[early, :] * SCALE).astype(BF16)
        back[j, HW:, :] = dv[early, :].astype(BF16)
        own[j, 2 * HW : 3 * HW, :] = (dk[late, :] * SCALE).astype(BF16)
        own[j, 3 * HW : 4 * HW, :] = dv[late, :].astype(BF16)
        own[j, 4 * HW :, :] = jnp.zeros((ROWS - 4 * HW, DH), BF16)


def far_backward(place, mine, past, kept, result, sent, told):
    return pl.pallas_call(
        far_backward_kernel,
        in_specs=[SM] + [VM] * 6,
        out_specs=[VM, VM],
        out_shape=[
            jax.ShapeDtypeStruct((GROUP, ROWS, DH), BF16),
            jax.ShapeDtypeStruct((GROUP, 2 * HW, DH), BF16),
        ],
        scratch_shapes=[
            pltpu.VMEM((DH, 2 * GROUP * HW), BF16),
            pltpu.VMEM((2 * GROUP * HW, DH), BF16),
            pltpu.VMEM((2 * GROUP * HW, DH), F32),
            pltpu.VMEM((2 * GROUP * HW, DH), F32),
            pltpu.VMEM((KEYS, PAIR), BF16),
        ],
        compiler_params=params(),
        cost_estimate=cost(32 * KEYS * PAIR * DH, 6_000_000),
        name="far_backward",
    )(place, mine, past, kept, result, sent, told)


def add_back_kernel(own, back, out):
    for j in range(GROUP):
        out[j, 2 * HW : 4 * HW, :] = (
            own[j, 2 * HW : 4 * HW, :].astype(F32) + back[j].astype(F32)
        ).astype(BF16)


def add_back(own, back):
    return pl.pallas_call(
        add_back_kernel,
        in_specs=[VM] * 2,
        out_specs=VM,
        out_shape=jax.ShapeDtypeStruct((GROUP, ROWS, DH), BF16),
        input_output_aliases={0: 0},
        compiler_params=params(),
        cost_estimate=cost(GROUP * 2 * HW * DH, 2_500_000),
        name="add_back",
    )(own, back)


def unproject_kernel(
    place, near0, near1, near2, near3, far, w_qkv, w_out, own, other, close, wq, wk, wv, wo, sems
):
    copies = weight_copies(place, w_qkv, w_out, (wq, wk, wv), wo, sems)
    for copy in copies:
        copy.start()
    for step, near in zip(STEPS, (near0, near1, near2, near3)):
        close[head_here(place, step)] = near[...]
    parts = []
    for part in range(4):
        rows = slice(part * HW, (part + 1) * HW)
        pieces = []
        for h in range(HALF):
            slot = slot_of_head(place, h)
            away = jnp.concatenate([far[slot, 0, rows, :], far[slot, 1, rows, :]], axis=0)
            here = jnp.concatenate([close[h, 0, rows, :], close[h, 1, rows, :]], axis=0)
            pieces.append((away.astype(F32) + here.astype(F32)).astype(BF16))
        parts.append(jnp.concatenate(pieces, axis=1))
    copies[0].wait()
    total = mm_nt(parts[1], wq[...])
    copies[1].wait()
    total = total + mm_nt(parts[2], wk[...])
    copies[2].wait()
    total = total + mm_nt(parts[3], wv[...])
    copies[3].wait()
    mixed = mm(parts[0], wo[...])
    own[0] = mixed[:HW]
    own[1] = total[:HW]
    other[0] = mixed[HW:].astype(BF16)
    other[1] = total[HW:].astype(BF16)


def unproject(place, blocks, far, w_qkv, w_out):
    return pl.pallas_call(
        unproject_kernel,
        in_specs=[SM] + [VM] * 5 + [ANY] * 2,
        out_specs=[VM, VM],
        scratch_shapes=[pltpu.VMEM((HALF, 2, 4 * HW, DH), BF16)]
        + [pltpu.VMEM((D, HALF * DH), BF16)] * 3
        + [pltpu.VMEM((HALF * DH, D), BF16), pltpu.SemaphoreType.DMA((4,))],
        out_shape=[jax.ShapeDtypeStruct((2, HW, D), F32), jax.ShapeDtypeStruct((2, HW, D), BF16)],
        compiler_params=pltpu.CompilerParams(vmem_limit_bytes=50 * 1024 * 1024),
        cost_estimate=cost(2 * PAIR * D * 4 * HALF * DH, 8_000_000),
        name="unproject",
    )(place, *blocks, far, w_qkv, w_out)


def finish_kernel(tokens, cot, gain, own, other, mixed, out):
    x = tokens[...].astype(F32)
    mixed[...] = (x + (own[0] + other[0].astype(F32))).astype(BF16)
    rinv = lax.rsqrt(jnp.mean(x * x, axis=-1, keepdims=True) + EPS)
    scaled = (own[1] + other[1].astype(F32)) * gain[...]
    mean = jnp.mean(scaled * x, axis=-1, keepdims=True)
    grad = rinv * scaled - x * (rinv * rinv * rinv * mean)
    out[...] = (cot[...].astype(F32) + grad).astype(BF16)


def finish(tokens, cot, gain, own, other):
    return pl.pallas_call(
        finish_kernel,
        in_specs=[VM] * 5,
        out_specs=[VM] * 2,
        out_shape=[jax.ShapeDtypeStruct((HW, D), BF16)] * 2,
        compiler_params=params(),
        cost_estimate=cost(HW * D * 10, 3_000_000),
        name="finish",
    )(tokens, cot, gain, own, other)


LANE = ("x", "zl")
SAME_HEAD = [
    [(x * 2 + zl) * 4 + (h + 4 - x) % 4 for x in range(4) for zl in range(2)] for h in range(4)
]


def swap(value):
    return lax.ppermute(value, "core", [(0, 1), (1, 0)])


def turn_ring(value, steps):
    return lax.ppermute(value, "zh", [(i, (i + steps) % 4) for i in range(4)])


def all_round(blocks, sign):
    return [blocks[0]] + [turn_ring(blocks[g], sign * STEPS[g]) for g in (1, 2, 3)]


def exchange(value, axes, groups=None):
    return lax.all_to_all(value, axes, 0, 0, axis_index_groups=groups, tiled=True)


def exchange_alone(value, go):
    return lax.cond(go, lambda v: exchange(v, LANE), jnp.zeros_like, value)


def per_device(tokens, gain, w_qkv, w_out, window, valid, cotangent):
    rows = lax.axis_size("y")
    place = jnp.stack(
        [lax.axis_index(axis) for axis in ("core", "x", "zh")]
    ).astype(jnp.int32)
    go = window[0] > 0
    tokens = tokens.reshape(HW, D)
    cot = cotangent.reshape(HW, D)
    other_tokens = swap(tokens)
    other_cot = swap(cot)
    gain = gain.reshape(1, D)
    weights = stage(place, w_qkv, w_out)
    packed, *blocks = project(
        place, valid, tokens, other_tokens, cot, other_cot, gain, weights
    )
    blocks = all_round(blocks, 1)
    mine = exchange(packed.reshape(2 * HALF, ROWS, DH), LANE)
    past = lax.ppermute(mine[:, K0:, :], "y", [(i, i + 1) for i in range(rows - 1)])
    near_kept, near_result, close = near_forward(*blocks)
    sent, far_kept, far_result = far_forward(place, window, mine, past, close)
    told = exchange(sent, ("x", "zl", "zh"), SAME_HEAD)
    own, back = far_backward(place, mine, past, far_kept, far_result, sent, told)
    back = lax.ppermute(back, "y", [(i + 1, i) for i in range(rows - 1)])
    returned = near_backward(place, blocks, near_kept, near_result, close, told)
    own, returned = lax.optimization_barrier((own, returned))
    returned = all_round(returned, -1)
    own = add_back(own, back)
    far = exchange_alone(own, go).reshape(HALF, 2, ROWS, DH)
    out_own, out_other = unproject(place, returned, far, w_qkv, w_out)
    mixed, d_tokens = finish(tokens, cot, gain, out_own, swap(out_other))
    return mixed.reshape(1, 1, HW, D), d_tokens.reshape(1, 1, HW, D)


def solution(mesh):
    grid = Mesh(mesh.devices.reshape(4, 4, 2, 4, 2), ("y", "x", "zl", "zh", "core"))
    frames, cams = ("y", "x", "zl"), ("zh", "core")
    split = P(frames, cams, None, None)
    return jax.shard_map(
        per_device,
        mesh=grid,
        in_specs=(split, P(), P(), P(), P(), P(frames), split),
        out_specs=(split, split),
        check_vma=False,
    )
```

```python
import math

import jax
import jax.numpy as jnp
from jax import lax
from jax.experimental import pallas as pl
from jax.experimental.pallas import tpu as pltpu
from jax.sharding import Mesh
from jax.sharding import PartitionSpec as P

D = 1024
H = 8
DH = 128
HW = 128
WIN = 8
EPS = 1e-05

HALF = H // 2
PAIR = 2 * HW
GROUP = 8
SCALE = DH ** (-0.5)
SCALE2 = SCALE * math.log2(math.e)
FLOOR = -3.0e38
F32 = jnp.float32
BF16 = jnp.bfloat16
NT = (((1,), (1,)), ((), ()))
VMEM_LIMIT = 20 * 1024 * 1024
STAGE_LIMIT = 48 * 1024 * 1024

Q0, G0, K0, V0, OK0, ROWS = 0, 128, 256, 384, 512, 528
TOKENS = 8 * HW
KEYS = (WIN + 1) * HW


def params(**kw):
    return pltpu.CompilerParams(vmem_limit_bytes=VMEM_LIMIT, **kw)


def mm(a, b):
    return jnp.dot(a, b, preferred_element_type=F32)


def mm_nt(a, b):
    return lax.dot_general(a, b, NT, preferred_element_type=F32)


def turn(a):
    return a.astype(F32).T


VM = pl.BlockSpec(memory_space=pltpu.VMEM)
SM = pl.BlockSpec(memory_space=pltpu.SMEM)
ANY = pl.BlockSpec(memory_space=pltpu.HBM)


def cost(flops, size, exps=0):
    return pl.CostEstimate(flops=flops, bytes_accessed=size, transcendentals=exps)


PIECES = 4


def weight_copies(place, w_qkv, w_out, parts, out, sems):
    begin = pl.multiple_of(place[0] * HALF * DH, HALF * DH)
    groups = []
    for part in range(3):
        columns = pl.ds(pl.multiple_of(begin + part * D, HALF * DH), HALF * DH)
        size = D // PIECES
        groups.append(
            [
                pltpu.make_async_copy(
                    w_qkv.at[pl.ds(n * size, size), columns],
                    parts[part].at[pl.ds(n * size, size), :],
                    sems.at[part * PIECES + n],
                )
                for n in range(PIECES)
            ]
        )
    size = HALF * DH // PIECES
    groups.append(
        [
            pltpu.make_async_copy(
                w_out.at[pl.ds(pl.multiple_of(begin + n * size, size), size), :],
                out.at[pl.ds(n * size, size), :],
                sems.at[3 * PIECES + n],
            )
            for n in range(PIECES)
        ]
    )
    return groups


def start_all(groups):
    for group in groups:
        for copy in group:
            copy.start()


def wait_all(group):
    for copy in group:
        copy.wait()


def stage_kernel(place, w_qkv, w_out, wq, wk, wv, out, sems):
    groups = weight_copies(place, w_qkv, w_out, (wq, wk, wv), out, sems)
    start_all(groups)
    for group in groups:
        wait_all(group)


def stage(place, w_qkv, w_out):
    return pl.pallas_call(
        stage_kernel,
        in_specs=[SM] + [ANY] * 2,
        out_specs=[VM] * 4,
        out_shape=[jax.ShapeDtypeStruct((D, HALF * DH), BF16)] * 3
        + [jax.ShapeDtypeStruct((HALF * DH, D), BF16)],
        scratch_shapes=[pltpu.SemaphoreType.DMA((4 * PIECES,))],
        compiler_params=pltpu.CompilerParams(vmem_limit_bytes=STAGE_LIMIT),
        cost_estimate=cost(0, 9_000_000),
        name="stage",
    )(place, w_qkv, w_out)


STEPS = (0, 2, 1, 3)


def slot_of_head(place, h):
    return lax.rem(h + HALF - place[2], HALF)


def head_here(place, step=0):
    return lax.rem(place[1] + place[2] + step, HALF)


def project_kernel(
    place, valid, own, other, cot_own, cot_other, gain, wq, wk, wv, wo, packed, near0, near1, near2, near3
):
    x = jnp.concatenate([own[...], other[...]], axis=0).astype(F32)
    rinv = lax.rsqrt(jnp.mean(x * x, axis=-1, keepdims=True) + EPS)
    normed = (x * rinv * gain[...]).astype(BF16)
    cot = jnp.concatenate([cot_own[...], cot_other[...]], axis=0)
    flags = jnp.full((ROWS - OK0, DH), valid[0], jnp.int32).astype(F32).astype(BF16)
    for row in (Q0, K0, V0, G0):
        if row == G0:
            got = mm_nt(cot, wo[...]).astype(BF16)
        else:
            got = mm(normed, {Q0: wq, K0: wk, V0: wv}[row][...]).astype(BF16)
        for h in range(HALF):
            for s in range(2):
                packed[slot_of_head(place, h), s, row : row + HW, :] = (
                    got[s * HW : (s + 1) * HW, h * DH : (h + 1) * DH]
                )
    for h in range(HALF):
        for s in range(2):
            packed[h, s, OK0:ROWS, :] = flags
    for step, near in zip(STEPS, (near0, near1, near2, near3)):
        slot = lax.rem(place[1] + step, HALF)
        for s in range(2):
            near[s] = packed[slot, s, :OK0, :]


def project(place, valid, own, other, cot_own, cot_other, gain, weights):
    return pl.pallas_call(
        project_kernel,
        in_specs=[SM, SM] + [VM] * 9,
        out_specs=[VM] * 5,
        out_shape=[jax.ShapeDtypeStruct((HALF, 2, ROWS, DH), BF16)]
        + [jax.ShapeDtypeStruct((2, OK0, DH), BF16)] * 4,
        compiler_params=params(),
        cost_estimate=cost(2 * PAIR * D * 4 * HALF * DH, 7_000_000),
        name="project",
    )(place, valid, own, other, cot_own, cot_other, gain, *weights)


def both(block, row):
    return jnp.concatenate([block[0, row : row + HW, :], block[1, row : row + HW, :]], axis=0)


def near_forward_kernel(near0, near1, near2, near3, kept, result, stats, scores):
    blocks = (near0, near1, near2, near3)
    turned = [turn(both(block, V0)).astype(BF16) for block in blocks]
    for g in range(4):
        cols = slice(g * PAIR, (g + 1) * PAIR)
        query = both(blocks[g], Q0)
        grad_t = turn(both(blocks[g], G0))
        peak = jnp.full((1, PAIR), -jnp.inf, F32)
        for z in range(4):
            block = mm_nt(both(blocks[z], K0), query)
            scores[z * PAIR : (z + 1) * PAIR, :] = block
            peak = jnp.maximum(peak, jnp.max(block, axis=0, keepdims=True))
        peak = peak * SCALE2
        total = jnp.zeros((1, PAIR), F32)
        for b in range(8):
            rows = slice(b * HW, (b + 1) * HW)
            block = jnp.exp2(scores[rows, :] * SCALE2 - peak)
            total = total + jnp.sum(block, axis=0, keepdims=True)
            kept[rows, cols] = block.astype(BF16)
        got = jnp.zeros((DH, PAIR), F32)
        for z in range(4):
            got = got + mm(turned[z], kept[z * PAIR : (z + 1) * PAIR, cols])
        result[:, cols] = got
        delta = jnp.sum(got * grad_t, axis=0, keepdims=True)
        told = jnp.concatenate([peak, total, delta, jnp.zeros((1, PAIR), F32)], axis=0)
        stats[2 * g] = told[:, :HW]
        stats[2 * g + 1] = told[:, HW:]


def near_forward(*blocks):
    return pl.pallas_call(
        near_forward_kernel,
        in_specs=[VM] * 4,
        out_specs=[VM] * 3,
        out_shape=[
            jax.ShapeDtypeStruct((TOKENS, TOKENS), BF16),
            jax.ShapeDtypeStruct((DH, TOKENS), F32),
            jax.ShapeDtypeStruct((8, 4, HW), F32),
        ],
        scratch_shapes=[pltpu.VMEM((TOKENS, PAIR), F32)],
        compiler_params=params(),
        cost_estimate=cost(80 * TOKENS * TOKENS * DH, 4_000_000, TOKENS * TOKENS),
        name="near_forward",
    )(*blocks)


def slot_of_near(place, step, s):
    return lax.rem(place[1] + step, 4) * 2 + s


def far_forward_kernel(place, win, mine, past, close, told, kept, result, keys, values_t, scores):
    width = win[place[0] * HALF + head_here(place)]
    for g in range(4):
        for s in range(2):
            told[slot_of_near(place, STEPS[g], s), 0:4, :] = close[2 * g + s]
    for j in range(GROUP):
        keys[j * HW : (j + 1) * HW, :] = past[j, :HW, :]
        keys[(GROUP + j) * HW : (GROUP + j + 1) * HW, :] = mine[j, K0 : K0 + HW, :]
        values_t[:, j * HW : (j + 1) * HW] = turn(past[j, HW : 2 * HW, :]).astype(BF16)
        values_t[:, (GROUP + j) * HW : (GROUP + j + 1) * HW] = turn(
            mine[j, V0 : V0 + HW, :]
        ).astype(BF16)
    for p in range(GROUP // 2):
        query = jnp.concatenate([mine[2 * p, :HW, :], mine[2 * p + 1, :HW, :]], axis=0)
        grad_t = jnp.concatenate(
            [turn(mine[2 * p, G0 : G0 + HW, :]), turn(mine[2 * p + 1, G0 : G0 + HW, :])], axis=1
        )
        peak = jnp.full((1, PAIR), -jnp.inf, F32)
        for b in range(WIN + 1):
            j = 2 * p + b
            if j < GROUP:
                flag = past[j, 2 * HW : 2 * HW + 1, :].astype(F32)
            else:
                flag = mine[j - GROUP, OK0 : OK0 + 1, :].astype(F32)
            lower = jnp.where((flag > 0.5) & (b >= WIN - width) & (b < WIN), 0.0, -jnp.inf)
            upper = jnp.where((flag > 0.5) & (b >= WIN + 1 - width), 0.0, -jnp.inf)
            bias = jnp.concatenate([lower, upper], axis=1)
            block = mm_nt(keys[j * HW : (j + 1) * HW, :], query) + bias
            scores[b * HW : (b + 1) * HW, :] = block
            peak = jnp.maximum(peak, jnp.max(block, axis=0, keepdims=True))
        peak = jnp.maximum(peak * SCALE2, FLOOR)
        total = jnp.zeros((1, PAIR), F32)
        for b in range(WIN + 1):
            block = jnp.exp2(scores[b * HW : (b + 1) * HW, :] * SCALE2 - peak)
            total = total + jnp.sum(block, axis=0, keepdims=True)
            kept[p, b * HW : (b + 1) * HW, :] = block.astype(BF16)
        got = mm(values_t[:, p * PAIR : p * PAIR + KEYS], kept[p])
        result[:, p * PAIR : (p + 1) * PAIR] = got
        delta = jnp.sum(got * grad_t, axis=0, keepdims=True)
        stats = jnp.concatenate([peak, total, delta, jnp.zeros((1, PAIR), F32)], axis=0)
        told[2 * p, 4:8, :] = stats[:, :HW]
        told[2 * p + 1, 4:8, :] = stats[:, HW:]


def far_forward(place, window, mine, past, close):
    return pl.pallas_call(
        far_forward_kernel,
        in_specs=[SM, SM, VM, VM, VM],
        out_specs=[VM] * 3,
        out_shape=[
            jax.ShapeDtypeStruct((GROUP, 8, HW), F32),
            jax.ShapeDtypeStruct((GROUP // 2, KEYS, PAIR), BF16),
            jax.ShapeDtypeStruct((DH, GROUP * HW), F32),
        ],
        scratch_shapes=[
            pltpu.VMEM((2 * GROUP * HW, DH), BF16),
            pltpu.VMEM((DH, 2 * GROUP * HW), BF16),
            pltpu.VMEM((KEYS, PAIR), F32),
        ],
        compiler_params=params(),
        cost_estimate=cost(16 * KEYS * PAIR * DH, 5_000_000, 4 * KEYS * PAIR),
        name="far_forward",
    )(place, window, mine, past, close)


def merge(this, other):
    top = jnp.maximum(this[0:1], other[0:1])
    here = jnp.exp2(this[0:1] - top)
    there = jnp.exp2(other[0:1] - top)
    inverse = 1.0 / (here * this[1:2] + there * other[1:2])
    here = here * inverse
    delta = here * this[2:3] + there * inverse * other[2:3]
    return here, here * delta


def near_backward_kernel(
    place, near0, near1, near2, near3, kept, result, stats, told,
    back0, back1, back2, back3, grads, grad_all, query_all,
):
    blocks = (near0, near1, near2, near3)
    outs = (back0, back1, back2, back3)
    for g in range(4):
        cols = slice(g * PAIR, (g + 1) * PAIR)
        this = jnp.concatenate([stats[2 * g], stats[2 * g + 1]], axis=1)
        other = jnp.concatenate(
            [told[slot_of_near(place, STEPS[g], s), 4:8, :] for s in range(2)], axis=1
        )
        weight, delta = merge(this, other)
        grad_t = (turn(both(blocks[g], G0)) * weight).astype(BF16)
        grad_all[:, cols] = grad_t
        query_all[cols, :] = both(blocks[g], Q0)
        attended = (result[:, cols] * weight).T.astype(BF16)
        for s in range(2):
            outs[g][s, :HW, :] = attended[s * HW : (s + 1) * HW]
        for z in range(4):
            rows = slice(z * PAIR, (z + 1) * PAIR)
            d_probs = mm(both(blocks[z], V0), grad_t)
            grads[rows, cols] = (kept[rows, cols].astype(F32) * (d_probs - delta)).astype(BF16)
    for z in range(4):
        rows = slice(z * PAIR, (z + 1) * PAIR)
        d_values = mm_nt(kept[rows, :], grad_all[...]).astype(BF16)
        d_keys = (mm(grads[rows, :], query_all[...]) * SCALE).astype(BF16)
        for s in range(2):
            outs[z][s, 2 * HW : 3 * HW, :] = d_keys[s * HW : (s + 1) * HW]
            outs[z][s, 3 * HW :, :] = d_values[s * HW : (s + 1) * HW]
    keys_t = jnp.concatenate([turn(both(block, K0)).astype(BF16) for block in blocks], axis=1)
    for g in range(4):
        cols = slice(g * PAIR, (g + 1) * PAIR)
        d_query = (mm(keys_t, grads[:, cols]) * SCALE).T.astype(BF16)
        for s in range(2):
            outs[g][s, HW : 2 * HW, :] = d_query[s * HW : (s + 1) * HW]


def near_backward(place, blocks, kept, result, stats, told):
    return pl.pallas_call(
        near_backward_kernel,
        in_specs=[SM] + [VM] * 8,
        out_specs=[VM] * 4,
        out_shape=[jax.ShapeDtypeStruct((2, 4 * HW, DH), BF16)] * 4,
        scratch_shapes=[
            pltpu.VMEM((TOKENS, TOKENS), BF16),
            pltpu.VMEM((DH, TOKENS), BF16),
            pltpu.VMEM((TOKENS, DH), BF16),
        ],
        compiler_params=params(),
        cost_estimate=cost(8 * TOKENS * TOKENS * DH, 5_000_000),
        name="near_backward",
    )(place, *blocks, kept, result, stats, told)


def far_backward_kernel(
    place, mine, past, kept, result, sent, told, own, back0, back1, keys_t, values, dk, dv, grads
):
    for j in range(GROUP):
        keys_t[:, j * HW : (j + 1) * HW] = turn(past[j, :HW, :]).astype(BF16)
        keys_t[:, (GROUP + j) * HW : (GROUP + j + 1) * HW] = turn(
            mine[j, K0 : K0 + HW, :]
        ).astype(BF16)
        values[j * HW : (j + 1) * HW, :] = past[j, HW : 2 * HW, :]
        values[(GROUP + j) * HW : (GROUP + j + 1) * HW, :] = mine[j, V0 : V0 + HW, :]
    dk[...] = jnp.zeros_like(dk)
    dv[...] = jnp.zeros_like(dv)
    for p in range(GROUP // 2):
        query = jnp.concatenate([mine[2 * p, :HW, :], mine[2 * p + 1, :HW, :]], axis=0)
        grad_t = jnp.concatenate(
            [turn(mine[2 * p, G0 : G0 + HW, :]), turn(mine[2 * p + 1, G0 : G0 + HW, :])], axis=1
        )
        this = jnp.concatenate([sent[2 * p, 4:8, :], sent[2 * p + 1, 4:8, :]], axis=1)
        other = jnp.concatenate([told[2 * p, 0:4, :], told[2 * p + 1, 0:4, :]], axis=1)
        weight, delta = merge(this, other)
        grad_t = (grad_t * weight).astype(BF16)
        at = p * PAIR
        attended = (result[:, at : at + PAIR] * weight).T.astype(BF16)
        for lo, size in ((0, 384), (384, 384), (768, 384)):
            rows = slice(lo, lo + size)
            spot = slice(at + lo, at + lo + size)
            d_probs = mm(values[spot, :], grad_t)
            block = kept[p, rows, :]
            d_scores = (block.astype(F32) * (d_probs - delta)).astype(BF16)
            grads[rows, :] = d_scores
            dv[spot, :] += mm_nt(block, grad_t)
            dk[spot, :] += mm(d_scores, query)
        d_query = (mm(keys_t[:, at : at + KEYS], grads[...]) * SCALE).T.astype(BF16)
        for i in range(2):
            own[2 * p + i, :HW, :] = attended[i * HW : (i + 1) * HW]
            own[2 * p + i, HW : 2 * HW, :] = d_query[i * HW : (i + 1) * HW]
    for j in range(GROUP):
        early = slice(j * HW, (j + 1) * HW)
        late = slice((GROUP + j) * HW, (GROUP + j + 1) * HW)
        d_keys = (dk[early, :] * SCALE).astype(BF16)
        d_values = dv[early, :].astype(BF16)
        back0[j] = d_keys
        back1[j] = d_values
        own[j, 2 * HW : 3 * HW, :] = (dk[late, :] * SCALE).astype(BF16)
        own[j, 3 * HW : 4 * HW, :] = dv[late, :].astype(BF16)
        own[j, 4 * HW :, :] = jnp.zeros((ROWS - 4 * HW, DH), BF16)


def far_backward(place, mine, past, kept, result, sent, told):
    return pl.pallas_call(
        far_backward_kernel,
        in_specs=[SM] + [VM] * 6,
        out_specs=[VM] * 3,
        out_shape=[jax.ShapeDtypeStruct((GROUP, ROWS, DH), BF16)]
        + [jax.ShapeDtypeStruct((GROUP, HW, DH), BF16)] * 2,
        scratch_shapes=[
            pltpu.VMEM((DH, 2 * GROUP * HW), BF16),
            pltpu.VMEM((2 * GROUP * HW, DH), BF16),
            pltpu.VMEM((2 * GROUP * HW, DH), F32),
            pltpu.VMEM((2 * GROUP * HW, DH), F32),
            pltpu.VMEM((KEYS, PAIR), BF16),
        ],
        compiler_params=params(),
        cost_estimate=cost(32 * KEYS * PAIR * DH, 6_000_000),
        name="far_backward",
    )(place, mine, past, kept, result, sent, told)


def add_back_kernel(own, back0, back1, out):
    for n, back in enumerate((back0, back1)):
        rows = slice((2 + n) * HW, (3 + n) * HW)
        for j in range(GROUP):
            out[j, rows, :] = (own[j, rows, :].astype(F32) + back[j].astype(F32)).astype(BF16)


def add_back(own, *back):
    return pl.pallas_call(
        add_back_kernel,
        in_specs=[VM] * 3,
        out_specs=VM,
        out_shape=jax.ShapeDtypeStruct((GROUP, ROWS, DH), BF16),
        input_output_aliases={0: 0},
        compiler_params=params(),
        cost_estimate=cost(GROUP * 2 * HW * DH, 2_500_000),
        name="add_back",
    )(own, *back)


def unproject_kernel(
    place, near0, near1, near2, near3, far, w_qkv, w_out, own, other, close, wq, wk, wv, wo, sems
):
    groups = weight_copies(place, w_qkv, w_out, (wq, wk, wv), wo, sems)
    start_all(groups)
    for step, near in zip(STEPS, (near0, near1, near2, near3)):
        close[head_here(place, step)] = near[...]
    parts = []
    for part in range(4):
        rows = slice(part * HW, (part + 1) * HW)
        pieces = []
        for h in range(HALF):
            slot = slot_of_head(place, h)
            away = jnp.concatenate([far[slot, 0, rows, :], far[slot, 1, rows, :]], axis=0)
            here = jnp.concatenate([close[h, 0, rows, :], close[h, 1, rows, :]], axis=0)
            pieces.append((away.astype(F32) + here.astype(F32)).astype(BF16))
        parts.append(jnp.concatenate(pieces, axis=1))
    wait_all(groups[0])
    total = mm_nt(parts[1], wq[...])
    wait_all(groups[1])
    total = total + mm_nt(parts[2], wk[...])
    wait_all(groups[2])
    total = total + mm_nt(parts[3], wv[...])
    wait_all(groups[3])
    mixed = mm(parts[0], wo[...])
    own[0] = mixed[:HW]
    own[1] = total[:HW]
    other[0] = mixed[HW:].astype(BF16)
    other[1] = total[HW:].astype(BF16)


def unproject(place, blocks, far, w_qkv, w_out):
    return pl.pallas_call(
        unproject_kernel,
        in_specs=[SM] + [VM] * 5 + [ANY] * 2,
        out_specs=[VM, VM],
        scratch_shapes=[pltpu.VMEM((HALF, 2, 4 * HW, DH), BF16)]
        + [pltpu.VMEM((D, HALF * DH), BF16)] * 3
        + [pltpu.VMEM((HALF * DH, D), BF16), pltpu.SemaphoreType.DMA((4 * PIECES,))],
        out_shape=[jax.ShapeDtypeStruct((2, HW, D), F32), jax.ShapeDtypeStruct((2, HW, D), BF16)],
        compiler_params=pltpu.CompilerParams(vmem_limit_bytes=50 * 1024 * 1024),
        cost_estimate=cost(2 * PAIR * D * 4 * HALF * DH, 8_000_000),
        name="unproject",
    )(place, *blocks, far, w_qkv, w_out)


def finish_kernel(tokens, cot, gain, own, other, mixed, out):
    x = tokens[...].astype(F32)
    mixed[...] = (x + (own[0] + other[0].astype(F32))).astype(BF16)
    rinv = lax.rsqrt(jnp.mean(x * x, axis=-1, keepdims=True) + EPS)
    scaled = (own[1] + other[1].astype(F32)) * gain[...]
    mean = jnp.mean(scaled * x, axis=-1, keepdims=True)
    grad = rinv * scaled - x * (rinv * rinv * rinv * mean)
    out[...] = (cot[...].astype(F32) + grad).astype(BF16)


def finish(tokens, cot, gain, own, other):
    return pl.pallas_call(
        finish_kernel,
        in_specs=[VM] * 5,
        out_specs=[VM] * 2,
        out_shape=[jax.ShapeDtypeStruct((HW, D), BF16)] * 2,
        compiler_params=params(),
        cost_estimate=cost(HW * D * 10, 3_000_000),
        name="finish",
    )(tokens, cot, gain, own, other)


LANE = ("x", "zl")
SAME_HEAD = [
    [(x * 2 + zl) * 4 + (h + 4 - x) % 4 for x in range(4) for zl in range(2)] for h in range(4)
]


def swap(value):
    return lax.ppermute(value, "core", [(0, 1), (1, 0)])


def turn_ring(value, steps):
    return lax.ppermute(value, "zh", [(i, (i + steps) % 4) for i in range(4)])


def all_round(blocks, sign):
    return [blocks[0]] + [turn_ring(blocks[g], sign * STEPS[g]) for g in (1, 2, 3)]


def exchange(value, axes, groups=None):
    return lax.all_to_all(value, axes, 0, 0, axis_index_groups=groups, tiled=True)


def exchange_alone(value, go):
    return lax.cond(go, lambda v: exchange(v, LANE), jnp.zeros_like, value)


def per_device(tokens, gain, w_qkv, w_out, window, valid, cotangent):
    rows = lax.axis_size("y")
    place = jnp.stack(
        [lax.axis_index(axis) for axis in ("core", "x", "zh")]
    ).astype(jnp.int32)
    go = window[0] > 0
    tokens = tokens.reshape(HW, D)
    cot = cotangent.reshape(HW, D)
    other_tokens = swap(tokens)
    other_cot = swap(cot)
    gain = gain.reshape(1, D)
    weights = stage(place, w_qkv, w_out)
    packed, *blocks = project(
        place, valid, tokens, other_tokens, cot, other_cot, gain, weights
    )
    blocks = all_round(blocks, 1)
    mine = exchange(packed.reshape(2 * HALF, ROWS, DH), LANE)
    past = lax.ppermute(mine[:, K0:, :], "y", [(i, i + 1) for i in range(rows - 1)])
    near_kept, near_result, close = near_forward(*blocks)
    sent, far_kept, far_result = far_forward(place, window, mine, past, close)
    told = exchange(sent, ("x", "zl", "zh"), SAME_HEAD)
    returned = near_backward(place, blocks, near_kept, near_result, close, told)
    told, returned = lax.optimization_barrier((told, returned))
    own, *back = far_backward(place, mine, past, far_kept, far_result, sent, told)
    back = [lax.ppermute(b, "y", [(i + 1, i) for i in range(rows - 1)]) for b in back]
    returned = all_round(returned, -1)
    own, returned = lax.optimization_barrier((own, returned))
    own = add_back(own, *back)
    far = exchange_alone(own, go).reshape(HALF, 2, ROWS, DH)
    out_own, out_other = unproject(place, returned, far, w_qkv, w_out)
    mixed, d_tokens = finish(tokens, cot, gain, out_own, swap(out_other))
    return mixed.reshape(1, 1, HW, D), d_tokens.reshape(1, 1, HW, D)


def solution(mesh):
    grid = Mesh(mesh.devices.reshape(4, 4, 2, 4, 2), ("y", "x", "zl", "zh", "core"))
    frames, cams = ("y", "x", "zl"), ("zh", "core")
    split = P(frames, cams, None, None)
    return jax.shard_map(
        per_device,
        mesh=grid,
        in_specs=(split, P(), P(), P(), P(), P(frames), split),
        out_specs=(split, split),
        check_vma=False,
    )
```

```python
import math

import jax
import jax.numpy as jnp
from jax import lax
from jax.experimental import pallas as pl
from jax.experimental.pallas import tpu as pltpu
from jax.sharding import Mesh
from jax.sharding import PartitionSpec as P

D = 1024
H = 8
DH = 128
HW = 128
WIN = 8
EPS = 1e-05

HALF = H // 2
PAIR = 2 * HW
GROUP = 8
SCALE = DH ** (-0.5)
SCALE2 = SCALE * math.log2(math.e)
FLOOR = -3.0e38
F32 = jnp.float32
BF16 = jnp.bfloat16
NT = (((1,), (1,)), ((), ()))
VMEM_LIMIT = 20 * 1024 * 1024
STAGE_LIMIT = 48 * 1024 * 1024
LAST_LIMIT = 46 * 1024 * 1024

Q0, G0, K0, V0, OK0, ROWS = 0, 128, 256, 384, 512, 528
TOKENS = 8 * HW
KEYS = (WIN + 1) * HW


def params(**kw):
    return pltpu.CompilerParams(vmem_limit_bytes=VMEM_LIMIT, **kw)


def mm(a, b):
    return jnp.dot(a, b, preferred_element_type=F32)


def mm_nt(a, b):
    return lax.dot_general(a, b, NT, preferred_element_type=F32)


def turn(a):
    return a.astype(F32).T


VM = pl.BlockSpec(memory_space=pltpu.VMEM)
SM = pl.BlockSpec(memory_space=pltpu.SMEM)
ANY = pl.BlockSpec(memory_space=pltpu.HBM)


def cost(flops, size, exps=0):
    return pl.CostEstimate(flops=flops, bytes_accessed=size, transcendentals=exps)


PIECES = 4


def weight_copies(place, w_qkv, w_out, parts, out, sems):
    begin = pl.multiple_of(place[0] * HALF * DH, HALF * DH)
    groups = []
    for part in range(3):
        columns = pl.ds(pl.multiple_of(begin + part * D, HALF * DH), HALF * DH)
        size = D // PIECES
        groups.append(
            [
                pltpu.make_async_copy(
                    w_qkv.at[pl.ds(n * size, size), columns],
                    parts[part].at[pl.ds(n * size, size), :],
                    sems.at[part * PIECES + n],
                )
                for n in range(PIECES)
            ]
        )
    size = HALF * DH // PIECES
    groups.append(
        [
            pltpu.make_async_copy(
                w_out.at[pl.ds(pl.multiple_of(begin + n * size, size), size), :],
                out.at[pl.ds(n * size, size), :],
                sems.at[3 * PIECES + n],
            )
            for n in range(PIECES)
        ]
    )
    return groups


def start_all(groups):
    for group in groups:
        for copy in group:
            copy.start()


def wait_all(group):
    for copy in group:
        copy.wait()


def stage_kernel(place, w_qkv, w_out, wq, wk, wv, out, sems):
    groups = weight_copies(place, w_qkv, w_out, (wq, wk, wv), out, sems)
    start_all(groups)
    for group in groups:
        wait_all(group)


def stage(place, w_qkv, w_out):
    return pl.pallas_call(
        stage_kernel,
        in_specs=[SM] + [ANY] * 2,
        out_specs=[VM] * 4,
        out_shape=[jax.ShapeDtypeStruct((D, HALF * DH), BF16)] * 3
        + [jax.ShapeDtypeStruct((HALF * DH, D), BF16)],
        scratch_shapes=[pltpu.SemaphoreType.DMA((4 * PIECES,))],
        compiler_params=pltpu.CompilerParams(vmem_limit_bytes=STAGE_LIMIT),
        cost_estimate=cost(0, 9_000_000),
        name="stage",
    )(place, w_qkv, w_out)


STEPS = (0, 2, 1, 3)


def slot_of_head(place, h):
    return lax.rem(h + HALF - place[2], HALF)


def head_here(place, step=0):
    return lax.rem(place[1] + place[2] + step, HALF)


def project_kernel(
    place, valid, own, other, cot_own, cot_other, gain, wq, wk, wv, wo, packed, near0, near1, near2, near3
):
    x = jnp.concatenate([own[...], other[...]], axis=0).astype(F32)
    rinv = lax.rsqrt(jnp.mean(x * x, axis=-1, keepdims=True) + EPS)
    normed = (x * rinv * gain[...]).astype(BF16)
    cot = jnp.concatenate([cot_own[...], cot_other[...]], axis=0)
    flags = jnp.full((ROWS - OK0, DH), valid[0], jnp.int32).astype(F32).astype(BF16)
    for row in (Q0, K0, V0, G0):
        if row == G0:
            got = mm_nt(cot, wo[...]).astype(BF16)
        else:
            got = mm(normed, {Q0: wq, K0: wk, V0: wv}[row][...]).astype(BF16)
        for h in range(HALF):
            for s in range(2):
                packed[slot_of_head(place, h), s, row : row + HW, :] = (
                    got[s * HW : (s + 1) * HW, h * DH : (h + 1) * DH]
                )
    for h in range(HALF):
        for s in range(2):
            packed[h, s, OK0:ROWS, :] = flags
    for step, near in zip(STEPS, (near0, near1, near2, near3)):
        slot = lax.rem(place[1] + step, HALF)
        for s in range(2):
            near[s] = packed[slot, s, :OK0, :]


def project(place, valid, own, other, cot_own, cot_other, gain, weights):
    return pl.pallas_call(
        project_kernel,
        in_specs=[SM, SM] + [VM] * 9,
        out_specs=[VM] * 5,
        out_shape=[jax.ShapeDtypeStruct((HALF, 2, ROWS, DH), BF16)]
        + [jax.ShapeDtypeStruct((2, OK0, DH), BF16)] * 4,
        compiler_params=params(),
        cost_estimate=cost(2 * PAIR * D * 4 * HALF * DH, 7_000_000),
        name="project",
    )(place, valid, own, other, cot_own, cot_other, gain, *weights)


def both(block, row):
    return jnp.concatenate([block[0, row : row + HW, :], block[1, row : row + HW, :]], axis=0)


def near_forward_kernel(near0, near1, near2, near3, kept, result, stats, scores):
    blocks = (near0, near1, near2, near3)
    turned = [turn(both(block, V0)).astype(BF16) for block in blocks]
    for g in range(4):
        cols = slice(g * PAIR, (g + 1) * PAIR)
        query = both(blocks[g], Q0)
        grad_t = turn(both(blocks[g], G0))
        peak = jnp.full((1, PAIR), -jnp.inf, F32)
        for z in range(4):
            block = mm_nt(both(blocks[z], K0), query)
            scores[z * PAIR : (z + 1) * PAIR, :] = block
            peak = jnp.maximum(peak, jnp.max(block, axis=0, keepdims=True))
        peak = peak * SCALE2
        total = jnp.zeros((1, PAIR), F32)
        for b in range(8):
            rows = slice(b * HW, (b + 1) * HW)
            block = jnp.exp2(scores[rows, :] * SCALE2 - peak)
            total = total + jnp.sum(block, axis=0, keepdims=True)
            kept[rows, cols] = block.astype(BF16)
        got = jnp.zeros((DH, PAIR), F32)
        for z in range(4):
            got = got + mm(turned[z], kept[z * PAIR : (z + 1) * PAIR, cols])
        result[:, cols] = got
        delta = jnp.sum(got * grad_t, axis=0, keepdims=True)
        told = jnp.concatenate([peak, total, delta, jnp.zeros((1, PAIR), F32)], axis=0)
        stats[2 * g] = told[:, :HW]
        stats[2 * g + 1] = told[:, HW:]


def near_forward(*blocks):
    return pl.pallas_call(
        near_forward_kernel,
        in_specs=[VM] * 4,
        out_specs=[VM] * 3,
        out_shape=[
            jax.ShapeDtypeStruct((TOKENS, TOKENS), BF16),
            jax.ShapeDtypeStruct((DH, TOKENS), F32),
            jax.ShapeDtypeStruct((8, 4, HW), F32),
        ],
        scratch_shapes=[pltpu.VMEM((TOKENS, PAIR), F32)],
        compiler_params=params(),
        cost_estimate=cost(80 * TOKENS * TOKENS * DH, 4_000_000, TOKENS * TOKENS),
        name="near_forward",
    )(*blocks)


def slot_of_near(place, step, s):
    return lax.rem(place[1] + step, 4) * 2 + s


def far_forward_kernel(place, win, mine, past, close, told, kept, result, keys, values_t, scores):
    width = win[place[0] * HALF + head_here(place)]
    for g in range(4):
        for s in range(2):
            told[slot_of_near(place, STEPS[g], s), 0:4, :] = close[2 * g + s]
    for j in range(GROUP):
        keys[j * HW : (j + 1) * HW, :] = past[j, :HW, :]
        keys[(GROUP + j) * HW : (GROUP + j + 1) * HW, :] = mine[j, K0 : K0 + HW, :]
        values_t[:, j * HW : (j + 1) * HW] = turn(past[j, HW : 2 * HW, :]).astype(BF16)
        values_t[:, (GROUP + j) * HW : (GROUP + j + 1) * HW] = turn(
            mine[j, V0 : V0 + HW, :]
        ).astype(BF16)
    for p in range(GROUP // 2):
        query = jnp.concatenate([mine[2 * p, :HW, :], mine[2 * p + 1, :HW, :]], axis=0)
        grad_t = jnp.concatenate(
            [turn(mine[2 * p, G0 : G0 + HW, :]), turn(mine[2 * p + 1, G0 : G0 + HW, :])], axis=1
        )
        peak = jnp.full((1, PAIR), -jnp.inf, F32)
        for b in range(WIN + 1):
            j = 2 * p + b
            if j < GROUP:
                flag = past[j, 2 * HW : 2 * HW + 1, :].astype(F32)
            else:
                flag = mine[j - GROUP, OK0 : OK0 + 1, :].astype(F32)
            lower = jnp.where((flag > 0.5) & (b >= WIN - width) & (b < WIN), 0.0, -jnp.inf)
            upper = jnp.where((flag > 0.5) & (b >= WIN + 1 - width), 0.0, -jnp.inf)
            bias = jnp.concatenate([lower, upper], axis=1)
            block = mm_nt(keys[j * HW : (j + 1) * HW, :], query) + bias
            scores[b * HW : (b + 1) * HW, :] = block
            peak = jnp.maximum(peak, jnp.max(block, axis=0, keepdims=True))
        peak = jnp.maximum(peak * SCALE2, FLOOR)
        total = jnp.zeros((1, PAIR), F32)
        for b in range(WIN + 1):
            block = jnp.exp2(scores[b * HW : (b + 1) * HW, :] * SCALE2 - peak)
            total = total + jnp.sum(block, axis=0, keepdims=True)
            kept[p, b * HW : (b + 1) * HW, :] = block.astype(BF16)
        got = mm(values_t[:, p * PAIR : p * PAIR + KEYS], kept[p])
        result[:, p * PAIR : (p + 1) * PAIR] = got
        delta = jnp.sum(got * grad_t, axis=0, keepdims=True)
        stats = jnp.concatenate([peak, total, delta, jnp.zeros((1, PAIR), F32)], axis=0)
        told[2 * p, 4:8, :] = stats[:, :HW]
        told[2 * p + 1, 4:8, :] = stats[:, HW:]


def far_forward(place, window, mine, past, close):
    return pl.pallas_call(
        far_forward_kernel,
        in_specs=[SM, SM, VM, VM, VM],
        out_specs=[VM] * 3,
        out_shape=[
            jax.ShapeDtypeStruct((GROUP, 8, HW), F32),
            jax.ShapeDtypeStruct((GROUP // 2, KEYS, PAIR), BF16),
            jax.ShapeDtypeStruct((DH, GROUP * HW), F32),
        ],
        scratch_shapes=[
            pltpu.VMEM((2 * GROUP * HW, DH), BF16),
            pltpu.VMEM((DH, 2 * GROUP * HW), BF16),
            pltpu.VMEM((KEYS, PAIR), F32),
        ],
        compiler_params=params(),
        cost_estimate=cost(16 * KEYS * PAIR * DH, 5_000_000, 4 * KEYS * PAIR),
        name="far_forward",
    )(place, window, mine, past, close)


def merge(this, other):
    top = jnp.maximum(this[0:1], other[0:1])
    here = jnp.exp2(this[0:1] - top)
    there = jnp.exp2(other[0:1] - top)
    inverse = 1.0 / (here * this[1:2] + there * other[1:2])
    here = here * inverse
    delta = here * this[2:3] + there * inverse * other[2:3]
    return here, here * delta


def near_backward_kernel(
    place, near0, near1, near2, near3, kept, result, stats, told,
    back0, back1, back2, back3, grads, grad_all, query_all,
):
    blocks = (near0, near1, near2, near3)
    outs = (back0, back1, back2, back3)
    for g in range(4):
        cols = slice(g * PAIR, (g + 1) * PAIR)
        this = jnp.concatenate([stats[2 * g], stats[2 * g + 1]], axis=1)
        other = jnp.concatenate(
            [told[slot_of_near(place, STEPS[g], s), 4:8, :] for s in range(2)], axis=1
        )
        weight, delta = merge(this, other)
        grad_t = (turn(both(blocks[g], G0)) * weight).astype(BF16)
        grad_all[:, cols] = grad_t
        query_all[cols, :] = both(blocks[g], Q0)
        attended = (result[:, cols] * weight).T.astype(BF16)
        for s in range(2):
            outs[g][s, :HW, :] = attended[s * HW : (s + 1) * HW]
        for z in range(4):
            rows = slice(z * PAIR, (z + 1) * PAIR)
            d_probs = mm(both(blocks[z], V0), grad_t)
            grads[rows, cols] = (kept[rows, cols].astype(F32) * (d_probs - delta)).astype(BF16)
    for z in range(4):
        rows = slice(z * PAIR, (z + 1) * PAIR)
        d_values = mm_nt(kept[rows, :], grad_all[...]).astype(BF16)
        d_keys = (mm(grads[rows, :], query_all[...]) * SCALE).astype(BF16)
        for s in range(2):
            outs[z][s, 2 * HW : 3 * HW, :] = d_keys[s * HW : (s + 1) * HW]
            outs[z][s, 3 * HW :, :] = d_values[s * HW : (s + 1) * HW]
    keys_t = jnp.concatenate([turn(both(block, K0)).astype(BF16) for block in blocks], axis=1)
    for g in range(4):
        cols = slice(g * PAIR, (g + 1) * PAIR)
        d_query = (mm(keys_t, grads[:, cols]) * SCALE).T.astype(BF16)
        for s in range(2):
            outs[g][s, HW : 2 * HW, :] = d_query[s * HW : (s + 1) * HW]


def near_backward(place, blocks, kept, result, stats, told):
    return pl.pallas_call(
        near_backward_kernel,
        in_specs=[SM] + [VM] * 8,
        out_specs=[VM] * 4,
        out_shape=[jax.ShapeDtypeStruct((2, 4 * HW, DH), BF16)] * 4,
        scratch_shapes=[
            pltpu.VMEM((TOKENS, TOKENS), BF16),
            pltpu.VMEM((DH, TOKENS), BF16),
            pltpu.VMEM((TOKENS, DH), BF16),
        ],
        compiler_params=params(),
        cost_estimate=cost(8 * TOKENS * TOKENS * DH, 5_000_000),
        name="near_backward",
    )(place, *blocks, kept, result, stats, told)


def far_backward_kernel(
    place, mine, past, kept, result, sent, told, own, back, keys_t, values, dk, dv, grads
):
    for j in range(GROUP):
        keys_t[:, j * HW : (j + 1) * HW] = turn(past[j, :HW, :]).astype(BF16)
        keys_t[:, (GROUP + j) * HW : (GROUP + j + 1) * HW] = turn(
            mine[j, K0 : K0 + HW, :]
        ).astype(BF16)
        values[j * HW : (j + 1) * HW, :] = past[j, HW : 2 * HW, :]
        values[(GROUP + j) * HW : (GROUP + j + 1) * HW, :] = mine[j, V0 : V0 + HW, :]
    dk[...] = jnp.zeros_like(dk)
    dv[...] = jnp.zeros_like(dv)
    for p in range(GROUP // 2):
        query = jnp.concatenate([mine[2 * p, :HW, :], mine[2 * p + 1, :HW, :]], axis=0)
        grad_t = jnp.concatenate(
            [turn(mine[2 * p, G0 : G0 + HW, :]), turn(mine[2 * p + 1, G0 : G0 + HW, :])], axis=1
        )
        this = jnp.concatenate([sent[2 * p, 4:8, :], sent[2 * p + 1, 4:8, :]], axis=1)
        other = jnp.concatenate([told[2 * p, 0:4, :], told[2 * p + 1, 0:4, :]], axis=1)
        weight, delta = merge(this, other)
        grad_t = (grad_t * weight).astype(BF16)
        at = p * PAIR
        attended = (result[:, at : at + PAIR] * weight).T.astype(BF16)
        for lo, size in ((0, 384), (384, 384), (768, 384)):
            rows = slice(lo, lo + size)
            spot = slice(at + lo, at + lo + size)
            d_probs = mm(values[spot, :], grad_t)
            block = kept[p, rows, :]
            d_scores = (block.astype(F32) * (d_probs - delta)).astype(BF16)
            grads[rows, :] = d_scores
            dv[spot, :] += mm_nt(block, grad_t)
            dk[spot, :] += mm(d_scores, query)
        d_query = (mm(keys_t[:, at : at + KEYS], grads[...]) * SCALE).T.astype(BF16)
        for i in range(2):
            own[2 * p + i, :HW, :] = attended[i * HW : (i + 1) * HW]
            own[2 * p + i, HW : 2 * HW, :] = d_query[i * HW : (i + 1) * HW]
    for j in range(GROUP):
        early = slice(j * HW, (j + 1) * HW)
        late = slice((GROUP + j) * HW, (GROUP + j + 1) * HW)
        back[j, :HW, :] = (dk[early, :] * SCALE).astype(BF16)
        back[j, HW:, :] = dv[early, :].astype(BF16)
        own[j, 2 * HW : 3 * HW, :] = (dk[late, :] * SCALE).astype(BF16)
        own[j, 3 * HW : 4 * HW, :] = dv[late, :].astype(BF16)
        own[j, 4 * HW :, :] = jnp.zeros((ROWS - 4 * HW, DH), BF16)


def far_backward(place, mine, past, kept, result, sent, told):
    return pl.pallas_call(
        far_backward_kernel,
        in_specs=[SM] + [VM] * 6,
        out_specs=[VM, VM],
        out_shape=[
            jax.ShapeDtypeStruct((GROUP, ROWS, DH), BF16),
            jax.ShapeDtypeStruct((GROUP, 2 * HW, DH), BF16),
        ],
        scratch_shapes=[
            pltpu.VMEM((DH, 2 * GROUP * HW), BF16),
            pltpu.VMEM((2 * GROUP * HW, DH), BF16),
            pltpu.VMEM((2 * GROUP * HW, DH), F32),
            pltpu.VMEM((2 * GROUP * HW, DH), F32),
            pltpu.VMEM((KEYS, PAIR), BF16),
        ],
        compiler_params=params(),
        cost_estimate=cost(32 * KEYS * PAIR * DH, 6_000_000),
        name="far_backward",
    )(place, mine, past, kept, result, sent, told)


def add_back_kernel(own, back, out):
    for j in range(GROUP):
        out[j, 2 * HW : 4 * HW, :] = (
            own[j, 2 * HW : 4 * HW, :].astype(F32) + back[j].astype(F32)
        ).astype(BF16)


def add_back(own, back):
    return pl.pallas_call(
        add_back_kernel,
        in_specs=[VM] * 2,
        out_specs=VM,
        out_shape=jax.ShapeDtypeStruct((GROUP, ROWS, DH), BF16),
        input_output_aliases={0: 0},
        compiler_params=params(),
        cost_estimate=cost(GROUP * 2 * HW * DH, 2_500_000),
        name="add_back",
    )(own, back)


def unproject_other_kernel(
    place, near0, near1, near2, near3, far, w_qkv, w_out, other, rows, wq, wk, wv, wo, close, sems
):
    groups = weight_copies(place, w_qkv, w_out, (wq, wk, wv), wo, sems)
    start_all(groups)
    for step, near in zip(STEPS, (near0, near1, near2, near3)):
        close[head_here(place, step)] = near[...]
    parts = []
    for part in range(4):
        span = slice(part * HW, (part + 1) * HW)
        pieces = []
        for h in range(HALF):
            slot = slot_of_head(place, h)
            sums = [
                far[slot, s, span, :].astype(F32) + close[h, s, span, :].astype(F32)
                for s in range(2)
            ]
            rows[part, :, h * DH : (h + 1) * DH] = sums[0].astype(BF16)
            pieces.append(sums[1].astype(BF16))
        parts.append(jnp.concatenate(pieces, axis=1))
    wait_all(groups[0])
    total = mm_nt(parts[1], wq[...])
    wait_all(groups[1])
    total = total + mm_nt(parts[2], wk[...])
    wait_all(groups[2])
    total = total + mm_nt(parts[3], wv[...])
    wait_all(groups[3])
    mixed = mm(parts[0], wo[...])
    other[0] = mixed.astype(BF16)
    other[1] = total.astype(BF16)


def unproject_other(place, blocks, far, w_qkv, w_out):
    return pl.pallas_call(
        unproject_other_kernel,
        in_specs=[SM] + [VM] * 5 + [ANY] * 2,
        out_specs=[VM] * 6,
        scratch_shapes=[
            pltpu.VMEM((HALF, 2, 4 * HW, DH), BF16),
            pltpu.SemaphoreType.DMA((4 * PIECES,)),
        ],
        out_shape=[
            jax.ShapeDtypeStruct((2, HW, D), BF16),
            jax.ShapeDtypeStruct((4, HW, HALF * DH), BF16),
        ]
        + [jax.ShapeDtypeStruct((D, HALF * DH), BF16)] * 3
        + [jax.ShapeDtypeStruct((HALF * DH, D), BF16)],
        compiler_params=pltpu.CompilerParams(vmem_limit_bytes=LAST_LIMIT),
        cost_estimate=cost(PAIR * D * 4 * HALF * DH, 8_000_000),
        name="unproject_other",
    )(place, *blocks, far, w_qkv, w_out)


def unproject_own_kernel(rows, wq, wk, wv, wo, own):
    own[0] = mm(rows[0], wo[...])
    own[1] = mm_nt(rows[1], wq[...]) + mm_nt(rows[2], wk[...]) + mm_nt(rows[3], wv[...])


def unproject_own(rows, weights):
    return pl.pallas_call(
        unproject_own_kernel,
        in_specs=[VM] * 5,
        out_specs=VM,
        out_shape=jax.ShapeDtypeStruct((2, HW, D), F32),
        compiler_params=params(),
        cost_estimate=cost(PAIR * D * 4 * HALF * DH, 6_000_000),
        name="unproject_own",
    )(rows, *weights)


def finish_kernel(tokens, cot, gain, own, other, mixed, out):
    x = tokens[...].astype(F32)
    mixed[...] = (x + (own[0] + other[0].astype(F32))).astype(BF16)
    rinv = lax.rsqrt(jnp.mean(x * x, axis=-1, keepdims=True) + EPS)
    scaled = (own[1] + other[1].astype(F32)) * gain[...]
    mean = jnp.mean(scaled * x, axis=-1, keepdims=True)
    grad = rinv * scaled - x * (rinv * rinv * rinv * mean)
    out[...] = (cot[...].astype(F32) + grad).astype(BF16)


def finish(tokens, cot, gain, own, other):
    return pl.pallas_call(
        finish_kernel,
        in_specs=[VM] * 5,
        out_specs=[VM] * 2,
        out_shape=[jax.ShapeDtypeStruct((HW, D), BF16)] * 2,
        compiler_params=params(),
        cost_estimate=cost(HW * D * 10, 3_000_000),
        name="finish",
    )(tokens, cot, gain, own, other)


LANE = ("x", "zl")
SAME_HEAD = [
    [(x * 2 + zl) * 4 + (h + 4 - x) % 4 for x in range(4) for zl in range(2)] for h in range(4)
]


def swap(value):
    return lax.ppermute(value, "core", [(0, 1), (1, 0)])


def turn_ring(value, steps):
    return lax.ppermute(value, "zh", [(i, (i + steps) % 4) for i in range(4)])


def all_round(blocks, sign):
    return [blocks[0]] + [turn_ring(blocks[g], sign * STEPS[g]) for g in (1, 2, 3)]


def exchange(value, axes, groups=None):
    return lax.all_to_all(value, axes, 0, 0, axis_index_groups=groups, tiled=True)


def exchange_alone(value, go):
    return lax.cond(go, lambda v: exchange(v, LANE), jnp.zeros_like, value)


def per_device(tokens, gain, w_qkv, w_out, window, valid, cotangent):
    rows = lax.axis_size("y")
    place = jnp.stack(
        [lax.axis_index(axis) for axis in ("core", "x", "zh")]
    ).astype(jnp.int32)
    go = window[0] > 0
    tokens = tokens.reshape(HW, D)
    cot = cotangent.reshape(HW, D)
    other_tokens = swap(tokens)
    other_cot = swap(cot)
    gain = gain.reshape(1, D)
    weights = stage(place, w_qkv, w_out)
    packed, *blocks = project(
        place, valid, tokens, other_tokens, cot, other_cot, gain, weights
    )
    blocks = all_round(blocks, 1)
    mine = exchange(packed.reshape(2 * HALF, ROWS, DH), LANE)
    past = lax.ppermute(mine[:, K0:, :], "y", [(i, i + 1) for i in range(rows - 1)])
    near_kept, near_result, close = near_forward(*blocks)
    sent, far_kept, far_result = far_forward(place, window, mine, past, close)
    told = exchange(sent, ("x", "zl", "zh"), SAME_HEAD)
    own, back = far_backward(place, mine, past, far_kept, far_result, sent, told)
    back = lax.ppermute(back, "y", [(i + 1, i) for i in range(rows - 1)])
    returned = near_backward(place, blocks, near_kept, near_result, close, told)
    own, returned = lax.optimization_barrier((own, returned))
    returned = all_round(returned, -1)
    own = add_back(own, back)
    far = exchange_alone(own, go).reshape(HALF, 2, ROWS, DH)
    out_other, own_rows, *weights = unproject_other(place, returned, far, w_qkv, w_out)
    out_other = swap(out_other)
    out_own = unproject_own(own_rows, weights)
    mixed, d_tokens = finish(tokens, cot, gain, out_own, out_other)
    return mixed.reshape(1, 1, HW, D), d_tokens.reshape(1, 1, HW, D)


def solution(mesh):
    grid = Mesh(mesh.devices.reshape(4, 4, 2, 4, 2), ("y", "x", "zl", "zh", "core"))
    frames, cams = ("y", "x", "zl"), ("zh", "core")
    split = P(frames, cams, None, None)
    return jax.shard_map(
        per_device,
        mesh=grid,
        in_specs=(split, P(), P(), P(), P(), P(frames), split),
        out_specs=(split, split),
        check_vma=False,
    )
```

```python
import math

import jax
import jax.numpy as jnp
from jax import lax
from jax.experimental import pallas as pl
from jax.experimental.pallas import tpu as pltpu
from jax.sharding import Mesh
from jax.sharding import PartitionSpec as P

D = 1024
H = 8
DH = 128
HW = 128
WIN = 8
EPS = 1e-05

HALF = H // 2
PAIR = 2 * HW
GROUP = 8
SCALE = DH ** (-0.5)
SCALE2 = SCALE * math.log2(math.e)
FLOOR = -3.0e38
F32 = jnp.float32
BF16 = jnp.bfloat16
NT = (((1,), (1,)), ((), ()))
VMEM_LIMIT = 20 * 1024 * 1024
STAGE_LIMIT = 48 * 1024 * 1024

Q0, G0, K0, V0, OK0, ROWS = 0, 128, 256, 384, 512, 528
TOKENS = 8 * HW
KEYS = (WIN + 1) * HW


def params(**kw):
    return pltpu.CompilerParams(vmem_limit_bytes=VMEM_LIMIT, **kw)


def mm(a, b):
    return jnp.dot(a, b, preferred_element_type=F32)


def mm_nt(a, b):
    return lax.dot_general(a, b, NT, preferred_element_type=F32)


def turn(a):
    return a.astype(F32).T


VM = pl.BlockSpec(memory_space=pltpu.VMEM)
SM = pl.BlockSpec(memory_space=pltpu.SMEM)
ANY = pl.BlockSpec(memory_space=pltpu.HBM)


def cost(flops, size, exps=0):
    return pl.CostEstimate(flops=flops, bytes_accessed=size, transcendentals=exps)


PIECES = 4


def weight_copies(place, w_qkv, w_out, targets, sems):
    begin = pl.multiple_of(place[0] * HALF * DH, HALF * DH)
    groups = []
    for part, target in targets:
        size = target.shape[0] // PIECES
        group = []
        for n in range(PIECES):
            if part < 3:
                columns = pl.ds(pl.multiple_of(begin + part * D, HALF * DH), HALF * DH)
                source = w_qkv.at[pl.ds(n * size, size), columns]
            else:
                source = w_out.at[pl.ds(pl.multiple_of(begin + n * size, size), size), :]
            spot = target.at[pl.ds(n * size, size), :]
            group.append(pltpu.make_async_copy(source, spot, sems.at[part * PIECES + n]))
        groups.append(group)
    return groups


def start_all(groups):
    for group in groups:
        for copy in group:
            copy.start()


def wait_all(group):
    for copy in group:
        copy.wait()


def stage_kernel(place, w_qkv, wq, wk, sems):
    groups = weight_copies(place, w_qkv, None, ((0, wq), (1, wk)), sems)
    start_all(groups)
    for group in groups:
        wait_all(group)


def stage(place, w_qkv):
    return pl.pallas_call(
        stage_kernel,
        in_specs=[SM, ANY],
        out_specs=[VM] * 2,
        out_shape=[jax.ShapeDtypeStruct((D, HALF * DH), BF16)] * 2,
        scratch_shapes=[pltpu.SemaphoreType.DMA((2 * PIECES,))],
        compiler_params=pltpu.CompilerParams(vmem_limit_bytes=STAGE_LIMIT),
        cost_estimate=cost(0, 9_000_000),
        name="stage",
    )(place, w_qkv)


STEPS = (0, 2, 1, 3)


def slot_of_head(place, h):
    return lax.rem(h + HALF - place[2], HALF)


def head_here(place, step=0):
    return lax.rem(place[1] + place[2] + step, HALF)


def project_kernel(
    place, valid, own, other, cot_own, cot_other, gain, wq, wk, w_qkv, w_out,
    packed, near0, near1, near2, near3, made, wv, wo, sems, out_sems,
):
    groups = weight_copies(place, w_qkv, w_out, ((2, wv), (3, wo)), sems)
    start_all(groups)
    flags = jnp.full((ROWS - OK0, DH), valid[0], jnp.int32).astype(F32).astype(BF16)
    for h in range(HALF):
        for s in range(2):
            made[h, s, OK0:ROWS, :] = flags
    x = jnp.concatenate([own[...], other[...]], axis=0).astype(F32)
    rinv = lax.rsqrt(jnp.mean(x * x, axis=-1, keepdims=True) + EPS)
    normed = (x * rinv * gain[...]).astype(BF16)
    leaving = []
    for n, (row, weight) in enumerate(((Q0, wq), (K0, wk), (V0, wv), (G0, wo))):
        if n >= 2:
            wait_all(groups[n - 2])
        if row == G0:
            cots = jnp.concatenate([cot_own[...], cot_other[...]], axis=0)
            got = mm_nt(cots, weight[...]).astype(BF16)
        else:
            got = mm(normed, weight[...]).astype(BF16)
        for h in range(HALF):
            for s in range(2):
                made[slot_of_head(place, h), s, row : row + HW, :] = (
                    got[s * HW : (s + 1) * HW, h * DH : (h + 1) * DH]
                )
        end = ROWS if row == V0 else row + HW
        span = pl.ds(row, end - row)
        moves = [(made.at[:, :, span, :], packed.at[:, :, span, :])]
        for step, near in zip(STEPS, (near0, near1, near2, near3)):
            slot = lax.rem(place[1] + step, HALF)
            rows = pl.ds(row, HW)
            moves.append((made.at[slot, :, rows, :], near.at[:, rows, :]))
        for m, (source, target) in enumerate(moves):
            copy = pltpu.make_async_copy(source, target, out_sems.at[5 * n + m])
            copy.start()
            leaving.append(copy)
    for copy in leaving:
        copy.wait()


def project(place, valid, own, other, cot_own, cot_other, gain, weights, w_qkv, w_out):
    return pl.pallas_call(
        project_kernel,
        in_specs=[SM, SM] + [VM] * 7 + [ANY] * 2,
        out_specs=[ANY] * 5,
        out_shape=[jax.ShapeDtypeStruct((HALF, 2, ROWS, DH), BF16)]
        + [jax.ShapeDtypeStruct((2, OK0, DH), BF16)] * 4,
        scratch_shapes=[
            pltpu.VMEM((HALF, 2, ROWS, DH), BF16),
            pltpu.VMEM((D, HALF * DH), BF16),
            pltpu.VMEM((HALF * DH, D), BF16),
            pltpu.SemaphoreType.DMA((4 * PIECES,)),
            pltpu.SemaphoreType.DMA((20,)),
        ],
        compiler_params=pltpu.CompilerParams(vmem_limit_bytes=STAGE_LIMIT),
        cost_estimate=cost(2 * PAIR * D * 4 * HALF * DH, 7_000_000),
        name="project",
    )(place, valid, own, other, cot_own, cot_other, gain, *weights, w_qkv, w_out)


def both(block, row):
    return jnp.concatenate([block[0, row : row + HW, :], block[1, row : row + HW, :]], axis=0)


def near_forward_kernel(near0, near1, near2, near3, kept, result, stats, scores):
    blocks = (near0, near1, near2, near3)
    turned = [turn(both(block, V0)).astype(BF16) for block in blocks]
    for g in range(4):
        cols = slice(g * PAIR, (g + 1) * PAIR)
        query = both(blocks[g], Q0)
        grad_t = turn(both(blocks[g], G0))
        peak = jnp.full((1, PAIR), -jnp.inf, F32)
        for z in range(4):
            block = mm_nt(both(blocks[z], K0), query)
            scores[z * PAIR : (z + 1) * PAIR, :] = block
            peak = jnp.maximum(peak, jnp.max(block, axis=0, keepdims=True))
        peak = peak * SCALE2
        total = jnp.zeros((1, PAIR), F32)
        for b in range(8):
            rows = slice(b * HW, (b + 1) * HW)
            block = jnp.exp2(scores[rows, :] * SCALE2 - peak)
            total = total + jnp.sum(block, axis=0, keepdims=True)
            kept[rows, cols] = block.astype(BF16)
        got = jnp.zeros((DH, PAIR), F32)
        for z in range(4):
            got = got + mm(turned[z], kept[z * PAIR : (z + 1) * PAIR, cols])
        result[:, cols] = got
        delta = jnp.sum(got * grad_t, axis=0, keepdims=True)
        told = jnp.concatenate([peak, total, delta, jnp.zeros((1, PAIR), F32)], axis=0)
        stats[2 * g] = told[:, :HW]
        stats[2 * g + 1] = told[:, HW:]


def near_forward(*blocks):
    return pl.pallas_call(
        near_forward_kernel,
        in_specs=[VM] * 4,
        out_specs=[VM] * 3,
        out_shape=[
            jax.ShapeDtypeStruct((TOKENS, TOKENS), BF16),
            jax.ShapeDtypeStruct((DH, TOKENS), F32),
            jax.ShapeDtypeStruct((8, 4, HW), F32),
        ],
        scratch_shapes=[pltpu.VMEM((TOKENS, PAIR), F32)],
        compiler_params=params(),
        cost_estimate=cost(80 * TOKENS * TOKENS * DH, 4_000_000, TOKENS * TOKENS),
        name="near_forward",
    )(*blocks)


def slot_of_near(place, step, s):
    return lax.rem(place[1] + step, 4) * 2 + s


def far_forward_kernel(place, win, mine, past, close, told, kept, result, keys, values_t, scores):
    width = win[place[0] * HALF + head_here(place)]
    for g in range(4):
        for s in range(2):
            told[slot_of_near(place, STEPS[g], s), 0:4, :] = close[2 * g + s]
    for j in range(GROUP):
        keys[j * HW : (j + 1) * HW, :] = past[j, :HW, :]
        keys[(GROUP + j) * HW : (GROUP + j + 1) * HW, :] = mine[j, K0 : K0 + HW, :]
        values_t[:, j * HW : (j + 1) * HW] = turn(past[j, HW : 2 * HW, :]).astype(BF16)
        values_t[:, (GROUP + j) * HW : (GROUP + j + 1) * HW] = turn(
            mine[j, V0 : V0 + HW, :]
        ).astype(BF16)
    for p in range(GROUP // 2):
        query = jnp.concatenate([mine[2 * p, :HW, :], mine[2 * p + 1, :HW, :]], axis=0)
        grad_t = jnp.concatenate(
            [turn(mine[2 * p, G0 : G0 + HW, :]), turn(mine[2 * p + 1, G0 : G0 + HW, :])], axis=1
        )
        peak = jnp.full((1, PAIR), -jnp.inf, F32)
        for b in range(WIN + 1):
            j = 2 * p + b
            if j < GROUP:
                flag = past[j, 2 * HW : 2 * HW + 1, :].astype(F32)
            else:
                flag = mine[j - GROUP, OK0 : OK0 + 1, :].astype(F32)
            lower = jnp.where((flag > 0.5) & (b >= WIN - width) & (b < WIN), 0.0, -jnp.inf)
            upper = jnp.where((flag > 0.5) & (b >= WIN + 1 - width), 0.0, -jnp.inf)
            bias = jnp.concatenate([lower, upper], axis=1)
            block = mm_nt(keys[j * HW : (j + 1) * HW, :], query) + bias
            scores[b * HW : (b + 1) * HW, :] = block
            peak = jnp.maximum(peak, jnp.max(block, axis=0, keepdims=True))
        peak = jnp.maximum(peak * SCALE2, FLOOR)
        total = jnp.zeros((1, PAIR), F32)
        for b in range(WIN + 1):
            block = jnp.exp2(scores[b * HW : (b + 1) * HW, :] * SCALE2 - peak)
            total = total + jnp.sum(block, axis=0, keepdims=True)
            kept[p, b * HW : (b + 1) * HW, :] = block.astype(BF16)
        got = mm(values_t[:, p * PAIR : p * PAIR + KEYS], kept[p])
        result[:, p * PAIR : (p + 1) * PAIR] = got
        delta = jnp.sum(got * grad_t, axis=0, keepdims=True)
        stats = jnp.concatenate([peak, total, delta, jnp.zeros((1, PAIR), F32)], axis=0)
        told[2 * p, 4:8, :] = stats[:, :HW]
        told[2 * p + 1, 4:8, :] = stats[:, HW:]


def far_forward(place, window, mine, past, close):
    return pl.pallas_call(
        far_forward_kernel,
        in_specs=[SM, SM, VM, VM, VM],
        out_specs=[VM] * 3,
        out_shape=[
            jax.ShapeDtypeStruct((GROUP, 8, HW), F32),
            jax.ShapeDtypeStruct((GROUP // 2, KEYS, PAIR), BF16),
            jax.ShapeDtypeStruct((DH, GROUP * HW), F32),
        ],
        scratch_shapes=[
            pltpu.VMEM((2 * GROUP * HW, DH), BF16),
            pltpu.VMEM((DH, 2 * GROUP * HW), BF16),
            pltpu.VMEM((KEYS, PAIR), F32),
        ],
        compiler_params=params(),
        cost_estimate=cost(16 * KEYS * PAIR * DH, 5_000_000, 4 * KEYS * PAIR),
        name="far_forward",
    )(place, window, mine, past, close)


def merge(this, other):
    top = jnp.maximum(this[0:1], other[0:1])
    here = jnp.exp2(this[0:1] - top)
    there = jnp.exp2(other[0:1] - top)
    inverse = 1.0 / (here * this[1:2] + there * other[1:2])
    here = here * inverse
    delta = here * this[2:3] + there * inverse * other[2:3]
    return here, here * delta


def near_backward_kernel(
    place, near0, near1, near2, near3, kept, result, stats, told,
    back0, back1, back2, back3, grads, grad_all, query_all,
):
    blocks = (near0, near1, near2, near3)
    outs = (back0, back1, back2, back3)
    for g in range(4):
        cols = slice(g * PAIR, (g + 1) * PAIR)
        this = jnp.concatenate([stats[2 * g], stats[2 * g + 1]], axis=1)
        other = jnp.concatenate(
            [told[slot_of_near(place, STEPS[g], s), 4:8, :] for s in range(2)], axis=1
        )
        weight, delta = merge(this, other)
        grad_t = (turn(both(blocks[g], G0)) * weight).astype(BF16)
        grad_all[:, cols] = grad_t
        query_all[cols, :] = both(blocks[g], Q0)
        attended = (result[:, cols] * weight).T.astype(BF16)
        for s in range(2):
            outs[g][s, :HW, :] = attended[s * HW : (s + 1) * HW]
        for z in range(4):
            rows = slice(z * PAIR, (z + 1) * PAIR)
            d_probs = mm(both(blocks[z], V0), grad_t)
            grads[rows, cols] = (kept[rows, cols].astype(F32) * (d_probs - delta)).astype(BF16)
    for z in range(4):
        rows = slice(z * PAIR, (z + 1) * PAIR)
        d_values = mm_nt(kept[rows, :], grad_all[...]).astype(BF16)
        d_keys = (mm(grads[rows, :], query_all[...]) * SCALE).astype(BF16)
        for s in range(2):
            outs[z][s, 2 * HW : 3 * HW, :] = d_keys[s * HW : (s + 1) * HW]
            outs[z][s, 3 * HW :, :] = d_values[s * HW : (s + 1) * HW]
    keys_t = jnp.concatenate([turn(both(block, K0)).astype(BF16) for block in blocks], axis=1)
    for g in range(4):
        cols = slice(g * PAIR, (g + 1) * PAIR)
        d_query = (mm(keys_t, grads[:, cols]) * SCALE).T.astype(BF16)
        for s in range(2):
            outs[g][s, HW : 2 * HW, :] = d_query[s * HW : (s + 1) * HW]


def near_backward(place, blocks, kept, result, stats, told):
    return pl.pallas_call(
        near_backward_kernel,
        in_specs=[SM] + [VM] * 8,
        out_specs=[VM] * 4,
        out_shape=[jax.ShapeDtypeStruct((2, 4 * HW, DH), BF16)] * 4,
        scratch_shapes=[
            pltpu.VMEM((TOKENS, TOKENS), BF16),
            pltpu.VMEM((DH, TOKENS), BF16),
            pltpu.VMEM((TOKENS, DH), BF16),
        ],
        compiler_params=params(),
        cost_estimate=cost(8 * TOKENS * TOKENS * DH, 5_000_000),
        name="near_backward",
    )(place, *blocks, kept, result, stats, told)


def far_backward_kernel(
    place, mine, past, kept, result, sent, told, own, back, keys_t, values, dk, dv, grads
):
    for j in range(GROUP):
        keys_t[:, j * HW : (j + 1) * HW] = turn(past[j, :HW, :]).astype(BF16)
        keys_t[:, (GROUP + j) * HW : (GROUP + j + 1) * HW] = turn(
            mine[j, K0 : K0 + HW, :]
        ).astype(BF16)
        values[j * HW : (j + 1) * HW, :] = past[j, HW : 2 * HW, :]
        values[(GROUP + j) * HW : (GROUP + j + 1) * HW, :] = mine[j, V0 : V0 + HW, :]
    dk[...] = jnp.zeros_like(dk)
    dv[...] = jnp.zeros_like(dv)
    for p in range(GROUP // 2):
        query = jnp.concatenate([mine[2 * p, :HW, :], mine[2 * p + 1, :HW, :]], axis=0)
        grad_t = jnp.concatenate(
            [turn(mine[2 * p, G0 : G0 + HW, :]), turn(mine[2 * p + 1, G0 : G0 + HW, :])], axis=1
        )
        this = jnp.concatenate([sent[2 * p, 4:8, :], sent[2 * p + 1, 4:8, :]], axis=1)
        other = jnp.concatenate([told[2 * p, 0:4, :], told[2 * p + 1, 0:4, :]], axis=1)
        weight, delta = merge(this, other)
        grad_t = (grad_t * weight).astype(BF16)
        at = p * PAIR
        attended = (result[:, at : at + PAIR] * weight).T.astype(BF16)
        for lo, size in ((0, 384), (384, 384), (768, 384)):
            rows = slice(lo, lo + size)
            spot = slice(at + lo, at + lo + size)
            d_probs = mm(values[spot, :], grad_t)
            block = kept[p, rows, :]
            d_scores = (block.astype(F32) * (d_probs - delta)).astype(BF16)
            grads[rows, :] = d_scores
            dv[spot, :] += mm_nt(block, grad_t)
            dk[spot, :] += mm(d_scores, query)
        d_query = (mm(keys_t[:, at : at + KEYS], grads[...]) * SCALE).T.astype(BF16)
        for i in range(2):
            own[2 * p + i, :HW, :] = attended[i * HW : (i + 1) * HW]
            own[2 * p + i, HW : 2 * HW, :] = d_query[i * HW : (i + 1) * HW]
    for j in range(GROUP):
        early = slice(j * HW, (j + 1) * HW)
        late = slice((GROUP + j) * HW, (GROUP + j + 1) * HW)
        back[j, :HW, :] = (dk[early, :] * SCALE).astype(BF16)
        back[j, HW:, :] = dv[early, :].astype(BF16)
        own[j, 2 * HW : 3 * HW, :] = (dk[late, :] * SCALE).astype(BF16)
        own[j, 3 * HW :, :] = dv[late, :].astype(BF16)


def far_backward(place, mine, past, kept, result, sent, told):
    return pl.pallas_call(
        far_backward_kernel,
        in_specs=[SM] + [VM] * 6,
        out_specs=[VM, VM],
        out_shape=[
            jax.ShapeDtypeStruct((GROUP, 4 * HW, DH), BF16),
            jax.ShapeDtypeStruct((GROUP, 2 * HW, DH), BF16),
        ],
        scratch_shapes=[
            pltpu.VMEM((DH, 2 * GROUP * HW), BF16),
            pltpu.VMEM((2 * GROUP * HW, DH), BF16),
            pltpu.VMEM((2 * GROUP * HW, DH), F32),
            pltpu.VMEM((2 * GROUP * HW, DH), F32),
            pltpu.VMEM((KEYS, PAIR), BF16),
        ],
        compiler_params=params(),
        cost_estimate=cost(32 * KEYS * PAIR * DH, 6_000_000),
        name="far_backward",
    )(place, mine, past, kept, result, sent, told)


def add_back_kernel(own, back, out):
    for j in range(GROUP):
        out[j, 2 * HW : 4 * HW, :] = (
            own[j, 2 * HW : 4 * HW, :].astype(F32) + back[j].astype(F32)
        ).astype(BF16)


def add_back(own, back):
    return pl.pallas_call(
        add_back_kernel,
        in_specs=[VM] * 2,
        out_specs=VM,
        out_shape=jax.ShapeDtypeStruct((GROUP, 4 * HW, DH), BF16),
        input_output_aliases={0: 0},
        compiler_params=params(),
        cost_estimate=cost(GROUP * 2 * HW * DH, 2_500_000),
        name="add_back",
    )(own, back)


def unproject_kernel(
    place, near0, near1, near2, near3, far, w_qkv, w_out, own, other, close, wq, wk, wv, wo, sems
):
    groups = weight_copies(place, w_qkv, w_out, ((0, wq), (1, wk), (2, wv), (3, wo)), sems)
    start_all(groups)
    for step, near in zip(STEPS, (near0, near1, near2, near3)):
        close[head_here(place, step)] = near[...]
    parts = []
    for part in range(4):
        rows = slice(part * HW, (part + 1) * HW)
        pieces = []
        for h in range(HALF):
            slot = slot_of_head(place, h)
            away = jnp.concatenate([far[slot, 0, rows, :], far[slot, 1, rows, :]], axis=0)
            here = jnp.concatenate([close[h, 0, rows, :], close[h, 1, rows, :]], axis=0)
            pieces.append((away.astype(F32) + here.astype(F32)).astype(BF16))
        parts.append(jnp.concatenate(pieces, axis=1))
    wait_all(groups[0])
    total = mm_nt(parts[1], wq[...])
    wait_all(groups[1])
    total = total + mm_nt(parts[2], wk[...])
    wait_all(groups[2])
    total = total + mm_nt(parts[3], wv[...])
    wait_all(groups[3])
    mixed = mm(parts[0], wo[...])
    own[0] = mixed[:HW]
    own[1] = total[:HW]
    other[0] = mixed[HW:].astype(BF16)
    other[1] = total[HW:].astype(BF16)


def unproject(place, blocks, far, w_qkv, w_out):
    return pl.pallas_call(
        unproject_kernel,
        in_specs=[SM] + [VM] * 5 + [ANY] * 2,
        out_specs=[VM, VM],
        scratch_shapes=[pltpu.VMEM((HALF, 2, 4 * HW, DH), BF16)]
        + [pltpu.VMEM((D, HALF * DH), BF16)] * 3
        + [pltpu.VMEM((HALF * DH, D), BF16), pltpu.SemaphoreType.DMA((4 * PIECES,))],
        out_shape=[jax.ShapeDtypeStruct((2, HW, D), F32), jax.ShapeDtypeStruct((2, HW, D), BF16)],
        compiler_params=pltpu.CompilerParams(vmem_limit_bytes=50 * 1024 * 1024),
        cost_estimate=cost(2 * PAIR * D * 4 * HALF * DH, 8_000_000),
        name="unproject",
    )(place, *blocks, far, w_qkv, w_out)


def finish_kernel(tokens, cot, gain, own, other, mixed, out):
    x = tokens[...].astype(F32)
    mixed[...] = (x + (own[0] + other[0].astype(F32))).astype(BF16)
    rinv = lax.rsqrt(jnp.mean(x * x, axis=-1, keepdims=True) + EPS)
    scaled = (own[1] + other[1].astype(F32)) * gain[...]
    mean = jnp.mean(scaled * x, axis=-1, keepdims=True)
    grad = rinv * scaled - x * (rinv * rinv * rinv * mean)
    out[...] = (cot[...].astype(F32) + grad).astype(BF16)


def finish(tokens, cot, gain, own, other):
    return pl.pallas_call(
        finish_kernel,
        in_specs=[VM] * 5,
        out_specs=[VM] * 2,
        out_shape=[jax.ShapeDtypeStruct((HW, D), BF16)] * 2,
        compiler_params=params(),
        cost_estimate=cost(HW * D * 10, 3_000_000),
        name="finish",
    )(tokens, cot, gain, own, other)


LANE = ("x", "zl")
SAME_HEAD = [
    [(x * 2 + zl) * 4 + (h + 4 - x) % 4 for x in range(4) for zl in range(2)] for h in range(4)
]


def swap(value):
    return lax.ppermute(value, "core", [(0, 1), (1, 0)])


def turn_ring(value, steps):
    return lax.ppermute(value, "zh", [(i, (i + steps) % 4) for i in range(4)])


def all_round(blocks, sign):
    return [blocks[0]] + [turn_ring(blocks[g], sign * STEPS[g]) for g in (1, 2, 3)]


def exchange(value, axes, groups=None):
    return lax.all_to_all(value, axes, 0, 0, axis_index_groups=groups, tiled=True)


def exchange_alone(value, go):
    return lax.cond(go, lambda v: exchange(v, LANE), jnp.zeros_like, value)


def per_device(tokens, gain, w_qkv, w_out, window, valid, cotangent):
    rows = lax.axis_size("y")
    place = jnp.stack(
        [lax.axis_index(axis) for axis in ("core", "x", "zh")]
    ).astype(jnp.int32)
    go = window[0] > 0
    tokens = tokens.reshape(HW, D)
    cot = cotangent.reshape(HW, D)
    other_tokens = swap(tokens)
    other_cot = swap(cot)
    gain = gain.reshape(1, D)
    weights = stage(place, w_qkv)
    packed, *blocks = project(
        place, valid, tokens, other_tokens, cot, other_cot, gain, weights, w_qkv, w_out
    )
    blocks = all_round(blocks, 1)
    mine = exchange(packed.reshape(2 * HALF, ROWS, DH), LANE)
    past = lax.ppermute(mine[:, K0:, :], "y", [(i, i + 1) for i in range(rows - 1)])
    near_kept, near_result, close = near_forward(*blocks)
    sent, far_kept, far_result = far_forward(place, window, mine, past, close)
    told = exchange(sent, ("x", "zl", "zh"), SAME_HEAD)
    own, back = far_backward(place, mine, past, far_kept, far_result, sent, told)
    back = lax.ppermute(back, "y", [(i + 1, i) for i in range(rows - 1)])
    returned = near_backward(place, blocks, near_kept, near_result, close, told)
    own, returned = lax.optimization_barrier((own, returned))
    returned = all_round(returned, -1)
    own = add_back(own, back)
    far = exchange_alone(own, go).reshape(HALF, 2, 4 * HW, DH)
    out_own, out_other = unproject(place, returned, far, w_qkv, w_out)
    mixed, d_tokens = finish(tokens, cot, gain, out_own, swap(out_other))
    return mixed.reshape(1, 1, HW, D), d_tokens.reshape(1, 1, HW, D)


def solution(mesh):
    grid = Mesh(mesh.devices.reshape(4, 4, 2, 4, 2), ("y", "x", "zl", "zh", "core"))
    frames, cams = ("y", "x", "zl"), ("zh", "core")
    split = P(frames, cams, None, None)
    return jax.shard_map(
        per_device,
        mesh=grid,
        in_specs=(split, P(), P(), P(), P(), P(frames), split),
        out_specs=(split, split),
        check_vma=False,
    )
```

```python
import math

import jax
import jax.numpy as jnp
from jax import lax
from jax.experimental import pallas as pl
from jax.experimental.pallas import tpu as pltpu
from jax.sharding import Mesh
from jax.sharding import PartitionSpec as P

D = 1024
H = 8
DH = 128
HW = 128
WIN = 8
EPS = 1e-05

HALF = H // 2
PAIR = 2 * HW
GROUP = 8
SCALE = DH ** (-0.5)
SCALE2 = SCALE * math.log2(math.e)
FLOOR = -3.0e38
F32 = jnp.float32
BF16 = jnp.bfloat16
NT = (((1,), (1,)), ((), ()))
VMEM_LIMIT = 20 * 1024 * 1024
STAGE_LIMIT = 48 * 1024 * 1024

Q0, G0, K0, V0, OK0, ROWS = 0, 128, 256, 384, 512, 528
TOKENS = 8 * HW
KEYS = (WIN + 1) * HW


def params(**kw):
    return pltpu.CompilerParams(vmem_limit_bytes=VMEM_LIMIT, **kw)


def mm(a, b):
    return jnp.dot(a, b, preferred_element_type=F32)


def mm_nt(a, b):
    return lax.dot_general(a, b, NT, preferred_element_type=F32)


def turn(a):
    return a.astype(F32).T


VM = pl.BlockSpec(memory_space=pltpu.VMEM)
SM = pl.BlockSpec(memory_space=pltpu.SMEM)
ANY = pl.BlockSpec(memory_space=pltpu.HBM)


def cost(flops, size, exps=0):
    return pl.CostEstimate(flops=flops, bytes_accessed=size, transcendentals=exps)


PIECES = 4


def weight_copies(place, w_qkv, w_out, targets, sems):
    begin = pl.multiple_of(place[0] * HALF * DH, HALF * DH)
    groups = []
    for part, target in targets:
        size = target.shape[0] // PIECES
        group = []
        for n in range(PIECES):
            if part < 3:
                columns = pl.ds(pl.multiple_of(begin + part * D, HALF * DH), HALF * DH)
                source = w_qkv.at[pl.ds(n * size, size), columns]
            else:
                source = w_out.at[pl.ds(pl.multiple_of(begin + n * size, size), size), :]
            spot = target.at[pl.ds(n * size, size), :]
            group.append(pltpu.make_async_copy(source, spot, sems.at[part * PIECES + n]))
        groups.append(group)
    return groups


def start_all(groups):
    for group in groups:
        for copy in group:
            copy.start()


def wait_all(group):
    for copy in group:
        copy.wait()


def stage_kernel(place, w_qkv, w_out, wq, wk, wv, wo, sems):
    groups = weight_copies(place, w_qkv, w_out, ((0, wq), (1, wk), (2, wv), (3, wo)), sems)
    start_all(groups)
    for group in groups:
        wait_all(group)


def stage(place, w_qkv, w_out):
    return pl.pallas_call(
        stage_kernel,
        in_specs=[SM, ANY, ANY],
        out_specs=[VM] * 4,
        out_shape=[jax.ShapeDtypeStruct((D, HALF * DH), BF16)] * 3
        + [jax.ShapeDtypeStruct((HALF * DH, D), BF16)],
        scratch_shapes=[pltpu.SemaphoreType.DMA((4 * PIECES,))],
        compiler_params=pltpu.CompilerParams(vmem_limit_bytes=STAGE_LIMIT),
        cost_estimate=cost(0, 9_000_000),
        name="stage",
    )(place, w_qkv, w_out)


STEPS = (0, 2, 1, 3)


def slot_of_head(place, h):
    return lax.rem(h + HALF - place[2], HALF)


def head_here(place, step=0):
    return lax.rem(place[1] + place[2] + step, HALF)


def project_kernel(
    place, valid, own, other, cot_own, cot_other, gain, wq, wk, wv, wo,
    packed, near0, near1, near2, near3, made, out_sems,
):
    flags = jnp.full((ROWS - OK0, DH), valid[0], jnp.int32).astype(F32).astype(BF16)
    for h in range(HALF):
        for s in range(2):
            made[h, s, OK0:ROWS, :] = flags
    x = jnp.concatenate([own[...], other[...]], axis=0).astype(F32)
    rinv = lax.rsqrt(jnp.mean(x * x, axis=-1, keepdims=True) + EPS)
    normed = (x * rinv * gain[...]).astype(BF16)
    leaving = []
    for n, (row, weight) in enumerate(((Q0, wq), (K0, wk), (V0, wv), (G0, wo))):
        if row == G0:
            cots = jnp.concatenate([cot_own[...], cot_other[...]], axis=0)
            got = mm_nt(cots, weight[...]).astype(BF16)
        else:
            got = mm(normed, weight[...]).astype(BF16)
        for h in range(HALF):
            for s in range(2):
                made[slot_of_head(place, h), s, row : row + HW, :] = (
                    got[s * HW : (s + 1) * HW, h * DH : (h + 1) * DH]
                )
        end = ROWS if row == V0 else row + HW
        span = pl.ds(row, end - row)
        moves = [(made.at[:, :, span, :], packed.at[:, :, span, :])]
        for step, near in zip(STEPS, (near0, near1, near2, near3)):
            slot = lax.rem(place[1] + step, HALF)
            rows = pl.ds(row, HW)
            moves.append((made.at[slot, :, rows, :], near.at[:, rows, :]))
        for m, (source, target) in enumerate(moves):
            copy = pltpu.make_async_copy(source, target, out_sems.at[5 * n + m])
            copy.start()
            leaving.append(copy)
    for copy in leaving:
        copy.wait()


def project(place, valid, own, other, cot_own, cot_other, gain, weights):
    return pl.pallas_call(
        project_kernel,
        in_specs=[SM, SM] + [VM] * 9,
        out_specs=[ANY] * 5,
        out_shape=[jax.ShapeDtypeStruct((HALF, 2, ROWS, DH), BF16)]
        + [jax.ShapeDtypeStruct((2, OK0, DH), BF16)] * 4,
        scratch_shapes=[
            pltpu.VMEM((HALF, 2, ROWS, DH), BF16),
            pltpu.SemaphoreType.DMA((20,)),
        ],
        compiler_params=params(),
        cost_estimate=cost(2 * PAIR * D * 4 * HALF * DH, 7_000_000),
        name="project",
    )(place, valid, own, other, cot_own, cot_other, gain, *weights)


def both(block, row):
    return jnp.concatenate([block[0, row : row + HW, :], block[1, row : row + HW, :]], axis=0)


def near_forward_kernel(near0, near1, near2, near3, kept, result, stats, scores):
    blocks = (near0, near1, near2, near3)
    turned = [turn(both(block, V0)).astype(BF16) for block in blocks]
    query = jnp.concatenate([both(block, Q0) for block in blocks], axis=0)
    peak = jnp.full((1, TOKENS), -jnp.inf, F32)
    for b in range(8):
        keys = blocks[b // 2][b % 2, K0 : K0 + HW, :]
        block = mm_nt(keys, query)
        scores[b * HW : (b + 1) * HW, :] = block
        peak = jnp.maximum(peak, jnp.max(block, axis=0, keepdims=True))
    peak = peak * SCALE2
    total = jnp.zeros((1, TOKENS), F32)
    for b in range(32):
        rows = slice(b * 32, (b + 1) * 32)
        block = jnp.exp2(scores[rows, :] * SCALE2 - peak)
        total = total + jnp.sum(block, axis=0, keepdims=True)
        kept[rows, :] = block.astype(BF16)
    turned = jnp.concatenate(turned, axis=1)
    for g in range(4):
        cols = slice(g * PAIR, (g + 1) * PAIR)
        got = mm(turned, kept[:, cols])
        result[:, cols] = got
        delta = jnp.sum(got * turn(both(blocks[g], G0)), axis=0, keepdims=True)
        told = jnp.concatenate(
            [peak[:, cols], total[:, cols], delta, jnp.zeros((1, PAIR), F32)], axis=0
        )
        stats[2 * g] = told[:, :HW]
        stats[2 * g + 1] = told[:, HW:]


def near_forward(*blocks):
    return pl.pallas_call(
        near_forward_kernel,
        in_specs=[VM] * 4,
        out_specs=[VM] * 3,
        out_shape=[
            jax.ShapeDtypeStruct((TOKENS, TOKENS), BF16),
            jax.ShapeDtypeStruct((DH, TOKENS), F32),
            jax.ShapeDtypeStruct((8, 4, HW), F32),
        ],
        scratch_shapes=[pltpu.VMEM((TOKENS, TOKENS), F32)],
        compiler_params=params(),
        cost_estimate=cost(80 * TOKENS * TOKENS * DH, 4_000_000, TOKENS * TOKENS),
        name="near_forward",
    )(*blocks)


def slot_of_near(place, step, s):
    return lax.rem(place[1] + step, 4) * 2 + s


def far_forward_kernel(place, win, mine, past, close, told, kept, result, values_t, scores):
    width = win[place[0] * HALF + head_here(place)]
    for g in range(4):
        for s in range(2):
            told[slot_of_near(place, STEPS[g], s), 0:4, :] = close[2 * g + s]
    for j in range(GROUP):
        values_t[:, j * HW : (j + 1) * HW] = turn(past[j, HW : 2 * HW, :]).astype(BF16)
        values_t[:, (GROUP + j) * HW : (GROUP + j + 1) * HW] = turn(
            mine[j, V0 : V0 + HW, :]
        ).astype(BF16)
    for p in range(GROUP // 2):
        query = jnp.concatenate([mine[2 * p, :HW, :], mine[2 * p + 1, :HW, :]], axis=0)
        grad_t = jnp.concatenate(
            [turn(mine[2 * p, G0 : G0 + HW, :]), turn(mine[2 * p + 1, G0 : G0 + HW, :])], axis=1
        )
        peak = jnp.full((1, PAIR), -jnp.inf, F32)
        for b in range(WIN + 1):
            j = 2 * p + b
            if j < GROUP:
                keys = past[j, :HW, :]
                flag = past[j, 2 * HW : 2 * HW + 1, :].astype(F32)
            else:
                keys = mine[j - GROUP, K0 : K0 + HW, :]
                flag = mine[j - GROUP, OK0 : OK0 + 1, :].astype(F32)
            lower = jnp.where((flag > 0.5) & (b >= WIN - width) & (b < WIN), 0.0, -jnp.inf)
            upper = jnp.where((flag > 0.5) & (b >= WIN + 1 - width), 0.0, -jnp.inf)
            bias = jnp.concatenate([lower, upper], axis=1)
            block = mm_nt(keys, query) + bias
            scores[b * HW : (b + 1) * HW, :] = block
            peak = jnp.maximum(peak, jnp.max(block, axis=0, keepdims=True))
        peak = jnp.maximum(peak * SCALE2, FLOOR)
        total = jnp.zeros((1, PAIR), F32)
        for b in range(WIN + 1):
            block = jnp.exp2(scores[b * HW : (b + 1) * HW, :] * SCALE2 - peak)
            total = total + jnp.sum(block, axis=0, keepdims=True)
            kept[p, b * HW : (b + 1) * HW, :] = block.astype(BF16)
        got = mm(values_t[:, p * PAIR : p * PAIR + KEYS], kept[p])
        result[:, p * PAIR : (p + 1) * PAIR] = got
        delta = jnp.sum(got * grad_t, axis=0, keepdims=True)
        stats = jnp.concatenate([peak, total, delta, jnp.zeros((1, PAIR), F32)], axis=0)
        told[2 * p, 4:8, :] = stats[:, :HW]
        told[2 * p + 1, 4:8, :] = stats[:, HW:]


def far_forward(place, window, mine, past, close):
    return pl.pallas_call(
        far_forward_kernel,
        in_specs=[SM, SM, VM, VM, VM],
        out_specs=[VM] * 3,
        out_shape=[
            jax.ShapeDtypeStruct((GROUP, 8, HW), F32),
            jax.ShapeDtypeStruct((GROUP // 2, KEYS, PAIR), BF16),
            jax.ShapeDtypeStruct((DH, GROUP * HW), F32),
        ],
        scratch_shapes=[
            pltpu.VMEM((DH, 2 * GROUP * HW), BF16),
            pltpu.VMEM((KEYS, PAIR), F32),
        ],
        compiler_params=params(),
        cost_estimate=cost(16 * KEYS * PAIR * DH, 5_000_000, 4 * KEYS * PAIR),
        name="far_forward",
    )(place, window, mine, past, close)


def merge(this, other):
    top = jnp.maximum(this[0:1], other[0:1])
    here = jnp.exp2(this[0:1] - top)
    there = jnp.exp2(other[0:1] - top)
    inverse = 1.0 / (here * this[1:2] + there * other[1:2])
    here = here * inverse
    delta = here * this[2:3] + there * inverse * other[2:3]
    return here, here * delta


def near_backward_kernel(
    place, near0, near1, near2, near3, kept, result, stats, told,
    back0, back1, back2, back3, grads, grad_all, query_all,
):
    blocks = (near0, near1, near2, near3)
    outs = (back0, back1, back2, back3)
    for g in range(4):
        cols = slice(g * PAIR, (g + 1) * PAIR)
        this = jnp.concatenate([stats[2 * g], stats[2 * g + 1]], axis=1)
        other = jnp.concatenate(
            [told[slot_of_near(place, STEPS[g], s), 4:8, :] for s in range(2)], axis=1
        )
        weight, delta = merge(this, other)
        grad_t = (turn(both(blocks[g], G0)) * weight).astype(BF16)
        grad_all[:, cols] = grad_t
        query_all[cols, :] = both(blocks[g], Q0)
        attended = (result[:, cols] * weight).T.astype(BF16)
        for s in range(2):
            outs[g][s, :HW, :] = attended[s * HW : (s + 1) * HW]
        for z in range(4):
            rows = slice(z * PAIR, (z + 1) * PAIR)
            d_probs = mm(both(blocks[z], V0), grad_t)
            grads[rows, cols] = (kept[rows, cols].astype(F32) * (d_probs - delta)).astype(BF16)
    for z in range(4):
        rows = slice(z * PAIR, (z + 1) * PAIR)
        d_values = mm_nt(kept[rows, :], grad_all[...]).astype(BF16)
        d_keys = (mm(grads[rows, :], query_all[...]) * SCALE).astype(BF16)
        for s in range(2):
            outs[z][s, 2 * HW : 3 * HW, :] = d_keys[s * HW : (s + 1) * HW]
            outs[z][s, 3 * HW :, :] = d_values[s * HW : (s + 1) * HW]
    keys_t = jnp.concatenate([turn(both(block, K0)).astype(BF16) for block in blocks], axis=1)
    for g in range(4):
        cols = slice(g * PAIR, (g + 1) * PAIR)
        d_query = (mm(keys_t, grads[:, cols]) * SCALE).T.astype(BF16)
        for s in range(2):
            outs[g][s, HW : 2 * HW, :] = d_query[s * HW : (s + 1) * HW]


def near_backward(place, blocks, kept, result, stats, told):
    return pl.pallas_call(
        near_backward_kernel,
        in_specs=[SM] + [VM] * 8,
        out_specs=[VM] * 4,
        out_shape=[jax.ShapeDtypeStruct((2, 4 * HW, DH), BF16)] * 4,
        scratch_shapes=[
            pltpu.VMEM((TOKENS, TOKENS), BF16),
            pltpu.VMEM((DH, TOKENS), BF16),
            pltpu.VMEM((TOKENS, DH), BF16),
        ],
        compiler_params=params(),
        cost_estimate=cost(8 * TOKENS * TOKENS * DH, 5_000_000),
        name="near_backward",
    )(place, *blocks, kept, result, stats, told)


def far_backward_kernel(
    place, mine, past, kept, result, sent, told, own, back, keys_t, values, dk, dv, grads
):
    for j in range(GROUP):
        keys_t[:, j * HW : (j + 1) * HW] = turn(past[j, :HW, :]).astype(BF16)
        keys_t[:, (GROUP + j) * HW : (GROUP + j + 1) * HW] = turn(
            mine[j, K0 : K0 + HW, :]
        ).astype(BF16)
        values[j * HW : (j + 1) * HW, :] = past[j, HW : 2 * HW, :]
        values[(GROUP + j) * HW : (GROUP + j + 1) * HW, :] = mine[j, V0 : V0 + HW, :]
    dk[...] = jnp.zeros_like(dk)
    dv[...] = jnp.zeros_like(dv)
    for p in range(GROUP // 2):
        query = jnp.concatenate([mine[2 * p, :HW, :], mine[2 * p + 1, :HW, :]], axis=0)
        grad_t = jnp.concatenate(
            [turn(mine[2 * p, G0 : G0 + HW, :]), turn(mine[2 * p + 1, G0 : G0 + HW, :])], axis=1
        )
        this = jnp.concatenate([sent[2 * p, 4:8, :], sent[2 * p + 1, 4:8, :]], axis=1)
        other = jnp.concatenate([told[2 * p, 0:4, :], told[2 * p + 1, 0:4, :]], axis=1)
        weight, delta = merge(this, other)
        grad_t = (grad_t * weight).astype(BF16)
        at = p * PAIR
        attended = (result[:, at : at + PAIR] * weight).T.astype(BF16)
        for lo, size in ((0, 384), (384, 384), (768, 384)):
            rows = slice(lo, lo + size)
            spot = slice(at + lo, at + lo + size)
            d_probs = mm(values[spot, :], grad_t)
            block = kept[p, rows, :]
            d_scores = (block.astype(F32) * (d_probs - delta)).astype(BF16)
            grads[rows, :] = d_scores
            dv[spot, :] += mm_nt(block, grad_t)
            dk[spot, :] += mm(d_scores, query)
        d_query = (mm(keys_t[:, at : at + KEYS], grads[...]) * SCALE).T.astype(BF16)
        for i in range(2):
            own[2 * p + i, :HW, :] = attended[i * HW : (i + 1) * HW]
            own[2 * p + i, HW : 2 * HW, :] = d_query[i * HW : (i + 1) * HW]
    for j in range(GROUP):
        early = slice(j * HW, (j + 1) * HW)
        late = slice((GROUP + j) * HW, (GROUP + j + 1) * HW)
        back[j, :HW, :] = (dk[early, :] * SCALE).astype(BF16)
        back[j, HW:, :] = dv[early, :].astype(BF16)
        own[j, 2 * HW : 3 * HW, :] = (dk[late, :] * SCALE).astype(BF16)
        own[j, 3 * HW :, :] = dv[late, :].astype(BF16)


def far_backward(place, mine, past, kept, result, sent, told):
    return pl.pallas_call(
        far_backward_kernel,
        in_specs=[SM] + [VM] * 6,
        out_specs=[VM, VM],
        out_shape=[
            jax.ShapeDtypeStruct((GROUP, 4 * HW, DH), BF16),
            jax.ShapeDtypeStruct((GROUP, 2 * HW, DH), BF16),
        ],
        scratch_shapes=[
            pltpu.VMEM((DH, 2 * GROUP * HW), BF16),
            pltpu.VMEM((2 * GROUP * HW, DH), BF16),
            pltpu.VMEM((2 * GROUP * HW, DH), F32),
            pltpu.VMEM((2 * GROUP * HW, DH), F32),
            pltpu.VMEM((KEYS, PAIR), BF16),
        ],
        compiler_params=params(),
        cost_estimate=cost(32 * KEYS * PAIR * DH, 6_000_000),
        name="far_backward",
    )(place, mine, past, kept, result, sent, told)


def add_back_kernel(own, back, out):
    for j in range(GROUP):
        out[j, 2 * HW : 4 * HW, :] = (
            own[j, 2 * HW : 4 * HW, :].astype(F32) + back[j].astype(F32)
        ).astype(BF16)


def add_back(own, back):
    return pl.pallas_call(
        add_back_kernel,
        in_specs=[VM] * 2,
        out_specs=VM,
        out_shape=jax.ShapeDtypeStruct((GROUP, 4 * HW, DH), BF16),
        input_output_aliases={0: 0},
        compiler_params=params(),
        cost_estimate=cost(GROUP * 2 * HW * DH, 2_500_000),
        name="add_back",
    )(own, back)


def unproject_kernel(
    place, near0, near1, near2, near3, far, w_qkv, w_out, own, other, close, wq, wk, wv, wo, sems
):
    groups = weight_copies(place, w_qkv, w_out, ((0, wq), (1, wk), (2, wv), (3, wo)), sems)
    start_all(groups)
    for step, near in zip(STEPS, (near0, near1, near2, near3)):
        close[head_here(place, step)] = near[...]
    parts = []
    for part in range(4):
        rows = slice(part * HW, (part + 1) * HW)
        pieces = []
        for h in range(HALF):
            slot = slot_of_head(place, h)
            away = jnp.concatenate([far[slot, 0, rows, :], far[slot, 1, rows, :]], axis=0)
            here = jnp.concatenate([close[h, 0, rows, :], close[h, 1, rows, :]], axis=0)
            pieces.append((away.astype(F32) + here.astype(F32)).astype(BF16))
        parts.append(jnp.concatenate(pieces, axis=1))
    wait_all(groups[0])
    total = mm_nt(parts[1], wq[...])
    wait_all(groups[1])
    total = total + mm_nt(parts[2], wk[...])
    wait_all(groups[2])
    total = total + mm_nt(parts[3], wv[...])
    wait_all(groups[3])
    mixed = mm(parts[0], wo[...])
    own[0] = mixed[:HW]
    own[1] = total[:HW]
    other[0] = mixed[HW:].astype(BF16)
    other[1] = total[HW:].astype(BF16)


def unproject(place, blocks, far, w_qkv, w_out):
    return pl.pallas_call(
        unproject_kernel,
        in_specs=[SM] + [VM] * 5 + [ANY] * 2,
        out_specs=[VM, VM],
        scratch_shapes=[pltpu.VMEM((HALF, 2, 4 * HW, DH), BF16)]
        + [pltpu.VMEM((D, HALF * DH), BF16)] * 3
        + [pltpu.VMEM((HALF * DH, D), BF16), pltpu.SemaphoreType.DMA((4 * PIECES,))],
        out_shape=[jax.ShapeDtypeStruct((2, HW, D), F32), jax.ShapeDtypeStruct((2, HW, D), BF16)],
        compiler_params=pltpu.CompilerParams(vmem_limit_bytes=50 * 1024 * 1024),
        cost_estimate=cost(2 * PAIR * D * 4 * HALF * DH, 8_000_000),
        name="unproject",
    )(place, *blocks, far, w_qkv, w_out)


def finish_kernel(tokens, cot, gain, own, other, mixed, out):
    x = tokens[...].astype(F32)
    mixed[...] = (x + (own[0] + other[0].astype(F32))).astype(BF16)
    rinv = lax.rsqrt(jnp.mean(x * x, axis=-1, keepdims=True) + EPS)
    scaled = (own[1] + other[1].astype(F32)) * gain[...]
    mean = jnp.mean(scaled * x, axis=-1, keepdims=True)
    grad = rinv * scaled - x * (rinv * rinv * rinv * mean)
    out[...] = (cot[...].astype(F32) + grad).astype(BF16)


def finish(tokens, cot, gain, own, other):
    return pl.pallas_call(
        finish_kernel,
        in_specs=[VM] * 5,
        out_specs=[VM] * 2,
        out_shape=[jax.ShapeDtypeStruct((HW, D), BF16)] * 2,
        compiler_params=params(),
        cost_estimate=cost(HW * D * 10, 3_000_000),
        name="finish",
    )(tokens, cot, gain, own, other)


LANE = ("x", "zl")
SAME_HEAD = [
    [(x * 2 + zl) * 4 + (h + 4 - x) % 4 for x in range(4) for zl in range(2)] for h in range(4)
]


def swap(value):
    return lax.ppermute(value, "core", [(0, 1), (1, 0)])


def turn_ring(value, steps):
    return lax.ppermute(value, "zh", [(i, (i + steps) % 4) for i in range(4)])


def all_round(blocks, sign):
    return [blocks[0]] + [turn_ring(blocks[g], sign * STEPS[g]) for g in (1, 2, 3)]


def exchange(value, axes, groups=None):
    return lax.all_to_all(value, axes, 0, 0, axis_index_groups=groups, tiled=True)


def exchange_alone(value, go):
    return lax.cond(go, lambda v: exchange(v, LANE), jnp.zeros_like, value)


def per_device(tokens, gain, w_qkv, w_out, window, valid, cotangent):
    rows = lax.axis_size("y")
    place = jnp.stack(
        [lax.axis_index(axis) for axis in ("core", "x", "zh")]
    ).astype(jnp.int32)
    go = window[0] > 0
    tokens = tokens.reshape(HW, D)
    cot = cotangent.reshape(HW, D)
    other_tokens = swap(tokens)
    other_cot = swap(cot)
    gain = gain.reshape(1, D)
    weights = stage(place, w_qkv, w_out)
    packed, *blocks = project(
        place, valid, tokens, other_tokens, cot, other_cot, gain, weights
    )
    blocks = all_round(blocks, 1)
    mine = exchange(packed.reshape(2 * HALF, ROWS, DH), LANE)
    past = lax.ppermute(mine[:, K0:, :], "y", [(i, i + 1) for i in range(rows - 1)])
    near_kept, near_result, close = near_forward(*blocks)
    sent, far_kept, far_result = far_forward(place, window, mine, past, close)
    told = exchange(sent, ("x", "zl", "zh"), SAME_HEAD)
    own, back = far_backward(place, mine, past, far_kept, far_result, sent, told)
    back = lax.ppermute(back, "y", [(i + 1, i) for i in range(rows - 1)])
    returned = near_backward(place, blocks, near_kept, near_result, close, told)
    own, returned = lax.optimization_barrier((own, returned))
    returned = all_round(returned, -1)
    own = add_back(own, back)
    far = exchange_alone(own, go).reshape(HALF, 2, 4 * HW, DH)
    out_own, out_other = unproject(place, returned, far, w_qkv, w_out)
    mixed, d_tokens = finish(tokens, cot, gain, out_own, swap(out_other))
    return mixed.reshape(1, 1, HW, D), d_tokens.reshape(1, 1, HW, D)


def solution(mesh):
    grid = Mesh(mesh.devices.reshape(4, 4, 2, 4, 2), ("y", "x", "zl", "zh", "core"))
    frames, cams = ("y", "x", "zl"), ("zh", "core")
    split = P(frames, cams, None, None)
    return jax.shard_map(
        per_device,
        mesh=grid,
        in_specs=(split, P(), P(), P(), P(), P(frames), split),
        out_specs=(split, split),
        check_vma=False,
    )
```

```python
import math

import jax
import jax.numpy as jnp
from jax import lax
from jax.experimental import pallas as pl
from jax.experimental.pallas import tpu as pltpu
from jax.sharding import Mesh
from jax.sharding import PartitionSpec as P

D = 1024
H = 8
DH = 128
HW = 128
WIN = 8
EPS = 1e-05

HALF = H // 2
PAIR = 2 * HW
GROUP = 8
SCALE = DH ** (-0.5)
SCALE2 = SCALE * math.log2(math.e)
FLOOR = -3.0e38
F32 = jnp.float32
BF16 = jnp.bfloat16
NT = (((1,), (1,)), ((), ()))
VMEM_LIMIT = 20 * 1024 * 1024
STAGE_LIMIT = 48 * 1024 * 1024

Q0, G0, K0, V0, OK0, ROWS = 0, 128, 256, 384, 512, 528
TOKENS = 8 * HW
KEYS = (WIN + 1) * HW


def params(**kw):
    return pltpu.CompilerParams(vmem_limit_bytes=VMEM_LIMIT, **kw)


def mm(a, b):
    return jnp.dot(a, b, preferred_element_type=F32)


def mm_nt(a, b):
    return lax.dot_general(a, b, NT, preferred_element_type=F32)


def turn(a):
    return a.astype(F32).T


VM = pl.BlockSpec(memory_space=pltpu.VMEM)
SM = pl.BlockSpec(memory_space=pltpu.SMEM)
ANY = pl.BlockSpec(memory_space=pltpu.HBM)


def cost(flops, size, exps=0):
    return pl.CostEstimate(flops=flops, bytes_accessed=size, transcendentals=exps)


PIECES = 4


def weight_copies(place, w_qkv, w_out, targets, sems):
    begin = pl.multiple_of(place[0] * HALF * DH, HALF * DH)
    groups = []
    for part, target in targets:
        size = target.shape[0] // PIECES
        group = []
        for n in range(PIECES):
            if part < 3:
                columns = pl.ds(pl.multiple_of(begin + part * D, HALF * DH), HALF * DH)
                source = w_qkv.at[pl.ds(n * size, size), columns]
            else:
                source = w_out.at[pl.ds(pl.multiple_of(begin + n * size, size), size), :]
            spot = target.at[pl.ds(n * size, size), :]
            group.append(pltpu.make_async_copy(source, spot, sems.at[part * PIECES + n]))
        groups.append(group)
    return groups


def start_all(groups):
    for group in groups:
        for copy in group:
            copy.start()


def wait_all(group):
    for copy in group:
        copy.wait()


def stage_kernel(place, w_qkv, w_out, wq, wk, wv, wo, sems):
    groups = weight_copies(place, w_qkv, w_out, ((0, wq), (1, wk), (2, wv), (3, wo)), sems)
    start_all(groups)
    for group in groups:
        wait_all(group)


def stage(place, w_qkv, w_out):
    return pl.pallas_call(
        stage_kernel,
        in_specs=[SM, ANY, ANY],
        out_specs=[VM] * 4,
        out_shape=[jax.ShapeDtypeStruct((D, HALF * DH), BF16)] * 3
        + [jax.ShapeDtypeStruct((HALF * DH, D), BF16)],
        scratch_shapes=[pltpu.SemaphoreType.DMA((4 * PIECES,))],
        compiler_params=pltpu.CompilerParams(vmem_limit_bytes=STAGE_LIMIT),
        cost_estimate=cost(0, 9_000_000),
        name="stage",
    )(place, w_qkv, w_out)


STEPS = (0, 2, 1, 3)


def slot_of_head(place, h):
    return lax.rem(h + HALF - place[2], HALF)


def head_here(place, step=0):
    return lax.rem(place[1] + place[2] + step, HALF)


def project_kernel(
    place, valid, own, other, cot_own, cot_other, gain, wq, wk, wv, wo, packed, near0, near1, near2, near3
):
    x = jnp.concatenate([own[...], other[...]], axis=0).astype(F32)
    rinv = lax.rsqrt(jnp.mean(x * x, axis=-1, keepdims=True) + EPS)
    normed = (x * rinv * gain[...]).astype(BF16)
    cot = jnp.concatenate([cot_own[...], cot_other[...]], axis=0)
    flags = jnp.full((ROWS - OK0, DH), valid[0], jnp.int32).astype(F32).astype(BF16)
    for row in (Q0, K0, V0, G0):
        if row == G0:
            got = mm_nt(cot, wo[...]).astype(BF16)
        else:
            got = mm(normed, {Q0: wq, K0: wk, V0: wv}[row][...]).astype(BF16)
        for h in range(HALF):
            for s in range(2):
                packed[slot_of_head(place, h), s, row : row + HW, :] = (
                    got[s * HW : (s + 1) * HW, h * DH : (h + 1) * DH]
                )
    for h in range(HALF):
        for s in range(2):
            packed[h, s, OK0:ROWS, :] = flags
    for step, near in zip(STEPS, (near0, near1, near2, near3)):
        slot = lax.rem(place[1] + step, HALF)
        for s in range(2):
            near[s] = packed[slot, s, :OK0, :]


def project(place, valid, own, other, cot_own, cot_other, gain, weights):
    return pl.pallas_call(
        project_kernel,
        in_specs=[SM, SM] + [VM] * 9,
        out_specs=[VM] * 5,
        out_shape=[jax.ShapeDtypeStruct((HALF, 2, ROWS, DH), BF16)]
        + [jax.ShapeDtypeStruct((2, OK0, DH), BF16)] * 4,
        compiler_params=params(),
        cost_estimate=cost(2 * PAIR * D * 4 * HALF * DH, 7_000_000),
        name="project",
    )(place, valid, own, other, cot_own, cot_other, gain, *weights)


def both(block, row):
    return jnp.concatenate([block[0, row : row + HW, :], block[1, row : row + HW, :]], axis=0)


def near_forward_kernel(near0, near1, near2, near3, kept, result, stats, scores):
    blocks = (near0, near1, near2, near3)
    turned = [turn(both(block, V0)).astype(BF16) for block in blocks]
    query = jnp.concatenate([both(block, Q0) for block in blocks], axis=0)
    peak = jnp.full((1, TOKENS), -jnp.inf, F32)
    for b in range(8):
        keys = blocks[b // 2][b % 2, K0 : K0 + HW, :]
        block = mm_nt(keys, query)
        scores[b * HW : (b + 1) * HW, :] = block
        peak = jnp.maximum(peak, jnp.max(block, axis=0, keepdims=True))
    peak = peak * SCALE2
    total = jnp.zeros((1, TOKENS), F32)
    for b in range(32):
        rows = slice(b * 32, (b + 1) * 32)
        block = jnp.exp2(scores[rows, :] * SCALE2 - peak)
        total = total + jnp.sum(block, axis=0, keepdims=True)
        kept[rows, :] = block.astype(BF16)
    turned = jnp.concatenate(turned, axis=1)
    for g in range(4):
        cols = slice(g * PAIR, (g + 1) * PAIR)
        got = mm(turned, kept[:, cols])
        result[:, cols] = got
        delta = jnp.sum(got * turn(both(blocks[g], G0)), axis=0, keepdims=True)
        told = jnp.concatenate(
            [peak[:, cols], total[:, cols], delta, jnp.zeros((1, PAIR), F32)], axis=0
        )
        stats[2 * g] = told[:, :HW]
        stats[2 * g + 1] = told[:, HW:]


def near_forward(*blocks):
    return pl.pallas_call(
        near_forward_kernel,
        in_specs=[VM] * 4,
        out_specs=[VM] * 3,
        out_shape=[
            jax.ShapeDtypeStruct((TOKENS, TOKENS), BF16),
            jax.ShapeDtypeStruct((DH, TOKENS), F32),
            jax.ShapeDtypeStruct((8, 4, HW), F32),
        ],
        scratch_shapes=[pltpu.VMEM((TOKENS, TOKENS), F32)],
        compiler_params=params(),
        cost_estimate=cost(80 * TOKENS * TOKENS * DH, 4_000_000, TOKENS * TOKENS),
        name="near_forward",
    )(*blocks)


def slot_of_near(place, step, s):
    return lax.rem(place[1] + step, 4) * 2 + s


def far_forward_kernel(place, win, mine, past, close, told, kept, result, values_t, scores):
    width = win[place[0] * HALF + head_here(place)]
    for g in range(4):
        for s in range(2):
            told[slot_of_near(place, STEPS[g], s), 0:4, :] = close[2 * g + s]
    for j in range(GROUP):
        values_t[:, j * HW : (j + 1) * HW] = turn(past[j, HW : 2 * HW, :]).astype(BF16)
        values_t[:, (GROUP + j) * HW : (GROUP + j + 1) * HW] = turn(
            mine[j, V0 : V0 + HW, :]
        ).astype(BF16)
    for p in range(GROUP // 2):
        query = jnp.concatenate([mine[2 * p, :HW, :], mine[2 * p + 1, :HW, :]], axis=0)
        grad_t = jnp.concatenate(
            [turn(mine[2 * p, G0 : G0 + HW, :]), turn(mine[2 * p + 1, G0 : G0 + HW, :])], axis=1
        )
        peak = jnp.full((1, PAIR), -jnp.inf, F32)
        for b in range(WIN + 1):
            j = 2 * p + b
            if j < GROUP:
                keys = past[j, :HW, :]
                flag = past[j, 2 * HW : 2 * HW + 1, :].astype(F32)
            else:
                keys = mine[j - GROUP, K0 : K0 + HW, :]
                flag = mine[j - GROUP, OK0 : OK0 + 1, :].astype(F32)
            lower = jnp.where((flag > 0.5) & (b >= WIN - width) & (b < WIN), 0.0, -jnp.inf)
            upper = jnp.where((flag > 0.5) & (b >= WIN + 1 - width), 0.0, -jnp.inf)
            bias = jnp.concatenate([lower, upper], axis=1)
            block = mm_nt(keys, query) + bias
            scores[b * HW : (b + 1) * HW, :] = block
            peak = jnp.maximum(peak, jnp.max(block, axis=0, keepdims=True))
        peak = jnp.maximum(peak * SCALE2, FLOOR)
        total = jnp.zeros((1, PAIR), F32)
        for b in range(WIN + 1):
            block = jnp.exp2(scores[b * HW : (b + 1) * HW, :] * SCALE2 - peak)
            total = total + jnp.sum(block, axis=0, keepdims=True)
            kept[p, b * HW : (b + 1) * HW, :] = block.astype(BF16)
        got = mm(values_t[:, p * PAIR : p * PAIR + KEYS], kept[p])
        result[:, p * PAIR : (p + 1) * PAIR] = got
        delta = jnp.sum(got * grad_t, axis=0, keepdims=True)
        stats = jnp.concatenate([peak, total, delta, jnp.zeros((1, PAIR), F32)], axis=0)
        told[2 * p, 4:8, :] = stats[:, :HW]
        told[2 * p + 1, 4:8, :] = stats[:, HW:]


def far_forward(place, window, mine, past, close):
    return pl.pallas_call(
        far_forward_kernel,
        in_specs=[SM, SM, VM, VM, VM],
        out_specs=[VM] * 3,
        out_shape=[
            jax.ShapeDtypeStruct((GROUP, 8, HW), F32),
            jax.ShapeDtypeStruct((GROUP // 2, KEYS, PAIR), BF16),
            jax.ShapeDtypeStruct((DH, GROUP * HW), F32),
        ],
        scratch_shapes=[
            pltpu.VMEM((DH, 2 * GROUP * HW), BF16),
            pltpu.VMEM((KEYS, PAIR), F32),
        ],
        compiler_params=params(),
        cost_estimate=cost(16 * KEYS * PAIR * DH, 5_000_000, 4 * KEYS * PAIR),
        name="far_forward",
    )(place, window, mine, past, close)


def merge(this, other):
    top = jnp.maximum(this[0:1], other[0:1])
    here = jnp.exp2(this[0:1] - top)
    there = jnp.exp2(other[0:1] - top)
    inverse = 1.0 / (here * this[1:2] + there * other[1:2])
    here = here * inverse
    delta = here * this[2:3] + there * inverse * other[2:3]
    return here, here * delta


def near_backward_kernel(
    place, near0, near1, near2, near3, kept, result, stats, told,
    back0, back1, back2, back3, grads, grad_all, query_all,
):
    blocks = (near0, near1, near2, near3)
    outs = (back0, back1, back2, back3)
    for g in range(4):
        cols = slice(g * PAIR, (g + 1) * PAIR)
        this = jnp.concatenate([stats[2 * g], stats[2 * g + 1]], axis=1)
        other = jnp.concatenate(
            [told[slot_of_near(place, STEPS[g], s), 4:8, :] for s in range(2)], axis=1
        )
        weight, delta = merge(this, other)
        grad_t = (turn(both(blocks[g], G0)) * weight).astype(BF16)
        grad_all[:, cols] = grad_t
        query_all[cols, :] = both(blocks[g], Q0)
        attended = (result[:, cols] * weight).T.astype(BF16)
        for s in range(2):
            outs[g][s, :HW, :] = attended[s * HW : (s + 1) * HW]
        for z in range(4):
            rows = slice(z * PAIR, (z + 1) * PAIR)
            d_probs = mm(both(blocks[z], V0), grad_t)
            grads[rows, cols] = (kept[rows, cols].astype(F32) * (d_probs - delta)).astype(BF16)
    for z in range(4):
        rows = slice(z * PAIR, (z + 1) * PAIR)
        d_values = mm_nt(kept[rows, :], grad_all[...]).astype(BF16)
        d_keys = (mm(grads[rows, :], query_all[...]) * SCALE).astype(BF16)
        for s in range(2):
            outs[z][s, 2 * HW : 3 * HW, :] = d_keys[s * HW : (s + 1) * HW]
            outs[z][s, 3 * HW :, :] = d_values[s * HW : (s + 1) * HW]
    keys_t = jnp.concatenate([turn(both(block, K0)).astype(BF16) for block in blocks], axis=1)
    for g in range(4):
        cols = slice(g * PAIR, (g + 1) * PAIR)
        d_query = (mm(keys_t, grads[:, cols]) * SCALE).T.astype(BF16)
        for s in range(2):
            outs[g][s, HW : 2 * HW, :] = d_query[s * HW : (s + 1) * HW]


def near_backward(place, blocks, kept, result, stats, told):
    return pl.pallas_call(
        near_backward_kernel,
        in_specs=[SM] + [VM] * 8,
        out_specs=[VM] * 4,
        out_shape=[jax.ShapeDtypeStruct((2, 4 * HW, DH), BF16)] * 4,
        scratch_shapes=[
            pltpu.VMEM((TOKENS, TOKENS), BF16),
            pltpu.VMEM((DH, TOKENS), BF16),
            pltpu.VMEM((TOKENS, DH), BF16),
        ],
        compiler_params=params(),
        cost_estimate=cost(8 * TOKENS * TOKENS * DH, 5_000_000),
        name="near_backward",
    )(place, *blocks, kept, result, stats, told)


def far_backward_kernel(
    place, mine, past, kept, result, sent, told, own, back, keys_t, values, dk, dv, grads
):
    for j in range(GROUP):
        keys_t[:, j * HW : (j + 1) * HW] = turn(past[j, :HW, :]).astype(BF16)
        keys_t[:, (GROUP + j) * HW : (GROUP + j + 1) * HW] = turn(
            mine[j, K0 : K0 + HW, :]
        ).astype(BF16)
        values[j * HW : (j + 1) * HW, :] = past[j, HW : 2 * HW, :]
        values[(GROUP + j) * HW : (GROUP + j + 1) * HW, :] = mine[j, V0 : V0 + HW, :]
    dk[...] = jnp.zeros_like(dk)
    dv[...] = jnp.zeros_like(dv)
    for p in range(GROUP // 2):
        query = jnp.concatenate([mine[2 * p, :HW, :], mine[2 * p + 1, :HW, :]], axis=0)
        grad_t = jnp.concatenate(
            [turn(mine[2 * p, G0 : G0 + HW, :]), turn(mine[2 * p + 1, G0 : G0 + HW, :])], axis=1
        )
        this = jnp.concatenate([sent[2 * p, 4:8, :], sent[2 * p + 1, 4:8, :]], axis=1)
        other = jnp.concatenate([told[2 * p, 0:4, :], told[2 * p + 1, 0:4, :]], axis=1)
        weight, delta = merge(this, other)
        grad_t = (grad_t * weight).astype(BF16)
        at = p * PAIR
        attended = (result[:, at : at + PAIR] * weight).T.astype(BF16)
        for lo, size in ((0, 384), (384, 384), (768, 384)):
            rows = slice(lo, lo + size)
            spot = slice(at + lo, at + lo + size)
            d_probs = mm(values[spot, :], grad_t)
            block = kept[p, rows, :]
            d_scores = (block.astype(F32) * (d_probs - delta)).astype(BF16)
            grads[rows, :] = d_scores
            dv[spot, :] += mm_nt(block, grad_t)
            dk[spot, :] += mm(d_scores, query)
        d_query = (mm(keys_t[:, at : at + KEYS], grads[...]) * SCALE).T.astype(BF16)
        for i in range(2):
            own[2 * p + i, :HW, :] = attended[i * HW : (i + 1) * HW]
            own[2 * p + i, HW : 2 * HW, :] = d_query[i * HW : (i + 1) * HW]
    for j in range(GROUP):
        early = slice(j * HW, (j + 1) * HW)
        late = slice((GROUP + j) * HW, (GROUP + j + 1) * HW)
        back[j, :HW, :] = (dk[early, :] * SCALE).astype(BF16)
        back[j, HW:, :] = dv[early, :].astype(BF16)
        own[j, 2 * HW : 3 * HW, :] = (dk[late, :] * SCALE).astype(BF16)
        own[j, 3 * HW :, :] = dv[late, :].astype(BF16)


def far_backward(place, mine, past, kept, result, sent, told):
    return pl.pallas_call(
        far_backward_kernel,
        in_specs=[SM] + [VM] * 6,
        out_specs=[VM, VM],
        out_shape=[
            jax.ShapeDtypeStruct((GROUP, 4 * HW, DH), BF16),
            jax.ShapeDtypeStruct((GROUP, 2 * HW, DH), BF16),
        ],
        scratch_shapes=[
            pltpu.VMEM((DH, 2 * GROUP * HW), BF16),
            pltpu.VMEM((2 * GROUP * HW, DH), BF16),
            pltpu.VMEM((2 * GROUP * HW, DH), F32),
            pltpu.VMEM((2 * GROUP * HW, DH), F32),
            pltpu.VMEM((KEYS, PAIR), BF16),
        ],
        compiler_params=params(),
        cost_estimate=cost(32 * KEYS * PAIR * DH, 6_000_000),
        name="far_backward",
    )(place, mine, past, kept, result, sent, told)


def add_back_kernel(own, back, out):
    for j in range(GROUP):
        out[j, 2 * HW : 4 * HW, :] = (
            own[j, 2 * HW : 4 * HW, :].astype(F32) + back[j].astype(F32)
        ).astype(BF16)


def add_back(own, back):
    return pl.pallas_call(
        add_back_kernel,
        in_specs=[VM] * 2,
        out_specs=VM,
        out_shape=jax.ShapeDtypeStruct((GROUP, 4 * HW, DH), BF16),
        input_output_aliases={0: 0},
        compiler_params=params(),
        cost_estimate=cost(GROUP * 2 * HW * DH, 2_500_000),
        name="add_back",
    )(own, back)


def unproject_kernel(
    place, near0, near1, near2, near3, far, w_qkv, w_out, own, other, close, wq, wk, wv, wo, sems
):
    groups = weight_copies(place, w_qkv, w_out, ((0, wq), (1, wk), (2, wv), (3, wo)), sems)
    start_all(groups)
    for step, near in zip(STEPS, (near0, near1, near2, near3)):
        close[head_here(place, step)] = near[...]
    parts = []
    for part in range(4):
        rows = slice(part * HW, (part + 1) * HW)
        pieces = []
        for h in range(HALF):
            slot = slot_of_head(place, h)
            away = jnp.concatenate([far[slot, 0, rows, :], far[slot, 1, rows, :]], axis=0)
            here = jnp.concatenate([close[h, 0, rows, :], close[h, 1, rows, :]], axis=0)
            pieces.append((away.astype(F32) + here.astype(F32)).astype(BF16))
        parts.append(jnp.concatenate(pieces, axis=1))
    wait_all(groups[0])
    total = mm_nt(parts[1], wq[...])
    wait_all(groups[1])
    total = total + mm_nt(parts[2], wk[...])
    wait_all(groups[2])
    total = total + mm_nt(parts[3], wv[...])
    wait_all(groups[3])
    mixed = mm(parts[0], wo[...])
    own[0] = mixed[:HW]
    own[1] = total[:HW]
    other[0] = mixed[HW:].astype(BF16)
    other[1] = total[HW:].astype(BF16)


def unproject(place, blocks, far, w_qkv, w_out):
    return pl.pallas_call(
        unproject_kernel,
        in_specs=[SM] + [VM] * 5 + [ANY] * 2,
        out_specs=[VM, VM],
        scratch_shapes=[pltpu.VMEM((HALF, 2, 4 * HW, DH), BF16)]
        + [pltpu.VMEM((D, HALF * DH), BF16)] * 3
        + [pltpu.VMEM((HALF * DH, D), BF16), pltpu.SemaphoreType.DMA((4 * PIECES,))],
        out_shape=[jax.ShapeDtypeStruct((2, HW, D), F32), jax.ShapeDtypeStruct((2, HW, D), BF16)],
        compiler_params=pltpu.CompilerParams(vmem_limit_bytes=50 * 1024 * 1024),
        cost_estimate=cost(2 * PAIR * D * 4 * HALF * DH, 8_000_000),
        name="unproject",
    )(place, *blocks, far, w_qkv, w_out)


def finish_kernel(tokens, cot, gain, own, other, mixed, out):
    x = tokens[...].astype(F32)
    mixed[...] = (x + (own[0] + other[0].astype(F32))).astype(BF16)
    rinv = lax.rsqrt(jnp.mean(x * x, axis=-1, keepdims=True) + EPS)
    scaled = (own[1] + other[1].astype(F32)) * gain[...]
    mean = jnp.mean(scaled * x, axis=-1, keepdims=True)
    grad = rinv * scaled - x * (rinv * rinv * rinv * mean)
    out[...] = (cot[...].astype(F32) + grad).astype(BF16)


def finish(tokens, cot, gain, own, other):
    return pl.pallas_call(
        finish_kernel,
        in_specs=[VM] * 5,
        out_specs=[VM] * 2,
        out_shape=[jax.ShapeDtypeStruct((HW, D), BF16)] * 2,
        compiler_params=params(),
        cost_estimate=cost(HW * D * 10, 3_000_000),
        name="finish",
    )(tokens, cot, gain, own, other)


LANE = ("x", "zl")
SAME_HEAD = [
    [(x * 2 + zl) * 4 + (h + 4 - x) % 4 for x in range(4) for zl in range(2)] for h in range(4)
]


def swap(value):
    return lax.ppermute(value, "core", [(0, 1), (1, 0)])


def turn_ring(value, steps):
    return lax.ppermute(value, "zh", [(i, (i + steps) % 4) for i in range(4)])


def all_round(blocks, sign):
    return [blocks[0]] + [turn_ring(blocks[g], sign * STEPS[g]) for g in (1, 2, 3)]


def exchange(value, axes, groups=None):
    return lax.all_to_all(value, axes, 0, 0, axis_index_groups=groups, tiled=True)


def exchange_alone(value, go):
    return lax.cond(go, lambda v: exchange(v, LANE), jnp.zeros_like, value)


def per_device(tokens, gain, w_qkv, w_out, window, valid, cotangent):
    rows = lax.axis_size("y")
    place = jnp.stack(
        [lax.axis_index(axis) for axis in ("core", "x", "zh")]
    ).astype(jnp.int32)
    go = window[0] > 0
    tokens = tokens.reshape(HW, D)
    cot = cotangent.reshape(HW, D)
    other_tokens = swap(tokens)
    other_cot = swap(cot)
    gain = gain.reshape(1, D)
    weights = stage(place, w_qkv, w_out)
    packed, *blocks = project(
        place, valid, tokens, other_tokens, cot, other_cot, gain, weights
    )
    blocks = all_round(blocks, 1)
    mine = exchange(packed.reshape(2 * HALF, ROWS, DH), LANE)
    past = lax.ppermute(mine[:, K0:, :], "y", [(i, i + 1) for i in range(rows - 1)])
    near_kept, near_result, close = near_forward(*blocks)
    sent, far_kept, far_result = far_forward(place, window, mine, past, close)
    told = exchange(sent, ("x", "zl", "zh"), SAME_HEAD)
    own, back = far_backward(place, mine, past, far_kept, far_result, sent, told)
    back = lax.ppermute(back, "y", [(i + 1, i) for i in range(rows - 1)])
    returned = near_backward(place, blocks, near_kept, near_result, close, told)
    own, returned = lax.optimization_barrier((own, returned))
    returned = all_round(returned, -1)
    own = add_back(own, back)
    far = exchange_alone(own, go).reshape(HALF, 2, 4 * HW, DH)
    out_own, out_other = unproject(place, returned, far, w_qkv, w_out)
    mixed, d_tokens = finish(tokens, cot, gain, out_own, swap(out_other))
    return mixed.reshape(1, 1, HW, D), d_tokens.reshape(1, 1, HW, D)


def solution(mesh):
    grid = Mesh(mesh.devices.reshape(4, 4, 2, 4, 2), ("y", "x", "zl", "zh", "core"))
    frames, cams = ("y", "x", "zl"), ("zh", "core")
    split = P(frames, cams, None, None)
    return jax.shard_map(
        per_device,
        mesh=grid,
        in_specs=(split, P(), P(), P(), P(), P(frames), split),
        out_specs=(split, split),
        check_vma=False,
    )
```

```python
import math

import jax
import jax.numpy as jnp
from jax import lax
from jax.experimental import pallas as pl
from jax.experimental.pallas import tpu as pltpu
from jax.sharding import Mesh
from jax.sharding import PartitionSpec as P

D = 1024
H = 8
DH = 128
HW = 128
WIN = 8
EPS = 1e-05

HALF = H // 2
PAIR = 2 * HW
GROUP = 8
SCALE = DH ** (-0.5)
SCALE2 = SCALE * math.log2(math.e)
FLOOR = -3.0e38
F32 = jnp.float32
BF16 = jnp.bfloat16
NT = (((1,), (1,)), ((), ()))
VMEM_LIMIT = 20 * 1024 * 1024
STAGE_LIMIT = 48 * 1024 * 1024

Q0, G0, K0, V0, OK0, ROWS = 0, 128, 256, 384, 512, 528
TOKENS = 8 * HW
KEYS = (WIN + 1) * HW


def params(**kw):
    return pltpu.CompilerParams(vmem_limit_bytes=VMEM_LIMIT, **kw)


def mm(a, b):
    return jnp.dot(a, b, preferred_element_type=F32)


def mm_nt(a, b):
    return lax.dot_general(a, b, NT, preferred_element_type=F32)


def turn(a):
    return a.astype(F32).T


VM = pl.BlockSpec(memory_space=pltpu.VMEM)
SM = pl.BlockSpec(memory_space=pltpu.SMEM)
ANY = pl.BlockSpec(memory_space=pltpu.HBM)


def cost(flops, size, exps=0):
    return pl.CostEstimate(flops=flops, bytes_accessed=size, transcendentals=exps)


PIECES = 4


def weight_copies(place, w_qkv, w_out, targets, sems):
    begin = pl.multiple_of(place[0] * HALF * DH, HALF * DH)
    groups = []
    for part, target in targets:
        size = target.shape[0] // PIECES
        group = []
        for n in range(PIECES):
            if part < 3:
                columns = pl.ds(pl.multiple_of(begin + part * D, HALF * DH), HALF * DH)
                source = w_qkv.at[pl.ds(n * size, size), columns]
            else:
                source = w_out.at[pl.ds(pl.multiple_of(begin + n * size, size), size), :]
            spot = target.at[pl.ds(n * size, size), :]
            group.append(pltpu.make_async_copy(source, spot, sems.at[part * PIECES + n]))
        groups.append(group)
    return groups


def start_all(groups):
    for group in groups:
        for copy in group:
            copy.start()


def wait_all(group):
    for copy in group:
        copy.wait()


def stage_kernel(place, w_qkv, w_out, wq, wk, wv, wo, sems):
    groups = weight_copies(place, w_qkv, w_out, ((0, wq), (1, wk), (2, wv), (3, wo)), sems)
    start_all(groups)
    for group in groups:
        wait_all(group)


def stage(place, w_qkv, w_out):
    return pl.pallas_call(
        stage_kernel,
        in_specs=[SM, ANY, ANY],
        out_specs=[VM] * 4,
        out_shape=[jax.ShapeDtypeStruct((D, HALF * DH), BF16)] * 3
        + [jax.ShapeDtypeStruct((HALF * DH, D), BF16)],
        scratch_shapes=[pltpu.SemaphoreType.DMA((4 * PIECES,))],
        compiler_params=pltpu.CompilerParams(vmem_limit_bytes=STAGE_LIMIT),
        cost_estimate=cost(0, 9_000_000),
        name="stage",
    )(place, w_qkv, w_out)


STEPS = (0, 2, 1, 3)


def slot_of_head(place, h):
    return lax.rem(h + HALF - place[2], HALF)


def head_here(place, step=0):
    return lax.rem(place[1] + place[2] + step, HALF)


def project_kernel(
    place, valid, own, other, cot_own, cot_other, gain, wq, wk, wv, wo, packed, near0, near1, near2, near3
):
    x = jnp.concatenate([own[...], other[...]], axis=0).astype(F32)
    rinv = lax.rsqrt(jnp.mean(x * x, axis=-1, keepdims=True) + EPS)
    normed = (x * rinv * gain[...]).astype(BF16)
    cot = jnp.concatenate([cot_own[...], cot_other[...]], axis=0)
    flags = jnp.full((ROWS - OK0, DH), valid[0], jnp.int32).astype(F32).astype(BF16)
    for row in (Q0, K0, V0, G0):
        if row == G0:
            got = mm_nt(cot, wo[...]).astype(BF16)
        else:
            got = mm(normed, {Q0: wq, K0: wk, V0: wv}[row][...]).astype(BF16)
        for h in range(HALF):
            for s in range(2):
                packed[slot_of_head(place, h), s, row : row + HW, :] = (
                    got[s * HW : (s + 1) * HW, h * DH : (h + 1) * DH]
                )
    for h in range(HALF):
        for s in range(2):
            packed[h, s, OK0:ROWS, :] = flags
    for step, near in zip(STEPS, (near0, near1, near2, near3)):
        slot = lax.rem(place[1] + step, HALF)
        for s in range(2):
            near[s] = packed[slot, s, :OK0, :]


def project(place, valid, own, other, cot_own, cot_other, gain, weights):
    return pl.pallas_call(
        project_kernel,
        in_specs=[SM, SM] + [VM] * 9,
        out_specs=[VM] * 5,
        out_shape=[jax.ShapeDtypeStruct((HALF, 2, ROWS, DH), BF16)]
        + [jax.ShapeDtypeStruct((2, OK0, DH), BF16)] * 4,
        compiler_params=params(),
        cost_estimate=cost(2 * PAIR * D * 4 * HALF * DH, 7_000_000),
        name="project",
    )(place, valid, own, other, cot_own, cot_other, gain, *weights)


def both(block, row):
    return jnp.concatenate([block[0, row : row + HW, :], block[1, row : row + HW, :]], axis=0)


def near_forward_kernel(near0, near1, near2, near3, kept, result, stats, scores):
    blocks = (near0, near1, near2, near3)
    turned = [turn(both(block, V0)).astype(BF16) for block in blocks]
    query = jnp.concatenate([both(block, Q0) for block in blocks], axis=0)
    peak = jnp.full((1, TOKENS), -jnp.inf, F32)
    for b in range(8):
        keys = blocks[b // 2][b % 2, K0 : K0 + HW, :]
        block = mm_nt(keys, query)
        scores[b * HW : (b + 1) * HW, :] = block
        peak = jnp.maximum(peak, jnp.max(block, axis=0, keepdims=True))
    peak = peak * SCALE2
    for b in range(32):
        rows = slice(b * 32, (b + 1) * 32)
        block = jnp.exp2(scores[rows, :] * SCALE2 - peak)
        kept[rows, :] = block.astype(BF16)
    turned = jnp.concatenate(turned, axis=1)
    for g in range(4):
        cols = slice(g * PAIR, (g + 1) * PAIR)
        got = mm(turned, kept[:, cols])
        total = mm(jnp.ones((8, TOKENS), BF16), kept[:, cols])[0:1]
        result[:, cols] = got
        delta = jnp.sum(got * turn(both(blocks[g], G0)), axis=0, keepdims=True)
        told = jnp.concatenate(
            [peak[:, cols], total, delta, jnp.zeros((1, PAIR), F32)], axis=0
        )
        stats[2 * g] = told[:, :HW]
        stats[2 * g + 1] = told[:, HW:]


def near_forward(*blocks):
    return pl.pallas_call(
        near_forward_kernel,
        in_specs=[VM] * 4,
        out_specs=[VM] * 3,
        out_shape=[
            jax.ShapeDtypeStruct((TOKENS, TOKENS), BF16),
            jax.ShapeDtypeStruct((DH, TOKENS), F32),
            jax.ShapeDtypeStruct((8, 4, HW), F32),
        ],
        scratch_shapes=[pltpu.VMEM((TOKENS, TOKENS), F32)],
        compiler_params=params(),
        cost_estimate=cost(80 * TOKENS * TOKENS * DH, 4_000_000, TOKENS * TOKENS),
        name="near_forward",
    )(*blocks)


def slot_of_near(place, step, s):
    return lax.rem(place[1] + step, 4) * 2 + s


def far_forward_kernel(place, win, mine, past, close, told, kept, result, values_t, scores):
    width = win[place[0] * HALF + head_here(place)]
    for g in range(4):
        for s in range(2):
            told[slot_of_near(place, STEPS[g], s), 0:4, :] = close[2 * g + s]
    for j in range(GROUP):
        values_t[:, j * HW : (j + 1) * HW] = turn(past[j, HW : 2 * HW, :]).astype(BF16)
        values_t[:, (GROUP + j) * HW : (GROUP + j + 1) * HW] = turn(
            mine[j, V0 : V0 + HW, :]
        ).astype(BF16)
    for p in range(GROUP // 2):
        query = jnp.concatenate([mine[2 * p, :HW, :], mine[2 * p + 1, :HW, :]], axis=0)
        grad_t = jnp.concatenate(
            [turn(mine[2 * p, G0 : G0 + HW, :]), turn(mine[2 * p + 1, G0 : G0 + HW, :])], axis=1
        )
        peak = jnp.full((1, PAIR), -jnp.inf, F32)
        for b in range(WIN + 1):
            j = 2 * p + b
            if j < GROUP:
                keys = past[j, :HW, :]
                flag = past[j, 2 * HW : 2 * HW + 1, :].astype(F32)
            else:
                keys = mine[j - GROUP, K0 : K0 + HW, :]
                flag = mine[j - GROUP, OK0 : OK0 + 1, :].astype(F32)
            lower = jnp.where((flag > 0.5) & (b >= WIN - width) & (b < WIN), 0.0, -jnp.inf)
            upper = jnp.where((flag > 0.5) & (b >= WIN + 1 - width), 0.0, -jnp.inf)
            bias = jnp.concatenate([lower, upper], axis=1)
            block = mm_nt(keys, query) + bias
            scores[b * HW : (b + 1) * HW, :] = block
            peak = jnp.maximum(peak, jnp.max(block, axis=0, keepdims=True))
        peak = jnp.maximum(peak * SCALE2, FLOOR)
        for b in range(WIN + 1):
            block = jnp.exp2(scores[b * HW : (b + 1) * HW, :] * SCALE2 - peak)
            kept[p, b * HW : (b + 1) * HW, :] = block.astype(BF16)
        got = mm(values_t[:, p * PAIR : p * PAIR + KEYS], kept[p])
        total = mm(jnp.ones((8, KEYS), BF16), kept[p])[0:1]
        result[:, p * PAIR : (p + 1) * PAIR] = got
        delta = jnp.sum(got * grad_t, axis=0, keepdims=True)
        stats = jnp.concatenate([peak, total, delta, jnp.zeros((1, PAIR), F32)], axis=0)
        told[2 * p, 4:8, :] = stats[:, :HW]
        told[2 * p + 1, 4:8, :] = stats[:, HW:]


def far_forward(place, window, mine, past, close):
    return pl.pallas_call(
        far_forward_kernel,
        in_specs=[SM, SM, VM, VM, VM],
        out_specs=[VM] * 3,
        out_shape=[
            jax.ShapeDtypeStruct((GROUP, 8, HW), F32),
            jax.ShapeDtypeStruct((GROUP // 2, KEYS, PAIR), BF16),
            jax.ShapeDtypeStruct((DH, GROUP * HW), F32),
        ],
        scratch_shapes=[
            pltpu.VMEM((DH, 2 * GROUP * HW), BF16),
            pltpu.VMEM((KEYS, PAIR), F32),
        ],
        compiler_params=params(),
        cost_estimate=cost(16 * KEYS * PAIR * DH, 5_000_000, 4 * KEYS * PAIR),
        name="far_forward",
    )(place, window, mine, past, close)


def merge(this, other):
    top = jnp.maximum(this[0:1], other[0:1])
    here = jnp.exp2(this[0:1] - top)
    there = jnp.exp2(other[0:1] - top)
    inverse = 1.0 / (here * this[1:2] + there * other[1:2])
    here = here * inverse
    delta = here * this[2:3] + there * inverse * other[2:3]
    return here, here * delta


def near_backward_kernel(
    place, near0, near1, near2, near3, kept, result, stats, told,
    back0, back1, back2, back3, grads, grad_all, query_all,
):
    blocks = (near0, near1, near2, near3)
    outs = (back0, back1, back2, back3)
    for g in range(4):
        cols = slice(g * PAIR, (g + 1) * PAIR)
        this = jnp.concatenate([stats[2 * g], stats[2 * g + 1]], axis=1)
        other = jnp.concatenate(
            [told[slot_of_near(place, STEPS[g], s), 4:8, :] for s in range(2)], axis=1
        )
        weight, delta = merge(this, other)
        grad_t = (turn(both(blocks[g], G0)) * weight).astype(BF16)
        grad_all[:, cols] = grad_t
        query_all[cols, :] = both(blocks[g], Q0)
        attended = (result[:, cols] * weight).T.astype(BF16)
        for s in range(2):
            outs[g][s, :HW, :] = attended[s * HW : (s + 1) * HW]
        for z in range(4):
            rows = slice(z * PAIR, (z + 1) * PAIR)
            d_probs = mm(both(blocks[z], V0), grad_t)
            grads[rows, cols] = (kept[rows, cols].astype(F32) * (d_probs - delta)).astype(BF16)
    for z in range(4):
        rows = slice(z * PAIR, (z + 1) * PAIR)
        d_values = mm_nt(kept[rows, :], grad_all[...]).astype(BF16)
        d_keys = (mm(grads[rows, :], query_all[...]) * SCALE).astype(BF16)
        for s in range(2):
            outs[z][s, 2 * HW : 3 * HW, :] = d_keys[s * HW : (s + 1) * HW]
            outs[z][s, 3 * HW :, :] = d_values[s * HW : (s + 1) * HW]
    keys_t = jnp.concatenate([turn(both(block, K0)).astype(BF16) for block in blocks], axis=1)
    for g in range(4):
        cols = slice(g * PAIR, (g + 1) * PAIR)
        d_query = (mm(keys_t, grads[:, cols]) * SCALE).T.astype(BF16)
        for s in range(2):
            outs[g][s, HW : 2 * HW, :] = d_query[s * HW : (s + 1) * HW]


def near_backward(place, blocks, kept, result, stats, told):
    return pl.pallas_call(
        near_backward_kernel,
        in_specs=[SM] + [VM] * 8,
        out_specs=[VM] * 4,
        out_shape=[jax.ShapeDtypeStruct((2, 4 * HW, DH), BF16)] * 4,
        scratch_shapes=[
            pltpu.VMEM((TOKENS, TOKENS), BF16),
            pltpu.VMEM((DH, TOKENS), BF16),
            pltpu.VMEM((TOKENS, DH), BF16),
        ],
        compiler_params=params(),
        cost_estimate=cost(8 * TOKENS * TOKENS * DH, 5_000_000),
        name="near_backward",
    )(place, *blocks, kept, result, stats, told)


def far_backward_kernel(
    place, mine, past, kept, result, sent, told, own, back, keys_t, values, dk, dv, grads
):
    for j in range(GROUP):
        keys_t[:, j * HW : (j + 1) * HW] = turn(past[j, :HW, :]).astype(BF16)
        keys_t[:, (GROUP + j) * HW : (GROUP + j + 1) * HW] = turn(
            mine[j, K0 : K0 + HW, :]
        ).astype(BF16)
        values[j * HW : (j + 1) * HW, :] = past[j, HW : 2 * HW, :]
        values[(GROUP + j) * HW : (GROUP + j + 1) * HW, :] = mine[j, V0 : V0 + HW, :]
    dk[...] = jnp.zeros_like(dk)
    dv[...] = jnp.zeros_like(dv)
    for p in range(GROUP // 2):
        query = jnp.concatenate([mine[2 * p, :HW, :], mine[2 * p + 1, :HW, :]], axis=0)
        grad_t = jnp.concatenate(
            [turn(mine[2 * p, G0 : G0 + HW, :]), turn(mine[2 * p + 1, G0 : G0 + HW, :])], axis=1
        )
        this = jnp.concatenate([sent[2 * p, 4:8, :], sent[2 * p + 1, 4:8, :]], axis=1)
        other = jnp.concatenate([told[2 * p, 0:4, :], told[2 * p + 1, 0:4, :]], axis=1)
        weight, delta = merge(this, other)
        grad_t = (grad_t * weight).astype(BF16)
        at = p * PAIR
        attended = (result[:, at : at + PAIR] * weight).T.astype(BF16)
        for lo, size in ((0, 384), (384, 384), (768, 384)):
            rows = slice(lo, lo + size)
            spot = slice(at + lo, at + lo + size)
            d_probs = mm(values[spot, :], grad_t)
            block = kept[p, rows, :]
            d_scores = (block.astype(F32) * (d_probs - delta)).astype(BF16)
            grads[rows, :] = d_scores
            dv[spot, :] += mm_nt(block, grad_t)
            dk[spot, :] += mm(d_scores, query)
        d_query = (mm(keys_t[:, at : at + KEYS], grads[...]) * SCALE).T.astype(BF16)
        for i in range(2):
            own[2 * p + i, :HW, :] = attended[i * HW : (i + 1) * HW]
            own[2 * p + i, HW : 2 * HW, :] = d_query[i * HW : (i + 1) * HW]
    for j in range(GROUP):
        early = slice(j * HW, (j + 1) * HW)
        late = slice((GROUP + j) * HW, (GROUP + j + 1) * HW)
        back[j, :HW, :] = (dk[early, :] * SCALE).astype(BF16)
        back[j, HW:, :] = dv[early, :].astype(BF16)
        own[j, 2 * HW : 3 * HW, :] = (dk[late, :] * SCALE).astype(BF16)
        own[j, 3 * HW :, :] = dv[late, :].astype(BF16)


def far_backward(place, mine, past, kept, result, sent, told):
    return pl.pallas_call(
        far_backward_kernel,
        in_specs=[SM] + [VM] * 6,
        out_specs=[VM, VM],
        out_shape=[
            jax.ShapeDtypeStruct((GROUP, 4 * HW, DH), BF16),
            jax.ShapeDtypeStruct((GROUP, 2 * HW, DH), BF16),
        ],
        scratch_shapes=[
            pltpu.VMEM((DH, 2 * GROUP * HW), BF16),
            pltpu.VMEM((2 * GROUP * HW, DH), BF16),
            pltpu.VMEM((2 * GROUP * HW, DH), F32),
            pltpu.VMEM((2 * GROUP * HW, DH), F32),
            pltpu.VMEM((KEYS, PAIR), BF16),
        ],
        compiler_params=params(),
        cost_estimate=cost(32 * KEYS * PAIR * DH, 6_000_000),
        name="far_backward",
    )(place, mine, past, kept, result, sent, told)


def add_back_kernel(own, back, out):
    for j in range(GROUP):
        out[j, 2 * HW : 4 * HW, :] = (
            own[j, 2 * HW : 4 * HW, :].astype(F32) + back[j].astype(F32)
        ).astype(BF16)


def add_back(own, back):
    return pl.pallas_call(
        add_back_kernel,
        in_specs=[VM] * 2,
        out_specs=VM,
        out_shape=jax.ShapeDtypeStruct((GROUP, 4 * HW, DH), BF16),
        input_output_aliases={0: 0},
        compiler_params=params(),
        cost_estimate=cost(GROUP * 2 * HW * DH, 2_500_000),
        name="add_back",
    )(own, back)


def unproject_kernel(
    place, near0, near1, near2, near3, far, w_qkv, w_out, own, other, close, wq, wk, wv, wo, sems
):
    groups = weight_copies(place, w_qkv, w_out, ((0, wq), (1, wk), (2, wv), (3, wo)), sems)
    start_all(groups)
    for step, near in zip(STEPS, (near0, near1, near2, near3)):
        close[head_here(place, step)] = near[...]
    parts = []
    for part in range(4):
        rows = slice(part * HW, (part + 1) * HW)
        pieces = []
        for h in range(HALF):
            slot = slot_of_head(place, h)
            away = jnp.concatenate([far[slot, 0, rows, :], far[slot, 1, rows, :]], axis=0)
            here = jnp.concatenate([close[h, 0, rows, :], close[h, 1, rows, :]], axis=0)
            pieces.append((away.astype(F32) + here.astype(F32)).astype(BF16))
        parts.append(jnp.concatenate(pieces, axis=1))
    wait_all(groups[0])
    total = mm_nt(parts[1], wq[...])
    wait_all(groups[1])
    total = total + mm_nt(parts[2], wk[...])
    wait_all(groups[2])
    total = total + mm_nt(parts[3], wv[...])
    wait_all(groups[3])
    mixed = mm(parts[0], wo[...])
    own[0] = mixed[:HW]
    own[1] = total[:HW]
    other[0] = mixed[HW:].astype(BF16)
    other[1] = total[HW:].astype(BF16)


def unproject(place, blocks, far, w_qkv, w_out):
    return pl.pallas_call(
        unproject_kernel,
        in_specs=[SM] + [VM] * 5 + [ANY] * 2,
        out_specs=[VM, VM],
        scratch_shapes=[pltpu.VMEM((HALF, 2, 4 * HW, DH), BF16)]
        + [pltpu.VMEM((D, HALF * DH), BF16)] * 3
        + [pltpu.VMEM((HALF * DH, D), BF16), pltpu.SemaphoreType.DMA((4 * PIECES,))],
        out_shape=[jax.ShapeDtypeStruct((2, HW, D), F32), jax.ShapeDtypeStruct((2, HW, D), BF16)],
        compiler_params=pltpu.CompilerParams(vmem_limit_bytes=50 * 1024 * 1024),
        cost_estimate=cost(2 * PAIR * D * 4 * HALF * DH, 8_000_000),
        name="unproject",
    )(place, *blocks, far, w_qkv, w_out)


def finish_kernel(tokens, cot, gain, own, other, mixed, out):
    x = tokens[...].astype(F32)
    mixed[...] = (x + (own[0] + other[0].astype(F32))).astype(BF16)
    rinv = lax.rsqrt(jnp.mean(x * x, axis=-1, keepdims=True) + EPS)
    scaled = (own[1] + other[1].astype(F32)) * gain[...]
    mean = jnp.mean(scaled * x, axis=-1, keepdims=True)
    grad = rinv * scaled - x * (rinv * rinv * rinv * mean)
    out[...] = (cot[...].astype(F32) + grad).astype(BF16)


def finish(tokens, cot, gain, own, other):
    return pl.pallas_call(
        finish_kernel,
        in_specs=[VM] * 5,
        out_specs=[VM] * 2,
        out_shape=[jax.ShapeDtypeStruct((HW, D), BF16)] * 2,
        compiler_params=params(),
        cost_estimate=cost(HW * D * 10, 3_000_000),
        name="finish",
    )(tokens, cot, gain, own, other)


LANE = ("x", "zl")
SAME_HEAD = [
    [(x * 2 + zl) * 4 + (h + 4 - x) % 4 for x in range(4) for zl in range(2)] for h in range(4)
]


def swap(value):
    return lax.ppermute(value, "core", [(0, 1), (1, 0)])


def turn_ring(value, steps):
    return lax.ppermute(value, "zh", [(i, (i + steps) % 4) for i in range(4)])


def all_round(blocks, sign):
    return [blocks[0]] + [turn_ring(blocks[g], sign * STEPS[g]) for g in (1, 2, 3)]


def exchange(value, axes, groups=None):
    return lax.all_to_all(value, axes, 0, 0, axis_index_groups=groups, tiled=True)


def exchange_alone(value, go):
    return lax.cond(go, lambda v: exchange(v, LANE), jnp.zeros_like, value)


def per_device(tokens, gain, w_qkv, w_out, window, valid, cotangent):
    rows = lax.axis_size("y")
    place = jnp.stack(
        [lax.axis_index(axis) for axis in ("core", "x", "zh")]
    ).astype(jnp.int32)
    go = window[0] > 0
    tokens = tokens.reshape(HW, D)
    cot = cotangent.reshape(HW, D)
    other_tokens = swap(tokens)
    other_cot = swap(cot)
    gain = gain.reshape(1, D)
    weights = stage(place, w_qkv, w_out)
    packed, *blocks = project(
        place, valid, tokens, other_tokens, cot, other_cot, gain, weights
    )
    blocks = all_round(blocks, 1)
    mine = exchange(packed.reshape(2 * HALF, ROWS, DH), LANE)
    past = lax.ppermute(mine[:, K0:, :], "y", [(i, i + 1) for i in range(rows - 1)])
    near_kept, near_result, close = near_forward(*blocks)
    sent, far_kept, far_result = far_forward(place, window, mine, past, close)
    told = exchange(sent, ("x", "zl", "zh"), SAME_HEAD)
    own, back = far_backward(place, mine, past, far_kept, far_result, sent, told)
    back = lax.ppermute(back, "y", [(i + 1, i) for i in range(rows - 1)])
    returned = near_backward(place, blocks, near_kept, near_result, close, told)
    own, returned = lax.optimization_barrier((own, returned))
    returned = all_round(returned, -1)
    own = add_back(own, back)
    far = exchange_alone(own, go).reshape(HALF, 2, 4 * HW, DH)
    out_own, out_other = unproject(place, returned, far, w_qkv, w_out)
    mixed, d_tokens = finish(tokens, cot, gain, out_own, swap(out_other))
    return mixed.reshape(1, 1, HW, D), d_tokens.reshape(1, 1, HW, D)


def solution(mesh):
    grid = Mesh(mesh.devices.reshape(4, 4, 2, 4, 2), ("y", "x", "zl", "zh", "core"))
    frames, cams = ("y", "x", "zl"), ("zh", "core")
    split = P(frames, cams, None, None)
    return jax.shard_map(
        per_device,
        mesh=grid,
        in_specs=(split, P(), P(), P(), P(), P(frames), split),
        out_specs=(split, split),
        check_vma=False,
    )
```
